32 devices in a mesh: rep: 4 (over z), fsdp: 8 (over y, x, core).
Axes of the slice: x: 2, y: 2, z: 4, core: 2. Of those that a mesh axis runs over, the one named last changes fastest.
Arguments:
- tokens: bfloat16 [32, 1024, 640], P(('rep', 'fsdp')), may hold values from -6 to 6
- masked: int32 [32, 1024], P(('rep', 'fsdp')), may hold values from 0 to 1, as said below
- cotangent: bfloat16 [32, 1024, 640], P(('rep', 'fsdp')), may hold values from -6 to 6
- norm1_gain: bfloat16 [640], P('fsdp'), may hold values from 0.5 to 1.5
- norm1_shift: bfloat16 [640], P('fsdp'), may hold values from -1.75 to 1.75
- w_qkv: bfloat16 [640, 1920], P('fsdp'), may hold values from -0.3125 to 0.3125
- bias_query: bfloat16 [640], P('fsdp'), may hold values from -3 to 3
- bias_value: bfloat16 [640], P('fsdp'), may hold values from -3 to 3
- w_out: bfloat16 [640, 640], P('fsdp'), may hold values from -2 to 2
- bias_out: bfloat16 [640], P('fsdp'), may hold values from -3 to 3
- norm2_gain: bfloat16 [640], P('fsdp'), may hold values from 0.5 to 1.5
- norm2_shift: bfloat16 [640], P('fsdp'), may hold values from -1.75 to 1.75
- w_up: bfloat16 [640, 5120], P('fsdp'), may hold values from -0.25 to 0.25
- bias_up: bfloat16 [5120], P('fsdp'), may hold values from -3 to 3
- w_down: bfloat16 [5120, 640], P('fsdp'), may hold values from -0.15625 to 0.15625
- bias_down: bfloat16 [640], P('fsdp'), may hold values from -3 to 3
Outputs:
- result: bfloat16 [32, 1024, 640], P(('rep', 'fsdp'))
- grad_tokens: bfloat16 [32, 1024, 640], P(('rep', 'fsdp'))
- grad_norm1_gain: float32 [640], P('fsdp')
- grad_norm1_shift: float32 [640], P('fsdp')
- grad_w_qkv: float32 [640, 1920], P('fsdp')
- grad_bias_query: float32 [640], P('fsdp')
- grad_bias_value: float32 [640], P('fsdp')
- grad_w_out: float32 [640, 640], P('fsdp')
- grad_bias_out: float32 [640], P('fsdp')
- grad_norm2_gain: float32 [640], P('fsdp')
- grad_norm2_shift: float32 [640], P('fsdp')
- grad_w_up: float32 [640, 5120], P('fsdp')
- grad_bias_up: float32 [5120], P('fsdp')
- grad_w_down: float32 [5120, 640], P('fsdp')
- grad_bias_down: float32 [640], P('fsdp')
The draws below stay inside these ranges and needn't reach their ends.
Inputs may be any that keep to these rules, and one draw needn't show every extreme that they name: Each sequence has its own rate of masked positions, between 5 and 30 in 100; positions are masked independently at that rate, so the number of masked positions in a sequence is random and not bounded by the rate.
All inputs are finite; a program needn't handle non-finite values.
Results may differ from the reference program's by a relative error of at most 0.015.
Values may be sent and summed in bfloat16 or wider, within the bound.
A program may use at most 192 MiB of HBM per device.

```python
import jax
import jax.numpy as jnp
from jax import lax

D = 640
HEADS = 20
HEAD_DIM = 32
FF = 5120
LEN = 1024
SEQS = 32


def draw_masked(key, part):
    key = jax.random.fold_in(key, 11)
    rate_key, draw_key = jax.random.split(key)
    rates = jax.random.randint(rate_key, (SEQS, 1), 5, 31)
    picks = jax.random.randint(draw_key, (SEQS, LEN), 0, 100)
    return (picks < rates).astype(jnp.int32)


def block_scale(stream_key, shape, cuts, low, largest):
    level, own = 1.0, jax.random.fold_in(stream_key, 6)
    for position, shards_of in cuts:
        heights = jnp.exp(jax.random.uniform(jax.random.fold_in(own, position), (shards_of,), jnp.float32, low / len(cuts), largest / len(cuts)))
        level = level * jnp.repeat(heights, shape[position] // shards_of).reshape([-1 if axis == position else 1 for axis in range(len(shape))])
    return level


def bell_draw(key, dims, spread, reach, shards=(), held_as=jnp.bfloat16):
    loudness = block_scale(key, dims, shards, -0.22, 0.18) if shards else 1.0
    array = jax.random.normal(key, dims, jnp.float32) * spread * loudness
    return jnp.minimum(jnp.maximum(array, -reach), reach).astype(held_as)


def setup_inputs(seed: int = 0) -> dict:
    key_list = jax.random.split(jax.random.key(seed), 17)
    tokens = bell_draw(key_list[0], (SEQS, LEN, D), 1.0, 6.0, ((0, 32),))
    masked = draw_masked(jax.random.fold_in(key_list[16], 71), 0)
    cotangent = bell_draw(key_list[2], (SEQS, LEN, D), 1.0, 6.0, ((0, 32),))
    norm1_gain = jnp.clip(1.0 + 0.1 * jax.random.normal(key_list[3], (D,), jnp.float32), 0.5, 1.5).astype(jnp.bfloat16)
    norm1_shift = bell_draw(key_list[4], (D,), 0.3, 1.75, ((0, 8),))
    w_qkv = bell_draw(key_list[5], (D, 3 * D), (D // 2) ** -0.5, 0.3125, ((0, 8),))
    bias_query = bell_draw(key_list[6], (D,), 0.5, 3.0, ((0, 8),))
    bias_value = bell_draw(key_list[7], (D,), 0.5, 3.0, ((0, 8),))
    w_out = bell_draw(key_list[8], (D, D), (max(D // 64, 1)) ** -0.5, 2.0, ((0, 8),))
    bias_out = bell_draw(key_list[9], (D,), 0.5, 3.0, ((0, 8),))
    norm2_gain = jnp.clip(1.0 + 0.1 * jax.random.normal(key_list[10], (D,), jnp.float32), 0.5, 1.5).astype(jnp.bfloat16)
    norm2_shift = bell_draw(key_list[11], (D,), 0.3, 1.75, ((0, 8),))
    w_up = bell_draw(key_list[12], (D, FF), D ** -0.5, 0.25, ((0, 8),))
    bias_up = bell_draw(key_list[13], (FF,), 0.5, 3.0, ((0, 8),))
    w_down = bell_draw(key_list[14], (FF, D), (FF // 4) ** -0.5, 0.15625, ((0, 8),))
    bias_down = bell_draw(key_list[15], (D,), 0.5, 3.0, ((0, 8),))
    return dict(tokens=tokens, masked=masked, cotangent=cotangent, norm1_gain=norm1_gain, norm1_shift=norm1_shift, w_qkv=w_qkv, bias_query=bias_query, bias_value=bias_value, w_out=w_out, bias_out=bias_out, norm2_gain=norm2_gain, norm2_shift=norm2_shift, w_up=w_up, bias_up=bias_up, w_down=w_down, bias_down=bias_down)


@jax.custom_vjp
def low(v):
    return lax.optimization_barrier(v.astype(jnp.bfloat16)).astype(jnp.float32)

@jax.custom_vjp
def low_back(v):
    return v

def low_keep(v):
    return (low(v), None)

def low_pass(kept, grad):
    return (grad,)

def back_keep(v):
    return (v, None)

def back_low(kept, grad):
    return (low(grad),)
low.defvjp(low_keep, low_pass)
low_back.defvjp(back_keep, back_low)
HIGH = lax.Precision.HIGHEST

def layer_norm(values, gain, shift):
    mean = lax.optimization_barrier(jnp.mean(values, axis=-1, keepdims=True))
    centred = values - mean
    variance = lax.optimization_barrier(jnp.mean(centred * centred, axis=-1, keepdims=True))
    return centred * lax.rsqrt(variance + 1e-05) * gain + shift

def one_head(operands):
    query_rows, key, value = operands
    attention_logits = low_back(jnp.dot(query_rows, key.T, precision=HIGH) * HEAD_DIM ** (-0.5))
    attention_probs = low(jax.nn.softmax(attention_logits, axis=-1))
    return jnp.dot(attention_probs, value, precision=HIGH)

def forward(inputs, params):
    norm1_gain, norm1_shift, w_qkv, bias_query, bias_value, w_out, bias_out, norm2_gain, norm2_shift, w_up, bias_up, w_down, bias_down = params
    length = inputs.shape[0]
    normed1 = low(layer_norm(inputs, norm1_gain, norm1_shift))
    full_bias = jnp.concatenate([bias_query, jnp.zeros_like(bias_query), bias_value])
    projected = low(low_back(jnp.dot(normed1, w_qkv, precision=HIGH) + full_bias))
    split = projected.reshape(length, 3, HEADS, HEAD_DIM).transpose(1, 2, 0, 3)
    heads_out = lax.map(jax.checkpoint(one_head), (split[0], split[1], split[2]))
    joined = low(low_back(heads_out.transpose(1, 0, 2).reshape(length, D)))
    attn = low_back(jnp.dot(joined, w_out, precision=HIGH) + bias_out)
    middle = inputs + attn
    normed2 = low(layer_norm(middle, norm2_gain, norm2_shift))
    hidden = low_back(jnp.dot(normed2, w_up, precision=HIGH) + bias_up)
    active = low(jax.nn.gelu(hidden, approximate=False))
    branch = low_back(jnp.dot(active, w_down, precision=HIGH) + bias_down)
    return middle + branch

def reference(tokens, masked, cotangent, norm1_gain, norm1_shift, w_qkv, bias_query, bias_value, w_out, bias_out, norm2_gain, norm2_shift, w_up, bias_up, w_down, bias_down):
    params = (norm1_gain, norm1_shift, w_qkv, bias_query, bias_value, w_out, bias_out, norm2_gain, norm2_shift, w_up, bias_up, w_down, bias_down)
    params = tuple((item.astype(jnp.float32) for item in params))

    def one_sequence(carry, item):
        sequence, mask_row, incoming = item
        inputs = sequence.astype(jnp.float32)
        layer_output, back = jax.vjp(forward, inputs, params)
        grad_seq = incoming.astype(jnp.float32) * mask_row.astype(jnp.float32)[:, None]
        grad_inputs, grad_params = back(grad_seq)
        carry = jax.tree.map(jnp.add, carry, grad_params)
        return (carry, (layer_output.astype(jnp.bfloat16), grad_inputs.astype(jnp.bfloat16)))
    start = tuple((jnp.zeros_like(item) for item in params))
    totals, (outputs, grads) = lax.scan(one_sequence, start, (tokens, masked, cotangent))
    return (outputs, grads, totals[0], totals[1], totals[2], totals[3], totals[4], totals[5], totals[6], totals[7], totals[8], totals[9], totals[10], totals[11], totals[12])
```

```python
import functools

import jax
import jax.numpy as jnp
from jax import lax
from jax.experimental import pallas as pl
from jax.experimental.pallas import tpu as pltpu
from jax.sharding import PartitionSpec as P

HEADS = 20
HEAD_DIM = 32
GROUP = 4
LANES = 128
SCALE = HEAD_DIM ** (-0.5)
LOG2E = 1.4426950408889634
FEW = 384
F32 = jnp.float32
BF16 = jnp.bfloat16
MB = 1024 * 1024

NN = (((1,), (0,)), ((), ()))
NT = (((1,), (1,)), ((), ()))


def dot(a, b, dims=NN):
    return lax.dot_general(a, b, dims, preferred_element_type=F32)


def norm_stats(x):
    mean = jnp.mean(x, axis=-1, keepdims=True)
    centred = x - mean
    variance = jnp.mean(centred * centred, axis=-1, keepdims=True)
    rstd = lax.rsqrt(variance + 1e-05)
    return centred * rstd, rstd


def norm_back(grad, xhat, rstd, gain):
    dxhat = grad * gain
    first = jnp.mean(dxhat, axis=-1, keepdims=True)
    second = jnp.mean(dxhat * xhat, axis=-1, keepdims=True)
    return rstd * (dxhat - first - xhat * second)


def cdf_parts(u):
    z = jnp.abs(u)
    t = 1.0 / (1.0 + 0.23164189 * z)
    e = jnp.exp2(u * u * (-0.5 * LOG2E))
    poly = t * (
        0.127414796 + t * (-0.142248368 + t * (0.7107068705 + t * (-0.7265760135 + t * 0.5307027145)))
    )
    tail = poly * e
    return jnp.where(u < 0, tail, 1.0 - tail), e


def one_hot_rows(slot, start, size):
    length = slot.shape[1]
    rows = lax.broadcasted_iota(jnp.int32, (size, length), 0).astype(F32) + start
    return jnp.where(rows == slot, 1.0, 0.0)


def unpermute(slot, src_ref, out_ref):
    length = slot.shape[1]
    wide = jnp.transpose(jnp.broadcast_to(slot, (LANES, length)))
    step = 256
    for start in range(0, length, step):
        col = wide[start : start + step, :1]
        cols = lax.broadcasted_iota(jnp.int32, (step, length), 1).astype(F32)
        pick = jnp.where(cols == col, 1.0, 0.0).astype(BF16)
        out_ref[start : start + step, :] = dot(pick, src_ref[...]).astype(BF16)


def attn_kernel(
    tokens_ref, mask_ref, vec_ref, wqkv_ref, wout_ref,
    slot_ref, xp_ref, h1_ref, qkv_ref, o_ref, lse_ref, x1_ref,
):
    length, width = tokens_ref.shape
    step = 256
    mask8 = jnp.broadcast_to(mask_ref[...], (8, length))
    cum = []
    for start in range(0, length, step):
        up = lax.broadcasted_iota(jnp.int32, (length, step), 0)
        to = lax.broadcasted_iota(jnp.int32, (length, step), 1) + start
        cum.append(dot(mask8.astype(BF16), jnp.where(up <= to, 1.0, 0.0).astype(BF16)))
    cum = jnp.concatenate(cum, axis=1)
    count = jnp.sum(mask8, axis=1, keepdims=True)
    pos = lax.broadcasted_iota(jnp.int32, (8, length), 1).astype(F32)
    slot = jnp.where(mask8 > 0.5, cum - 1.0, count + pos - cum)
    slot_ref[...] = slot
    gain = vec_ref[0:1, :]
    shift = vec_ref[1:2, :]
    bq = vec_ref[2:3, :]
    bv = vec_ref[3:4, :]
    bout = vec_ref[4:5, :]

    def project(i, _):
        rows = pl.ds(pl.multiple_of(i * step, step), step)
        pick = one_hot_rows(slot[:1], (i * step).astype(F32), step).astype(BF16)
        x = dot(pick, tokens_ref[...])
        xp_ref[rows, :] = x.astype(BF16)
        xhat, _ = norm_stats(x)
        h1 = (xhat * gain + shift).astype(BF16)
        h1_ref[rows, :] = h1
        qkv_ref[rows, :width] = (dot(h1, wqkv_ref[:, :width]) + bq).astype(BF16)
        qkv_ref[rows, width : 2 * width] = dot(h1, wqkv_ref[:, width : 2 * width]).astype(BF16)
        qkv_ref[rows, 2 * width :] = (dot(h1, wqkv_ref[:, 2 * width :]) + bv).astype(BF16)
        return 0

    lax.fori_loop(0, length // step, project, 0)

    c = SCALE * LOG2E
    lane = lax.broadcasted_iota(jnp.int32, (step, LANES), 1)

    def attend(n, _):
        t = n // (length // step)
        i = n % (length // step)
        rows = pl.ds(pl.multiple_of(i * step, step), step)
        q = qkv_ref[rows, pl.ds(pl.multiple_of(t * LANES, LANES), LANES)]
        k = qkv_ref[:, pl.ds(pl.multiple_of(width + t * LANES, LANES), LANES)]
        v = qkv_ref[:, pl.ds(pl.multiple_of(2 * width + t * LANES, LANES), LANES)]
        vo = jnp.concatenate([v, jnp.ones_like(v)], axis=1)
        out = jnp.zeros((step, LANES), F32)
        lses = jnp.zeros((step, LANES), F32)
        for h in range(GROUP):
            mine = lane // HEAD_DIM == h
            s = dot(jnp.where(mine, q, jnp.zeros_like(q)), k, NT)
            top = jnp.max(s, axis=-1, keepdims=True)
            p = jnp.exp2((s - top) * c).astype(BF16)
            ov = dot(p, vo)
            total = ov[:, LANES:]
            out = jnp.where(mine, ov[:, :LANES] / total, out)
            lses = jnp.where(lane == h, top * c + jnp.log2(total), lses)
        o_ref[rows, pl.ds(pl.multiple_of(t * LANES, LANES), LANES)] = out.astype(BF16)
        lse_ref[pl.ds(pl.multiple_of(t * 8, 8), 8), rows] = jnp.transpose(lses)[:8, :]
        return 0

    lax.fori_loop(0, (width // LANES) * (length // step), attend, 0)

    def join(i, _):
        rows = pl.ds(pl.multiple_of(i * step, step), step)
        x1_ref[rows, :] = xp_ref[rows, :].astype(F32) + dot(o_ref[rows, :], wout_ref[...]) + bout
        return 0

    lax.fori_loop(0, length // step, join, 0)


def attn_forward(tokens, mask, vecs, wqkv, wout):
    length, width = tokens.shape
    sds = jax.ShapeDtypeStruct
    groups = width // LANES
    return pl.pallas_call(
        attn_kernel,
        out_shape=(
            sds((8, length), F32),
            sds((length, width), BF16),
            sds((length, width), BF16),
            sds((length, 3 * width), BF16),
            sds((length, width), BF16),
            sds((8 * groups, length), F32),
            sds((length, width), F32),
        ),
        compiler_params=pltpu.CompilerParams(vmem_limit_bytes=56 * MB),
        name="attn_forward",
    )(tokens, mask, vecs, wqkv, wout)


def ffn_kernel(
    few,
    x1_ref, cot_ref, slot_ref, mask_ref, vec_ref, bup_ref, wup_ref, wdn_ref, wout_ref, o_ref,
    res_ref, gup_ref, gdn_ref, gbup_ref, g1_ref, do_ref, gout_ref, small_ref,
    acc, h2, h2t, gy, gyt, dh2, outp,
):
    j = pl.program_id(0)
    last = pl.num_programs(0) - 1
    length, width = x1_ref.shape
    gain = vec_ref[5:6, :]
    shift = vec_ref[6:7, :]
    bdown = vec_ref[7:8, :]
    blocks = []
    start = 0
    part = few if few <= 384 else 256
    while start < few:
        blocks.append((start, part, True))
        start += part
    while start < length:
        size = min(320, length - start)
        blocks.append((start, size, False))
        start += size

    @pl.when(j == 0)
    def _():
        for start, size, back in blocks:
            rows = slice(start, start + size)
            x1 = x1_ref[rows, :]
            xhat, _ = norm_stats(x1)
            hidden = (xhat * gain + shift).astype(BF16)
            h2[rows, :] = hidden
            acc[rows, :] = x1 + bdown
            if back:
                h2t[:, rows] = jnp.transpose(hidden)
                pick = one_hot_rows(slot_ref[0:1, :], float(start), size) * mask_ref[...]
                g = dot(pick.astype(BF16), cot_ref[...])
                gy[rows, :] = g.astype(BF16)
                gyt[:, rows] = jnp.transpose(g.astype(BF16))
                dh2[rows, :] = jnp.zeros((size, width), F32)

    gup = gdn = gbup = None
    for start, size, back in blocks:
        rows = slice(start, start + size)
        u = dot(h2[rows, :], wup_ref[...]) + bup_ref[...]
        cdf, e = cdf_parts(u)
        a = (u * cdf).astype(BF16)
        acc[rows, :] += dot(a, wdn_ref[...])
        if back:
            da = dot(gy[rows, :], wdn_ref[...], NT)
            du = ((cdf + u * e * 0.3989422804014327) * da).astype(BF16)
            p_up = dot(h2t[:, rows], du)
            p_dn = dot(gyt[:, rows], a)
            p_b = jnp.sum(du.astype(F32), axis=0, keepdims=True)
            gup = p_up if gup is None else gup + p_up
            gdn = p_dn if gdn is None else gdn + p_dn
            gbup = p_b if gbup is None else gbup + p_b
            dh2[rows, :] += dot(du, wup_ref[...], NT)
    gup_ref[...] = gup.astype(BF16)
    gdn_ref[...] = gdn.astype(BF16)
    gbup_ref[...] = gbup

    @pl.when(j == last)
    def _():
        ggain = gshift = gbdown = gbout = gout = jnp.zeros((1, 1), F32)
        for start, size, back in blocks:
            rows = slice(start, start + size)
            outp[rows, :] = acc[rows, :].astype(BF16)
            if back:
                xhat, rstd = norm_stats(x1_ref[rows, :])
                d = dh2[rows, :]
                g = gy[rows, :].astype(F32)
                g1 = g + norm_back(d, xhat, rstd, gain)
                g1_ref[rows, :] = g1
                g1b = g1.astype(BF16)
                do_ref[rows, :] = dot(g1b, wout_ref[...], NT).astype(BF16)
                gout = gout + dot(jnp.transpose(o_ref[rows, :]), g1b)
                ggain = ggain + jnp.sum(d * xhat, axis=0, keepdims=True)
                gshift = gshift + jnp.sum(d, axis=0, keepdims=True)
                gbdown = gbdown + jnp.sum(g, axis=0, keepdims=True)
                gbout = gbout + jnp.sum(g1b.astype(F32), axis=0, keepdims=True)
        gout_ref[...] = gout.astype(BF16)
        small_ref[0:1, :] = gbout
        small_ref[1:2, :] = ggain
        small_ref[2:3, :] = gshift
        small_ref[3:4, :] = gbdown
        small_ref[4:8, :] = jnp.zeros((4, width), F32)
        unpermute(slot_ref[0:1, :], outp, res_ref)


def feed_forward(few, x1, cot, slot, mask, vecs, bup, wup, wdn, wout, o):
    length, width = x1.shape
    hidden = wup.shape[1]
    fc = 512
    sds = jax.ShapeDtypeStruct
    whole = lambda *shape: pl.BlockSpec(shape, lambda j: (0,) * len(shape))
    return pl.pallas_call(
        functools.partial(ffn_kernel, few),
        grid=(hidden // fc,),
        in_specs=[
            whole(length, width),
            whole(length, width),
            whole(8, length),
            whole(1, length),
            whole(8, width),
            pl.BlockSpec((1, fc), lambda j: (0, j)),
            pl.BlockSpec((width, fc), lambda j: (0, j)),
            pl.BlockSpec((fc, width), lambda j: (j, 0)),
            whole(width, width),
            whole(few, width),
        ],
        out_specs=[
            whole(length, width),
            pl.BlockSpec((width, fc), lambda j: (0, j)),
            pl.BlockSpec((width, fc), lambda j: (0, j)),
            pl.BlockSpec((1, fc), lambda j: (0, j)),
            whole(few, width),
            whole(few, width),
            whole(width, width),
            whole(8, width),
        ],
        out_shape=(
            sds((length, width), BF16),
            sds((width, hidden), BF16),
            sds((width, hidden), BF16),
            sds((1, hidden), F32),
            sds((few, width), F32),
            sds((few, width), BF16),
            sds((width, width), BF16),
            sds((8, width), F32),
        ),
        scratch_shapes=[
            pltpu.VMEM((length, width), F32),
            pltpu.VMEM((length, width), BF16),
            pltpu.VMEM((width, few), BF16),
            pltpu.VMEM((few, width), BF16),
            pltpu.VMEM((width, few), BF16),
            pltpu.VMEM((few, width), F32),
            pltpu.VMEM((length, width), BF16),
        ],
        compiler_params=pltpu.CompilerParams(vmem_limit_bytes=56 * MB),
        name="feed_forward",
    )(x1, cot, slot, mask, vecs, bup, wup, wdn, wout, o)


def back_kernel(
    few,
    q_ref, k_ref, v_ref, do_ref, o_ref, lse_ref, h1_ref, xp_ref, vec_ref,
    wq_ref, wk_ref, wv_ref, g1_ref, slot_ref,
    gtok_ref, gq_ref, gk_ref, gv_ref, small_ref,
    h1t, dh1, dqt, dkv, gtp,
):
    t = pl.program_id(0)
    last = pl.num_programs(0) - 1
    length, width = h1_ref.shape
    groups = width // LANES
    step = 256
    c = SCALE * LOG2E
    gain = vec_ref[0:1, :]

    @pl.when(t == 0)
    def _():
        for start in range(0, length, step):
            h1t[:, start : start + step] = jnp.transpose(h1_ref[start : start + step, :])
        dh1[...] = jnp.zeros_like(dh1)

    q = q_ref[...]
    do = do_ref[...]
    lane = lax.broadcasted_iota(jnp.int32, (few, LANES), 1)
    head = lax.broadcasted_iota(jnp.int32, (8, LANES), 0)
    lane8 = lax.broadcasted_iota(jnp.int32, (8, LANES), 1)
    pick = jnp.where(lane8 // HEAD_DIM == head, 1.0, 0.0)
    delta = lax.dot_general(
        pick, do.astype(F32) * o_ref[...].astype(F32), NT,
        precision=lax.Precision.HIGHEST, preferred_element_type=F32,
    )
    dqt[...] = jnp.zeros_like(dqt)
    zero = jnp.zeros_like(q)
    qs = [jnp.where(lane // HEAD_DIM == h, q, zero) for h in range(GROUP)]
    dos = [jnp.where(lane // HEAD_DIM == h, do, zero) for h in range(GROUP)]

    def keys(i, _):
        rows = pl.ds(pl.multiple_of(i * step, step), step)
        k = k_ref[rows, :]
        v = v_ref[rows, :]
        kt = jnp.transpose(k)
        dk = jnp.zeros((step, LANES), F32)
        dv = jnp.zeros((step, LANES), F32)
        for h in range(GROUP):
            s = dot(k, qs[h], NT)
            p = jnp.exp2(s * c - lse_ref[h : h + 1, :])
            dp = dot(v, dos[h], NT)
            ds = (p * (dp - delta[h : h + 1, :])).astype(BF16)
            dv = dv + dot(p.astype(BF16), dos[h])
            dk = dk + dot(ds, qs[h])
            part = slice(h * HEAD_DIM, (h + 1) * HEAD_DIM)
            dqt[part, :] += dot(kt[part, :], ds)
        dkv[rows, :LANES] = (dk * SCALE).astype(BF16)
        dkv[rows, LANES:] = dv.astype(BF16)
        return 0

    lax.fori_loop(0, length // step, keys, 0)
    dq = (jnp.transpose(dqt[...]) * SCALE).astype(BF16)
    gq_ref[...] = dot(h1t[:, :few], dq).astype(BF16)
    gkv = dot(h1t[...], dkv[...]).astype(BF16)
    gk_ref[...] = gkv[:, :LANES]
    gv_ref[...] = gkv[:, LANES:]
    small_ref[0:1, :] = jnp.zeros((1, LANES), F32)
    small_ref[2:3, :] = jnp.sum(dq.astype(F32), axis=0, keepdims=True)
    small_ref[3:4, :] = jnp.sum(dkv[:, LANES:].astype(F32), axis=0, keepdims=True)
    wkv = jnp.concatenate([wk_ref[...], wv_ref[...]], axis=1)
    for start in range(0, length, step):
        rows = slice(start, start + step)
        dh1[rows, :] += dot(dkv[rows, :], wkv, NT)
    dh1[:few, :] += dot(dq, wq_ref[...], NT)


def back_finish(
    few,
    dh1_ref, xp_ref, vec_ref, g1_ref, slot_ref, gtok_ref, small_ref, gtp,
):
    length, width = xp_ref.shape
    gain = vec_ref[0:1, :]
    step = 128
    ggain = gshift = jnp.zeros((1, width), F32)
    for start in range(0, length, step):
        rows = slice(start, start + step)
        xhat, rstd = norm_stats(xp_ref[rows, :].astype(F32))
        d = dh1_ref[rows, :]
        g = norm_back(d, xhat, rstd, gain)
        if start < few:
            g = g + g1_ref[rows, :]
        gtp[rows, :] = g.astype(BF16)
        ggain = ggain + jnp.sum(d * xhat, axis=0, keepdims=True)
        gshift = gshift + jnp.sum(d, axis=0, keepdims=True)
    small_ref[0:1, :] = ggain
    small_ref[1:2, :] = gshift
    unpermute(slot_ref[0:1, :], gtp, gtok_ref)


def back_all(few, *refs):
    (q, k, v, do, o, lse, h1, xp, vec, wq, wk, wv, g1, slot,
     gtok, gq, gk, gv, small, norms, h1t, dh1, dqt, dkv, gtp) = refs
    back_kernel(few, q, k, v, do, o, lse, h1, xp, vec, wq, wk, wv, g1, slot,
                gtok, gq, gk, gv, small, h1t, dh1, dqt, dkv, gtp)

    @pl.when(pl.program_id(0) == pl.num_programs(0) - 1)
    def _():
        norms[...] = jnp.zeros_like(norms)
        back_finish(few, dh1, xp, vec, g1, slot, gtok, norms, gtp)


def attn_backward(few, qkv, do, o, lse, h1, xp, vecs, wqkv, g1, slot):
    length, width = h1.shape
    groups = width // LANES
    sds = jax.ShapeDtypeStruct
    whole = lambda *shape: pl.BlockSpec(shape, lambda t: (0,) * len(shape))
    cols = lambda rows, first: pl.BlockSpec((rows, LANES), lambda t: (0, first + t))
    return pl.pallas_call(
        functools.partial(back_all, few),
        grid=(groups,),
        in_specs=[
            cols(few, 0),
            cols(length, groups),
            cols(length, 2 * groups),
            cols(few, 0),
            cols(few, 0),
            pl.BlockSpec((8, few), lambda t: (t, 0)),
            whole(length, width),
            whole(length, width),
            whole(8, width),
            cols(width, 0),
            cols(width, groups),
            cols(width, 2 * groups),
            whole(few, width),
            whole(8, length),
        ],
        out_specs=[
            whole(length, width),
            cols(width, 0),
            cols(width, 0),
            cols(width, 0),
            cols(8, 0),
            whole(8, width),
        ],
        out_shape=(
            sds((length, width), BF16),
            sds((width, width), BF16),
            sds((width, width), BF16),
            sds((width, width), BF16),
            sds((8, width), F32),
            sds((8, width), F32),
        ),
        scratch_shapes=[
            pltpu.VMEM((width, length), BF16),
            pltpu.VMEM((length, width), F32),
            pltpu.VMEM((LANES, few), F32),
            pltpu.VMEM((length, 2 * LANES), BF16),
            pltpu.VMEM((length, width), BF16),
        ],
        compiler_params=pltpu.CompilerParams(vmem_limit_bytes=56 * MB),
        name="attn_backward",
    )(qkv, qkv, qkv, do, o, lse, h1, xp, vecs, wqkv, wqkv, wqkv, g1, slot)


def local(
    tokens, masked, cotangent, norm1_gain, norm1_shift, w_qkv, bias_query, bias_value, w_out,
    bias_out, norm2_gain, norm2_shift, w_up, bias_up, w_down, bias_down,
):
    seqs, length, width = tokens.shape
    hidden = w_up.shape[1]
    share = w_qkv.shape[0]
    x = tokens.reshape(seqs * length, width)
    cot = cotangent.reshape(seqs * length, width)
    mask = masked.astype(F32)
    most = lax.pmax(jnp.sum(masked), ("rep", "fsdp"))
    packed = jnp.stack(
        [norm1_gain, norm1_shift, bias_query, bias_value, bias_out, norm2_gain, norm2_shift, bias_down]
    )
    vecs = lax.all_gather(packed, "fsdp", axis=1, tiled=True).astype(F32)
    bup = lax.all_gather(bias_up, "fsdp", axis=0, tiled=True).astype(F32).reshape(1, hidden)
    gather = lambda w: lax.all_gather(w, "fsdp", axis=0, tiled=True)
    wqkv, wout, wup, wdn = gather(w_qkv), gather(w_out), gather(w_up), gather(w_down)

    slot, xp, h1, qkv, o, lse, x1 = attn_forward(x, mask, vecs, wqkv, wout)

    def backward(few):
        def run():
            res, gup, gdn, gbup, g1, do, gout, small2 = feed_forward(
                few, x1, cot, slot, mask, vecs, bup, wup, wdn, wout, o
            )
            gtok, gq, gk, gv, small1, norms = attn_backward(
                few, qkv, do, o, lse, h1, xp, vecs, wqkv, g1, slot
            )
            small = jnp.concatenate(
                [norms[:2], small1[2:4], small2[:4], gbup.reshape(8, width)], axis=0
            )
            return res, gtok, gup, gdn, gout, gq, gk, gv, small

        return run

    res, gtok, gup, gdn, gout, gq, gk, gv, small = lax.cond(
        most <= FEW, backward(FEW), backward(length)
    )

    def scatter(g, dim):
        part = lax.psum_scatter(g, "fsdp", scatter_dimension=dim, tiled=True)
        return lax.psum(part, "rep").astype(F32)

    gup = scatter(gup, 0)
    gdn = jnp.transpose(scatter(gdn, 1))
    gattn = scatter(jnp.concatenate([gout, gq, gk, gv], axis=1), 0)
    gout, gqkv = gattn[:, :width], gattn[:, width:]
    small = lax.psum(small, ("rep", "fsdp"))
    me = lax.axis_index("fsdp")
    mine = lax.dynamic_slice_in_dim(small[:8], me * share, share, axis=1)
    gbup = lax.dynamic_slice_in_dim(small[8:].reshape(hidden), me * bias_up.shape[0], bias_up.shape[0])
    return (
        res.reshape(seqs, length, width),
        gtok.reshape(seqs, length, width),
        mine[0], mine[1], gqkv, mine[2], mine[3], gout, mine[4], mine[5], mine[6],
        gup, gbup, gdn, mine[7],
    )


def solution(mesh):
    rows3 = P(("rep", "fsdp"), None, None)
    vec = P("fsdp")
    mat = P("fsdp", None)
    in_specs = (
        rows3, P(("rep", "fsdp"), None), rows3,
        vec, vec, mat, vec, vec, mat, vec, vec, vec, mat, vec, mat, vec,
    )
    out_specs = (rows3, rows3, vec, vec, mat, vec, vec, mat, vec, vec, vec, mat, vec, mat, vec)
    return jax.shard_map(local, mesh=mesh, in_specs=in_specs, out_specs=out_specs, check_vma=False)
```

```python
import functools

import jax
import jax.numpy as jnp
from jax import lax
from jax.experimental import pallas as pl
from jax.experimental.pallas import tpu as pltpu
from jax.sharding import PartitionSpec as P

HEADS = 20
HEAD_DIM = 32
GROUP = 4
LANES = 128
SCALE = HEAD_DIM ** (-0.5)
LOG2E = 1.4426950408889634
FEW = 384
F32 = jnp.float32
BF16 = jnp.bfloat16
MB = 1024 * 1024

NN = (((1,), (0,)), ((), ()))
NT = (((1,), (1,)), ((), ()))


def dot(a, b, dims=NN):
    return lax.dot_general(a, b, dims, preferred_element_type=F32)


def norm_stats(x):
    mean = jnp.mean(x, axis=-1, keepdims=True)
    centred = x - mean
    variance = jnp.mean(centred * centred, axis=-1, keepdims=True)
    rstd = lax.rsqrt(variance + 1e-05)
    return centred * rstd, rstd


def norm_back(grad, xhat, rstd, gain):
    dxhat = grad * gain
    first = jnp.mean(dxhat, axis=-1, keepdims=True)
    second = jnp.mean(dxhat * xhat, axis=-1, keepdims=True)
    return rstd * (dxhat - first - xhat * second)


def cdf_parts(u):
    z = jnp.abs(u)
    t = 1.0 / (1.0 + 0.23164189 * z)
    e = jnp.exp2(u * u * (-0.5 * LOG2E))
    poly = t * (
        0.127414796 + t * (-0.142248368 + t * (0.7107068705 + t * (-0.7265760135 + t * 0.5307027145)))
    )
    tail = poly * e
    return jnp.where(u < 0, tail, 1.0 - tail), e


def one_hot_rows(slot, start, size):
    length = slot.shape[1]
    rows = lax.broadcasted_iota(jnp.int32, (size, length), 0).astype(F32) + start
    return jnp.where(rows == slot, 1.0, 0.0)


def unpermute(slot, src_ref, out_ref):
    length = slot.shape[1]
    wide = jnp.transpose(jnp.broadcast_to(slot, (LANES, length)))
    step = 256
    for start in range(0, length, step):
        col = wide[start : start + step, :1]
        cols = lax.broadcasted_iota(jnp.int32, (step, length), 1).astype(F32)
        pick = jnp.where(cols == col, 1.0, 0.0).astype(BF16)
        out_ref[start : start + step, :] = dot(pick, src_ref[...]).astype(BF16)


def slots_of(mask_ref):
    length = mask_ref.shape[1]
    step = 256
    mask8 = jnp.broadcast_to(mask_ref[...], (8, length))
    cum = []
    for start in range(0, length, step):
        up = lax.broadcasted_iota(jnp.int32, (length, step), 0)
        to = lax.broadcasted_iota(jnp.int32, (length, step), 1) + start
        cum.append(dot(mask8.astype(BF16), jnp.where(up <= to, 1.0, 0.0).astype(BF16)))
    cum = jnp.concatenate(cum, axis=1)
    count = jnp.sum(mask8, axis=1, keepdims=True)
    pos = lax.broadcasted_iota(jnp.int32, (8, length), 1).astype(F32)
    return jnp.where(mask8 > 0.5, cum - 1.0, count + pos - cum), count


def permute_rows(tokens_ref, slot, xp_ref):
    step = 256

    def body(i, _):
        rows = pl.ds(pl.multiple_of(i * step, step), step)
        pick = one_hot_rows(slot[:1], (i * step).astype(F32), step).astype(BF16)
        xp_ref[rows, :] = dot(pick, tokens_ref[...]).astype(BF16)
        return 0

    lax.fori_loop(0, tokens_ref.shape[0] // step, body, 0)


def first_norm(xp_ref, vec_ref, h1_ref):
    step = 128
    gain = vec_ref[0:1, :]
    shift = vec_ref[1:2, :]

    def body(i, _):
        rows = pl.ds(pl.multiple_of(i * step, step), step)
        xhat, _ = norm_stats(xp_ref[rows, :].astype(F32))
        h1_ref[rows, :] = (xhat * gain + shift).astype(BF16)
        return 0

    lax.fori_loop(0, xp_ref.shape[0] // step, body, 0)


def project(h1_ref, vec_ref, wqkv_ref, qkv_ref):
    length, width = h1_ref.shape
    step = 256
    bq = vec_ref[2:3, :]
    bv = vec_ref[3:4, :]

    def body(i, _):
        rows = pl.ds(pl.multiple_of(i * step, step), step)
        h1 = h1_ref[rows, :]
        qkv_ref[rows, :width] = (dot(h1, wqkv_ref[:, :width]) + bq).astype(BF16)
        qkv_ref[rows, width : 2 * width] = dot(h1, wqkv_ref[:, width : 2 * width]).astype(BF16)
        qkv_ref[rows, 2 * width :] = (dot(h1, wqkv_ref[:, 2 * width :]) + bv).astype(BF16)
        return 0

    lax.fori_loop(0, length // step, body, 0)


def attend(qkv_ref, o_ref, lse_ref, beside):
    length, width = o_ref.shape
    step = 256
    c = SCALE * LOG2E
    lane = lax.broadcasted_iota(jnp.int32, (step, LANES), 1)

    def body(n, _):
        beside(n)
        t = n // (length // step)
        i = n % (length // step)
        rows = pl.ds(pl.multiple_of(i * step, step), step)
        q = qkv_ref[rows, pl.ds(pl.multiple_of(t * LANES, LANES), LANES)]
        k = qkv_ref[:, pl.ds(pl.multiple_of(width + t * LANES, LANES), LANES)]
        v = qkv_ref[:, pl.ds(pl.multiple_of(2 * width + t * LANES, LANES), LANES)]
        vo = jnp.concatenate([v, jnp.ones_like(v)], axis=1)
        out = jnp.zeros((step, LANES), F32)
        lses = jnp.zeros((step, LANES), F32)
        for h in range(GROUP):
            mine = lane // HEAD_DIM == h
            s = dot(jnp.where(mine, q, jnp.zeros_like(q)), k, NT)
            top = jnp.max(s, axis=-1, keepdims=True)
            p = jnp.exp2((s - top) * c).astype(BF16)
            ov = dot(p, vo)
            total = ov[:, LANES:]
            out = jnp.where(mine, ov[:, :LANES] / total, out)
            lses = jnp.where(lane == h, top * c + jnp.log2(total), lses)
        o_ref[rows, pl.ds(pl.multiple_of(t * LANES, LANES), LANES)] = out.astype(BF16)
        lse_ref[pl.ds(pl.multiple_of(t * 8, 8), 8), rows] = jnp.transpose(lses)[:8, :]
        return 0

    lax.fori_loop(0, (width // LANES) * (length // step), body, 0)


def join(xp_ref, o_ref, wout_ref, vec_ref, x1_ref):
    step = 256
    bout = vec_ref[4:5, :]

    def body(i, _):
        rows = pl.ds(pl.multiple_of(i * step, step), step)
        x1_ref[rows, :] = xp_ref[rows, :].astype(F32) + dot(o_ref[rows, :], wout_ref[...]) + bout
        return 0

    lax.fori_loop(0, xp_ref.shape[0] // step, body, 0)


def attn_kernel(
    tokens_ref, mask_ref, vec_ref, wqkv_ref, wout_ref,
    slot_ref, xp_ref, h1_ref, qkv_ref, o_ref, lse_ref, x1_ref,
):
    slot, _ = slots_of(mask_ref)
    slot_ref[...] = slot
    permute_rows(tokens_ref, slot, xp_ref)
    first_norm(xp_ref, vec_ref, h1_ref)
    project(h1_ref, vec_ref, wqkv_ref, qkv_ref)
    attend(qkv_ref, o_ref, lse_ref, lambda n: None)
    join(xp_ref, o_ref, wout_ref, vec_ref, x1_ref)


class Place:
    def __init__(self):
        self.me = me = lax.axis_index("fsdp")
        core = me % 2
        x = me // 2 % 2
        y = me // 4
        self.sib = me + 1 - 2 * core
        self.xn = me + 2 - 4 * x
        self.yn = me + 4 - 8 * y
        self.dg = me + 6 - 4 * x - 8 * y


def remote(src, dst, send, recv, to):
    return pltpu.make_async_remote_copy(
        src_ref=src, dst_ref=dst, send_sem=send, recv_sem=recv,
        device_id=to, device_id_type=pl.DeviceIdType.MESH,
    )


class Gather:
    def __init__(self, place, own, full, cut, send, recv, local):
        self.place = place
        rows = own.shape[0]
        at = lambda s, lo=0, hi=rows: full.at[pl.ds(pl.multiple_of(s * rows + lo, 16), hi - lo), :]
        me, sib, xn, yn, dg = place.me, place.sib, place.xn, place.yn, place.dg
        moves = [
            (own, at(me), sib), (own, at(me), xn), (own, at(me), yn),
            (at(xn), at(xn), sib), (at(yn), at(yn), sib),
            (at(xn, 0, cut), at(xn, 0, cut), yn), (at(yn, cut), at(yn, cut), xn),
            (at(dg, 0, cut), at(dg, 0, cut), sib), (at(dg, cut), at(dg, cut), sib),
        ]
        self.copies = [
            remote(src, dst, send.at[i], recv.at[i], {"fsdp": to}) for i, (src, dst, to) in enumerate(moves)
        ]
        self.local = pltpu.make_async_copy(own, at(me), local)

    def first(self):
        self.copies[1].start()
        self.copies[2].start()
        self.copies[0].start()
        self.local.start()

    def second(self):
        self.copies[1].wait_recv()
        self.copies[5].start()
        self.copies[3].start()
        self.copies[2].wait_recv()
        self.copies[6].start()
        self.copies[4].start()

    def third(self):
        self.copies[5].wait_recv()
        self.copies[7].start()
        self.copies[6].wait_recv()
        self.copies[8].start()

    def finish(self):
        for i in (0, 3, 4, 7, 8):
            self.copies[i].wait_recv()
        self.local.wait()
        for copy in self.copies:
            copy.wait_send()


def gather_attn_kernel(
    reps,
    tokens_ref, mask_ref, pack_ref, wqkv_in, wout_in, wup_in, wdn_in,
    slot_ref, xp_ref, h1_ref, qkv_ref, o_ref, lse_ref, x1_ref, vec_ref, bup_ref, over_ref,
    wqkv_ref, wout_ref, wup_ref, wdn_ref,
    packs, overs, send, recv, local, psend, precv, rsend, rrecv,
):
    width = tokens_ref.shape[1]
    share = wqkv_in.shape[0]
    place = Place()
    me = place.me
    rep = lax.axis_index("rep")
    shards = packs.shape[0]
    barrier = pltpu.get_barrier_semaphore()
    for d in range(1, shards):
        pl.semaphore_signal(
            barrier, inc=1, device_id={"fsdp": (me + d) % shards}, device_id_type=pl.DeviceIdType.MESH
        )
    for d in range(1, reps):
        pl.semaphore_signal(
            barrier, inc=1, device_id={"rep": (rep + d) % reps}, device_id_type=pl.DeviceIdType.MESH
        )
    slot, count = slots_of(mask_ref)
    slot_ref[...] = slot
    row = lax.broadcasted_iota(jnp.int32, (16, LANES), 0)
    over = jnp.where(count[:1] > FEW, 1.0, 0.0)
    packs[me] = jnp.where(row == 13, over, pack_ref[...].astype(F32)).astype(BF16)
    pl.semaphore_wait(barrier, shards + reps - 2)

    gathers = []
    for n, (own, full, cut) in enumerate(
        ((wqkv_in, wqkv_ref, 48), (wout_in, wout_ref, 32), (wup_in, wup_ref, 48), (wdn_in, wdn_ref, 320))
    ):
        gathers.append(Gather(place, own, full, cut, send.at[n], recv.at[n], local.at[n]))
    qkv, out, up, down = gathers
    vectors = []
    for d in range(1, shards):
        copy = remote(
            packs.at[me], packs.at[me], psend.at[d - 1], precv.at[d - 1], {"fsdp": (me + d) % shards}
        )
        copy.start()
        vectors.append(copy)
    qkv.first()
    permute_rows(tokens_ref, slot, xp_ref)
    for copy in vectors:
        copy.wait_recv()
    all_over = packs[0]
    for s in range(1, shards):
        all_over = jnp.maximum(all_over, packs[s])
    overs[rep] = all_over
    flags = []
    for d in range(1, reps):
        copy = remote(overs.at[rep], overs.at[rep], rsend.at[d - 1], rrecv.at[d - 1], {"rep": (rep + d) % reps})
        copy.start()
        flags.append(copy)
    qkv.second()
    out.first()
    up.first()
    vecs = jnp.zeros((16, width), F32)
    for s in range(shards):
        pack = packs[s]
        lane = lax.broadcasted_iota(jnp.int32, (LANES, width), 0)
        col = lax.broadcasted_iota(jnp.int32, (LANES, width), 1) - s * share
        spot = jnp.where((lane == col) & (lane < share), 1.0, 0.0).astype(BF16)
        vecs = vecs + dot(pack, spot)
        wide = pack.astype(F32)
        for r in range(width // LANES):
            bup_ref[0:1, s * width + r * LANES : s * width + (r + 1) * LANES] = wide[8 + r : 9 + r, :]
    vec_ref[...] = vecs[:8]
    first_norm(xp_ref, vec_ref, h1_ref)
    qkv.third()
    qkv.finish()
    project(h1_ref, vec_ref, wqkv_ref, qkv_ref)

    def beside(n):
        for at, step in (
            (0, out.second), (2, out.third), (4, up.second), (5, down.first), (9, up.third), (14, down.second),
            (18, down.third),
        ):
            pl.when(n == at)(step)

    attend(qkv_ref, o_ref, lse_ref, beside)
    out.finish()
    join(xp_ref, o_ref, wout_ref, vec_ref, x1_ref)
    for copy in flags:
        copy.wait()
    for copy in vectors:
        copy.wait_send()
    worst = overs[0]
    for z in range(1, reps):
        worst = jnp.maximum(worst, overs[z])
    over_ref[...] = worst[13:14, :].astype(F32)
    up.finish()
    down.finish()


def gather_attn(reps, shards, tokens, mask, pack, w_qkv, w_out, w_up, w_down):
    length, width = tokens.shape
    hidden = w_up.shape[1]
    sds = jax.ShapeDtypeStruct
    groups = width // LANES
    vmem = pl.BlockSpec(memory_space=pltpu.VMEM)
    hbm = pl.BlockSpec(memory_space=pl.ANY)
    dma = pltpu.SemaphoreType.DMA
    return pl.pallas_call(
        functools.partial(gather_attn_kernel, reps),
        in_specs=[vmem] * 3 + [hbm] * 4,
        out_specs=[vmem] * 12 + [hbm] * 2,
        out_shape=(
            sds((8, length), F32),
            sds((length, width), BF16),
            sds((length, width), BF16),
            sds((length, 3 * width), BF16),
            sds((length, width), BF16),
            sds((8 * groups, length), F32),
            sds((length, width), F32),
            sds((8, width), F32),
            sds((1, hidden), F32),
            sds((1, LANES), F32),
            sds((width, 3 * width), BF16),
            sds((width, width), BF16),
            sds((width, hidden), BF16),
            sds((hidden, width), BF16),
        ),
        scratch_shapes=[
            pltpu.VMEM((shards, 16, LANES), BF16),
            pltpu.VMEM((reps, 16, LANES), BF16),
            dma((4, 9)), dma((4, 9)), dma((4,)),
            dma((shards - 1,)), dma((shards - 1,)),
            dma((reps - 1,)), dma((reps - 1,)),
        ],
        compiler_params=pltpu.CompilerParams(
            vmem_limit_bytes=56 * MB, collective_id=0, has_side_effects=True
        ),
        name="gather_attn",
    )(tokens, mask, pack, w_qkv, w_out, w_up, w_down)


def attn_forward(tokens, mask, vecs, wqkv, wout):
    length, width = tokens.shape
    sds = jax.ShapeDtypeStruct
    groups = width // LANES
    return pl.pallas_call(
        attn_kernel,
        out_shape=(
            sds((8, length), F32),
            sds((length, width), BF16),
            sds((length, width), BF16),
            sds((length, 3 * width), BF16),
            sds((length, width), BF16),
            sds((8 * groups, length), F32),
            sds((length, width), F32),
        ),
        compiler_params=pltpu.CompilerParams(vmem_limit_bytes=56 * MB),
        name="attn_forward",
    )(tokens, mask, vecs, wqkv, wout)


def ffn_kernel(
    few,
    x1_ref, cot_ref, slot_ref, mask_ref, vec_ref, bup_ref, wup_ref, wdn_ref, wout_ref, o_ref,
    res_ref, gup_ref, gdn_ref, gbup_ref, g1_ref, do_ref, gout_ref, small_ref,
    acc, h2, h2t, gy, gyt, dh2, outp,
):
    j = pl.program_id(0)
    last = pl.num_programs(0) - 1
    length, width = x1_ref.shape
    gain = vec_ref[5:6, :]
    shift = vec_ref[6:7, :]
    bdown = vec_ref[7:8, :]
    blocks = []
    start = 0
    part = few if few <= 384 else 256
    while start < few:
        blocks.append((start, part, True))
        start += part
    while start < length:
        size = min(320, length - start)
        blocks.append((start, size, False))
        start += size

    @pl.when(j == 0)
    def _():
        for start, size, back in blocks:
            rows = slice(start, start + size)
            x1 = x1_ref[rows, :]
            xhat, _ = norm_stats(x1)
            hidden = (xhat * gain + shift).astype(BF16)
            h2[rows, :] = hidden
            acc[rows, :] = x1 + bdown
            if back:
                h2t[:, rows] = jnp.transpose(hidden)
                pick = one_hot_rows(slot_ref[0:1, :], float(start), size) * mask_ref[...]
                g = dot(pick.astype(BF16), cot_ref[...])
                gy[rows, :] = g.astype(BF16)
                gyt[:, rows] = jnp.transpose(g.astype(BF16))
                dh2[rows, :] = jnp.zeros((size, width), F32)

    gup = gdn = gbup = None
    for start, size, back in blocks:
        rows = slice(start, start + size)
        u = dot(h2[rows, :], wup_ref[...]) + bup_ref[...]
        cdf, e = cdf_parts(u)
        a = (u * cdf).astype(BF16)
        acc[rows, :] += dot(a, wdn_ref[...])
        if back:
            da = dot(gy[rows, :], wdn_ref[...], NT)
            du = ((cdf + u * e * 0.3989422804014327) * da).astype(BF16)
            p_up = dot(h2t[:, rows], du)
            p_dn = dot(gyt[:, rows], a)
            p_b = jnp.sum(du.astype(F32), axis=0, keepdims=True)
            gup = p_up if gup is None else gup + p_up
            gdn = p_dn if gdn is None else gdn + p_dn
            gbup = p_b if gbup is None else gbup + p_b
            dh2[rows, :] += dot(du, wup_ref[...], NT)
    gup_ref[...] = gup.astype(BF16)
    gdn_ref[...] = gdn.astype(BF16)
    gbup_ref[...] = gbup

    @pl.when(j == last)
    def _():
        ggain = gshift = gbdown = gbout = gout = jnp.zeros((1, 1), F32)
        for start, size, back in blocks:
            rows = slice(start, start + size)
            outp[rows, :] = acc[rows, :].astype(BF16)
            if back:
                xhat, rstd = norm_stats(x1_ref[rows, :])
                d = dh2[rows, :]
                g = gy[rows, :].astype(F32)
                g1 = g + norm_back(d, xhat, rstd, gain)
                g1_ref[rows, :] = g1
                g1b = g1.astype(BF16)
                do_ref[rows, :] = dot(g1b, wout_ref[...], NT).astype(BF16)
                gout = gout + dot(jnp.transpose(o_ref[rows, :]), g1b)
                ggain = ggain + jnp.sum(d * xhat, axis=0, keepdims=True)
                gshift = gshift + jnp.sum(d, axis=0, keepdims=True)
                gbdown = gbdown + jnp.sum(g, axis=0, keepdims=True)
                gbout = gbout + jnp.sum(g1b.astype(F32), axis=0, keepdims=True)
        gout_ref[...] = gout.astype(BF16)
        small_ref[0:1, :] = gbout
        small_ref[1:2, :] = ggain
        small_ref[2:3, :] = gshift
        small_ref[3:4, :] = gbdown
        small_ref[4:8, :] = jnp.zeros((4, width), F32)
        unpermute(slot_ref[0:1, :], outp, res_ref)


def feed_forward(few, x1, cot, slot, mask, vecs, bup, wup, wdn, wout, o):
    length, width = x1.shape
    hidden = wup.shape[1]
    fc = 512
    sds = jax.ShapeDtypeStruct
    whole = lambda *shape: pl.BlockSpec(shape, lambda j: (0,) * len(shape))
    return pl.pallas_call(
        functools.partial(ffn_kernel, few),
        grid=(hidden // fc,),
        in_specs=[
            whole(length, width),
            whole(length, width),
            whole(8, length),
            whole(1, length),
            whole(8, width),
            pl.BlockSpec((1, fc), lambda j: (0, j)),
            pl.BlockSpec((width, fc), lambda j: (0, j)),
            pl.BlockSpec((fc, width), lambda j: (j, 0)),
            whole(width, width),
            whole(few, width),
        ],
        out_specs=[
            whole(length, width),
            pl.BlockSpec((width, fc), lambda j: (0, j)),
            pl.BlockSpec((width, fc), lambda j: (0, j)),
            pl.BlockSpec((1, fc), lambda j: (0, j)),
            whole(few, width),
            whole(few, width),
            whole(width, width),
            whole(8, width),
        ],
        out_shape=(
            sds((length, width), BF16),
            sds((width, hidden), BF16),
            sds((width, hidden), BF16),
            sds((1, hidden), F32),
            sds((few, width), F32),
            sds((few, width), BF16),
            sds((width, width), BF16),
            sds((8, width), F32),
        ),
        scratch_shapes=[
            pltpu.VMEM((length, width), F32),
            pltpu.VMEM((length, width), BF16),
            pltpu.VMEM((width, few), BF16),
            pltpu.VMEM((few, width), BF16),
            pltpu.VMEM((width, few), BF16),
            pltpu.VMEM((few, width), F32),
            pltpu.VMEM((length, width), BF16),
        ],
        compiler_params=pltpu.CompilerParams(vmem_limit_bytes=56 * MB),
        name="feed_forward",
    )(x1, cot, slot, mask, vecs, bup, wup, wdn, wout, o)


def back_kernel(
    few,
    q_ref, k_ref, v_ref, do_ref, o_ref, lse_ref, h1_ref, xp_ref, vec_ref,
    wq_ref, wk_ref, wv_ref, g1_ref, slot_ref,
    gtok_ref, gq_ref, gk_ref, gv_ref, small_ref,
    h1t, dh1, dqt, dkv, gtp,
):
    t = pl.program_id(0)
    last = pl.num_programs(0) - 1
    length, width = h1_ref.shape
    groups = width // LANES
    step = 256
    c = SCALE * LOG2E
    gain = vec_ref[0:1, :]

    @pl.when(t == 0)
    def _():
        for start in range(0, length, step):
            h1t[:, start : start + step] = jnp.transpose(h1_ref[start : start + step, :])
        dh1[...] = jnp.zeros_like(dh1)

    q = q_ref[...]
    do = do_ref[...]
    lane = lax.broadcasted_iota(jnp.int32, (few, LANES), 1)
    head = lax.broadcasted_iota(jnp.int32, (8, LANES), 0)
    lane8 = lax.broadcasted_iota(jnp.int32, (8, LANES), 1)
    pick = jnp.where(lane8 // HEAD_DIM == head, 1.0, 0.0)
    delta = lax.dot_general(
        pick, do.astype(F32) * o_ref[...].astype(F32), NT,
        precision=lax.Precision.HIGHEST, preferred_element_type=F32,
    )
    dqt[...] = jnp.zeros_like(dqt)
    zero = jnp.zeros_like(q)
    qs = [jnp.where(lane // HEAD_DIM == h, q, zero) for h in range(GROUP)]
    dos = [jnp.where(lane // HEAD_DIM == h, do, zero) for h in range(GROUP)]

    def keys(i, _):
        rows = pl.ds(pl.multiple_of(i * step, step), step)
        k = k_ref[rows, :]
        v = v_ref[rows, :]
        kt = jnp.transpose(k)
        dk = jnp.zeros((step, LANES), F32)
        dv = jnp.zeros((step, LANES), F32)
        for h in range(GROUP):
            s = dot(k, qs[h], NT)
            p = jnp.exp2(s * c - lse_ref[h : h + 1, :])
            dp = dot(v, dos[h], NT)
            ds = (p * (dp - delta[h : h + 1, :])).astype(BF16)
            dv = dv + dot(p.astype(BF16), dos[h])
            dk = dk + dot(ds, qs[h])
            part = slice(h * HEAD_DIM, (h + 1) * HEAD_DIM)
            dqt[part, :] += dot(kt[part, :], ds)
        dkv[rows, :LANES] = (dk * SCALE).astype(BF16)
        dkv[rows, LANES:] = dv.astype(BF16)
        return 0

    lax.fori_loop(0, length // step, keys, 0)
    dq = (jnp.transpose(dqt[...]) * SCALE).astype(BF16)
    gq_ref[...] = dot(h1t[:, :few], dq).astype(BF16)
    gkv = dot(h1t[...], dkv[...]).astype(BF16)
    gk_ref[...] = gkv[:, :LANES]
    gv_ref[...] = gkv[:, LANES:]
    small_ref[0:1, :] = jnp.zeros((1, LANES), F32)
    small_ref[2:3, :] = jnp.sum(dq.astype(F32), axis=0, keepdims=True)
    small_ref[3:4, :] = jnp.sum(dkv[:, LANES:].astype(F32), axis=0, keepdims=True)
    wkv = jnp.concatenate([wk_ref[...], wv_ref[...]], axis=1)
    for start in range(0, length, step):
        rows = slice(start, start + step)
        dh1[rows, :] += dot(dkv[rows, :], wkv, NT)
    dh1[:few, :] += dot(dq, wq_ref[...], NT)


def back_finish(
    few,
    dh1_ref, xp_ref, vec_ref, g1_ref, slot_ref, gtok_ref, small_ref, gtp,
):
    length, width = xp_ref.shape
    gain = vec_ref[0:1, :]
    step = 128
    ggain = gshift = jnp.zeros((1, width), F32)
    for start in range(0, length, step):
        rows = slice(start, start + step)
        xhat, rstd = norm_stats(xp_ref[rows, :].astype(F32))
        d = dh1_ref[rows, :]
        g = norm_back(d, xhat, rstd, gain)
        if start < few:
            g = g + g1_ref[rows, :]
        gtp[rows, :] = g.astype(BF16)
        ggain = ggain + jnp.sum(d * xhat, axis=0, keepdims=True)
        gshift = gshift + jnp.sum(d, axis=0, keepdims=True)
    small_ref[0:1, :] = ggain
    small_ref[1:2, :] = gshift
    unpermute(slot_ref[0:1, :], gtp, gtok_ref)


def back_all(few, *refs):
    (q, k, v, do, o, lse, h1, xp, vec, wq, wk, wv, g1, slot,
     gtok, gq, gk, gv, small, norms, h1t, dh1, dqt, dkv, gtp) = refs
    back_kernel(few, q, k, v, do, o, lse, h1, xp, vec, wq, wk, wv, g1, slot,
                gtok, gq, gk, gv, small, h1t, dh1, dqt, dkv, gtp)

    @pl.when(pl.program_id(0) == pl.num_programs(0) - 1)
    def _():
        norms[...] = jnp.zeros_like(norms)
        back_finish(few, dh1, xp, vec, g1, slot, gtok, norms, gtp)


def attn_backward(few, qkv, do, o, lse, h1, xp, vecs, wqkv, g1, slot):
    length, width = h1.shape
    groups = width // LANES
    sds = jax.ShapeDtypeStruct
    whole = lambda *shape: pl.BlockSpec(shape, lambda t: (0,) * len(shape))
    cols = lambda rows, first: pl.BlockSpec((rows, LANES), lambda t: (0, first + t))
    return pl.pallas_call(
        functools.partial(back_all, few),
        grid=(groups,),
        in_specs=[
            cols(few, 0),
            cols(length, groups),
            cols(length, 2 * groups),
            cols(few, 0),
            cols(few, 0),
            pl.BlockSpec((8, few), lambda t: (t, 0)),
            whole(length, width),
            whole(length, width),
            whole(8, width),
            cols(width, 0),
            cols(width, groups),
            cols(width, 2 * groups),
            whole(few, width),
            whole(8, length),
        ],
        out_specs=[
            whole(length, width),
            cols(width, 0),
            cols(width, 0),
            cols(width, 0),
            cols(8, 0),
            whole(8, width),
        ],
        out_shape=(
            sds((length, width), BF16),
            sds((width, width), BF16),
            sds((width, width), BF16),
            sds((width, width), BF16),
            sds((8, width), F32),
            sds((8, width), F32),
        ),
        scratch_shapes=[
            pltpu.VMEM((width, length), BF16),
            pltpu.VMEM((length, width), F32),
            pltpu.VMEM((LANES, few), F32),
            pltpu.VMEM((length, 2 * LANES), BF16),
            pltpu.VMEM((length, width), BF16),
        ],
        compiler_params=pltpu.CompilerParams(vmem_limit_bytes=56 * MB),
        name="attn_backward",
    )(qkv, qkv, qkv, do, o, lse, h1, xp, vecs, wqkv, wqkv, wqkv, g1, slot)


def local(
    reps, shards,
    tokens, masked, cotangent, norm1_gain, norm1_shift, w_qkv, bias_query, bias_value, w_out,
    bias_out, norm2_gain, norm2_shift, w_up, bias_up, w_down, bias_down,
):
    seqs, length, width = tokens.shape
    hidden = w_up.shape[1]
    share = w_qkv.shape[0]
    close = shards == 8 and share % 16 == 0 and share <= LANES and w_down.shape[0] == width
    x = tokens.reshape(seqs * length, width)
    cot = cotangent.reshape(seqs * length, width)
    mask = masked.astype(F32)
    if close:
        pack = jnp.concatenate(
            [
                jnp.pad(
                    jnp.stack(
                        [norm1_gain, norm1_shift, bias_query, bias_value, bias_out, norm2_gain, norm2_shift, bias_down]
                    ),
                    ((0, 0), (0, LANES - share)),
                ),
                jnp.pad(bias_up.reshape(-1, LANES), ((0, 3), (0, 0))),
            ]
        )
        slot, xp, h1, qkv, o, lse, x1, vecs, bup, over, wqkv, wout, wup, wdn = gather_attn(
            reps, shards, x, mask, pack, w_qkv, w_out, w_up, w_down
        )
        small_enough = over[0, 0] < 0.5
    else:
        small_enough = lax.pmax(jnp.sum(masked), ("rep", "fsdp")) <= FEW
        packed = jnp.stack(
            [norm1_gain, norm1_shift, bias_query, bias_value, bias_out, norm2_gain, norm2_shift, bias_down]
        )
        vecs = lax.all_gather(packed, "fsdp", axis=1, tiled=True).astype(F32)
        bup = lax.all_gather(bias_up, "fsdp", axis=0, tiled=True).astype(F32).reshape(1, hidden)
        gather = lambda w: lax.all_gather(w, "fsdp", axis=0, tiled=True)
        wqkv, wout, wup, wdn = gather(w_qkv), gather(w_out), gather(w_up), gather(w_down)
        slot, xp, h1, qkv, o, lse, x1 = attn_forward(x, mask, vecs, wqkv, wout)

    def backward(few):
        def run():
            res, gup, gdn, gbup, g1, do, gout, small2 = feed_forward(
                few, x1, cot, slot, mask, vecs, bup, wup, wdn, wout, o
            )
            gtok, gq, gk, gv, small1, norms = attn_backward(
                few, qkv, do, o, lse, h1, xp, vecs, wqkv, g1, slot
            )
            small = jnp.concatenate(
                [norms[:2], small1[2:4], small2[:4], gbup.reshape(8, width)], axis=0
            )
            return res, gtok, gup, gdn, gout, gq, gk, gv, small

        return run

    res, gtok, gup, gdn, gout, gq, gk, gv, small = lax.cond(
        small_enough, backward(FEW), backward(length)
    )

    def scatter(g, dim):
        part = lax.psum_scatter(g, "fsdp", scatter_dimension=dim, tiled=True)
        return lax.psum(part, "rep").astype(F32)

    gup = scatter(gup, 0)
    gdn = jnp.transpose(scatter(gdn, 1))
    gattn = scatter(jnp.concatenate([gout, gq, gk, gv], axis=1), 0)
    gout, gqkv = gattn[:, :width], gattn[:, width:]
    small = lax.psum(small, ("rep", "fsdp"))
    me = lax.axis_index("fsdp")
    mine = lax.dynamic_slice_in_dim(small[:8], me * share, share, axis=1)
    gbup = lax.dynamic_slice_in_dim(small[8:].reshape(hidden), me * bias_up.shape[0], bias_up.shape[0])
    return (
        res.reshape(seqs, length, width),
        gtok.reshape(seqs, length, width),
        mine[0], mine[1], gqkv, mine[2], mine[3], gout, mine[4], mine[5], mine[6],
        gup, gbup, gdn, mine[7],
    )


def solution(mesh):
    rows3 = P(("rep", "fsdp"), None, None)
    vec = P("fsdp")
    mat = P("fsdp", None)
    in_specs = (
        rows3, P(("rep", "fsdp"), None), rows3,
        vec, vec, mat, vec, vec, mat, vec, vec, vec, mat, vec, mat, vec,
    )
    out_specs = (rows3, rows3, vec, vec, mat, vec, vec, mat, vec, vec, vec, mat, vec, mat, vec)
    body = functools.partial(local, mesh.shape["rep"], mesh.shape["fsdp"])
    return jax.shard_map(body, mesh=mesh, in_specs=in_specs, out_specs=out_specs, check_vma=False)
```

```python
import functools

import jax
import jax.numpy as jnp
from jax import lax
from jax.experimental import pallas as pl
from jax.experimental.pallas import tpu as pltpu
from jax.sharding import PartitionSpec as P

HEADS = 20
HEAD_DIM = 32
GROUP = 4
LANES = 128
SCALE = HEAD_DIM ** (-0.5)
LOG2E = 1.4426950408889634
FEW = 384
F32 = jnp.float32
BF16 = jnp.bfloat16
MB = 1024 * 1024

NN = (((1,), (0,)), ((), ()))
NT = (((1,), (1,)), ((), ()))


def dot(a, b, dims=NN):
    return lax.dot_general(a, b, dims, preferred_element_type=F32)


def norm_stats(x):
    mean = jnp.mean(x, axis=-1, keepdims=True)
    centred = x - mean
    variance = jnp.mean(centred * centred, axis=-1, keepdims=True)
    rstd = lax.rsqrt(variance + 1e-05)
    return centred * rstd, rstd


def norm_back(grad, xhat, rstd, gain):
    dxhat = grad * gain
    first = jnp.mean(dxhat, axis=-1, keepdims=True)
    second = jnp.mean(dxhat * xhat, axis=-1, keepdims=True)
    return rstd * (dxhat - first - xhat * second)


def cdf_parts(u):
    z = jnp.abs(u)
    t = 1.0 / (1.0 + 0.23164189 * z)
    e = jnp.exp2(u * u * (-0.5 * LOG2E))
    poly = t * (
        0.127414796 + t * (-0.142248368 + t * (0.7107068705 + t * (-0.7265760135 + t * 0.5307027145)))
    )
    tail = poly * e
    return jnp.where(u < 0, tail, 1.0 - tail), e


def one_hot_rows(slot, start, size):
    length = slot.shape[1]
    rows = lax.broadcasted_iota(jnp.int32, (size, length), 0).astype(F32) + start
    return jnp.where(rows == slot, 1.0, 0.0)


def unpermute(slot, src_ref, out_ref):
    length = slot.shape[1]
    wide = jnp.transpose(jnp.broadcast_to(slot, (LANES, length)))
    step = 256
    for start in range(0, length, step):
        col = wide[start : start + step, :1]
        cols = lax.broadcasted_iota(jnp.int32, (step, length), 1).astype(F32)
        pick = jnp.where(cols == col, 1.0, 0.0).astype(BF16)
        out_ref[start : start + step, :] = dot(pick, src_ref[...]).astype(BF16)


def slots_of(mask_ref):
    length = mask_ref.shape[1]
    step = 256
    mask8 = jnp.broadcast_to(mask_ref[...], (8, length))
    cum = []
    for start in range(0, length, step):
        up = lax.broadcasted_iota(jnp.int32, (length, step), 0)
        to = lax.broadcasted_iota(jnp.int32, (length, step), 1) + start
        cum.append(dot(mask8.astype(BF16), jnp.where(up <= to, 1.0, 0.0).astype(BF16)))
    cum = jnp.concatenate(cum, axis=1)
    count = jnp.sum(mask8, axis=1, keepdims=True)
    pos = lax.broadcasted_iota(jnp.int32, (8, length), 1).astype(F32)
    return jnp.where(mask8 > 0.5, cum - 1.0, count + pos - cum), count


def permute_rows(tokens_ref, slot, xp_ref):
    step = 256

    def body(i, _):
        rows = pl.ds(pl.multiple_of(i * step, step), step)
        pick = one_hot_rows(slot[:1], (i * step).astype(F32), step).astype(BF16)
        xp_ref[rows, :] = dot(pick, tokens_ref[...]).astype(BF16)
        return 0

    lax.fori_loop(0, tokens_ref.shape[0] // step, body, 0)


def first_norm(xp_ref, vec_ref, h1_ref):
    step = 128
    gain = vec_ref[0:1, :]
    shift = vec_ref[1:2, :]

    def body(i, _):
        rows = pl.ds(pl.multiple_of(i * step, step), step)
        xhat, _ = norm_stats(xp_ref[rows, :].astype(F32))
        h1_ref[rows, :] = (xhat * gain + shift).astype(BF16)
        return 0

    lax.fori_loop(0, xp_ref.shape[0] // step, body, 0)


def project(h1_ref, vec_ref, wqkv_ref, qkv_ref):
    length, width = h1_ref.shape
    step = 256
    bq = vec_ref[2:3, :]
    bv = vec_ref[3:4, :]

    def body(i, _):
        rows = pl.ds(pl.multiple_of(i * step, step), step)
        h1 = h1_ref[rows, :]
        qkv_ref[rows, :width] = (dot(h1, wqkv_ref[:, :width]) + bq).astype(BF16)
        qkv_ref[rows, width : 2 * width] = dot(h1, wqkv_ref[:, width : 2 * width]).astype(BF16)
        qkv_ref[rows, 2 * width :] = (dot(h1, wqkv_ref[:, 2 * width :]) + bv).astype(BF16)
        return 0

    lax.fori_loop(0, length // step, body, 0)


def attend(qkv_ref, o_ref, lse_ref, beside):
    length, width = o_ref.shape
    step = 256
    c = SCALE * LOG2E
    lane = lax.broadcasted_iota(jnp.int32, (step, LANES), 1)

    def body(n, _):
        beside(n)
        t = n // (length // step)
        i = n % (length // step)
        rows = pl.ds(pl.multiple_of(i * step, step), step)
        q = qkv_ref[rows, pl.ds(pl.multiple_of(t * LANES, LANES), LANES)]
        k = qkv_ref[:, pl.ds(pl.multiple_of(width + t * LANES, LANES), LANES)]
        v = qkv_ref[:, pl.ds(pl.multiple_of(2 * width + t * LANES, LANES), LANES)]
        vo = jnp.concatenate([v, jnp.ones_like(v)], axis=1)
        out = jnp.zeros((step, LANES), F32)
        lses = jnp.zeros((step, LANES), F32)
        for h in range(GROUP):
            mine = lane // HEAD_DIM == h
            s = dot(jnp.where(mine, q, jnp.zeros_like(q)), k, NT)
            top = jnp.max(s, axis=-1, keepdims=True)
            p = jnp.exp2((s - top) * c).astype(BF16)
            ov = dot(p, vo)
            total = ov[:, LANES:]
            out = jnp.where(mine, ov[:, :LANES] / total, out)
            lses = jnp.where(lane == h, top * c + jnp.log2(total), lses)
        o_ref[rows, pl.ds(pl.multiple_of(t * LANES, LANES), LANES)] = out.astype(BF16)
        lse_ref[pl.ds(pl.multiple_of(t * 8, 8), 8), rows] = jnp.transpose(lses)[:8, :]
        return 0

    lax.fori_loop(0, (width // LANES) * (length // step), body, 0)


def join(xp_ref, o_ref, wout_ref, vec_ref, x1_ref):
    step = 256
    bout = vec_ref[4:5, :]

    def body(i, _):
        rows = pl.ds(pl.multiple_of(i * step, step), step)
        x1_ref[rows, :] = xp_ref[rows, :].astype(F32) + dot(o_ref[rows, :], wout_ref[...]) + bout
        return 0

    lax.fori_loop(0, xp_ref.shape[0] // step, body, 0)


def attn_kernel(
    tokens_ref, mask_ref, vec_ref, wqkv_ref, wout_ref,
    slot_ref, xp_ref, h1_ref, qkv_ref, o_ref, lse_ref, x1_ref,
):
    slot, _ = slots_of(mask_ref)
    slot_ref[...] = slot
    permute_rows(tokens_ref, slot, xp_ref)
    first_norm(xp_ref, vec_ref, h1_ref)
    project(h1_ref, vec_ref, wqkv_ref, qkv_ref)
    attend(qkv_ref, o_ref, lse_ref, lambda n: None)
    join(xp_ref, o_ref, wout_ref, vec_ref, x1_ref)


class Place:
    def __init__(self):
        self.me = me = lax.axis_index("fsdp")
        core = me % 2
        x = me // 2 % 2
        y = me // 4
        self.sib = me + 1 - 2 * core
        self.xn = me + 2 - 4 * x
        self.yn = me + 4 - 8 * y
        self.dg = me + 6 - 4 * x - 8 * y


def remote(src, dst, send, recv, to):
    return pltpu.make_async_remote_copy(
        src_ref=src, dst_ref=dst, send_sem=send, recv_sem=recv,
        device_id=to, device_id_type=pl.DeviceIdType.MESH,
    )


class Gather:
    def __init__(self, place, own, full, cut, send, recv, local):
        self.place = place
        rows = own.shape[0]
        at = lambda s, lo=0, hi=rows: full.at[pl.ds(pl.multiple_of(s * rows + lo, 16), hi - lo), :]
        me, sib, xn, yn, dg = place.me, place.sib, place.xn, place.yn, place.dg
        moves = [
            (own, at(me), sib), (own, at(me), xn), (own, at(me), yn),
            (at(xn), at(xn), sib), (at(yn), at(yn), sib),
            (at(xn, 0, cut), at(xn, 0, cut), yn), (at(yn, cut), at(yn, cut), xn),
            (at(dg, 0, cut), at(dg, 0, cut), sib), (at(dg, cut), at(dg, cut), sib),
        ]
        self.copies = [
            remote(src, dst, send.at[i], recv.at[i], {"fsdp": to}) for i, (src, dst, to) in enumerate(moves)
        ]
        self.local = pltpu.make_async_copy(own, at(me), local)

    def first(self):
        self.copies[1].start()
        self.copies[2].start()
        self.copies[0].start()
        self.local.start()

    def second(self):
        self.copies[1].wait_recv()
        self.copies[5].start()
        self.copies[3].start()
        self.copies[2].wait_recv()
        self.copies[6].start()
        self.copies[4].start()

    def third(self):
        self.copies[5].wait_recv()
        self.copies[7].start()
        self.copies[6].wait_recv()
        self.copies[8].start()

    def finish(self):
        for i in (0, 3, 4, 7, 8):
            self.copies[i].wait_recv()
        self.local.wait()
        for copy in self.copies:
            copy.wait_send()


def gather_attn_kernel(
    reps,
    tokens_ref, mask_ref, pack_ref, wqkv_in, wout_in, wup_in, wdn_in,
    slot_ref, xp_ref, h1_ref, qkv_ref, o_ref, lse_ref, x1_ref, vec_ref, bup_ref, over_ref,
    wqkv_ref, wout_ref, wup_ref, wdn_ref,
    packs, overs, send, recv, local, psend, precv, rsend, rrecv,
):
    width = tokens_ref.shape[1]
    share = wqkv_in.shape[0]
    place = Place()
    me = place.me
    rep = lax.axis_index("rep")
    shards = packs.shape[0]
    barrier = pltpu.get_barrier_semaphore()
    for d in range(1, shards):
        pl.semaphore_signal(
            barrier, inc=1, device_id={"fsdp": (me + d) % shards}, device_id_type=pl.DeviceIdType.MESH
        )
    for d in range(1, reps):
        pl.semaphore_signal(
            barrier, inc=1, device_id={"rep": (rep + d) % reps}, device_id_type=pl.DeviceIdType.MESH
        )
    slot, count = slots_of(mask_ref)
    slot_ref[...] = slot
    row = lax.broadcasted_iota(jnp.int32, (16, LANES), 0)
    over = jnp.where(count[:1] > FEW, 1.0, 0.0)
    packs[me] = jnp.where(row == 13, over, pack_ref[...].astype(F32)).astype(BF16)
    pl.semaphore_wait(barrier, shards + reps - 2)

    gathers = []
    for n, (own, full, cut) in enumerate(
        ((wqkv_in, wqkv_ref, 48), (wout_in, wout_ref, 32), (wup_in, wup_ref, 48), (wdn_in, wdn_ref, 320))
    ):
        gathers.append(Gather(place, own, full, cut, send.at[n], recv.at[n], local.at[n]))
    qkv, out, up, down = gathers
    vectors = []
    for d in range(1, shards):
        copy = remote(
            packs.at[me], packs.at[me], psend.at[d - 1], precv.at[d - 1], {"fsdp": (me + d) % shards}
        )
        copy.start()
        vectors.append(copy)
    qkv.first()
    permute_rows(tokens_ref, slot, xp_ref)
    for copy in vectors:
        copy.wait_recv()
    all_over = packs[0]
    for s in range(1, shards):
        all_over = jnp.maximum(all_over, packs[s])
    overs[rep] = all_over
    flags = []
    for d in range(1, reps):
        copy = remote(overs.at[rep], overs.at[rep], rsend.at[d - 1], rrecv.at[d - 1], {"rep": (rep + d) % reps})
        copy.start()
        flags.append(copy)
    qkv.second()
    out.first()
    up.first()
    vecs = jnp.zeros((16, width), F32)
    for s in range(shards):
        pack = packs[s]
        lane = lax.broadcasted_iota(jnp.int32, (LANES, width), 0)
        col = lax.broadcasted_iota(jnp.int32, (LANES, width), 1) - s * share
        spot = jnp.where((lane == col) & (lane < share), 1.0, 0.0).astype(BF16)
        vecs = vecs + dot(pack, spot)
        wide = pack.astype(F32)
        for r in range(width // LANES):
            bup_ref[0:1, s * width + r * LANES : s * width + (r + 1) * LANES] = wide[8 + r : 9 + r, :]
    vec_ref[...] = vecs[:8]
    first_norm(xp_ref, vec_ref, h1_ref)
    qkv.third()
    qkv.finish()
    project(h1_ref, vec_ref, wqkv_ref, qkv_ref)

    def beside(n):
        for at, step in (
            (0, out.second), (2, out.third), (4, up.second), (5, down.first), (9, up.third), (14, down.second),
            (18, down.third),
        ):
            pl.when(n == at)(step)

    attend(qkv_ref, o_ref, lse_ref, beside)
    out.finish()
    join(xp_ref, o_ref, wout_ref, vec_ref, x1_ref)
    for copy in flags:
        copy.wait()
    for copy in vectors:
        copy.wait_send()
    worst = overs[0]
    for z in range(1, reps):
        worst = jnp.maximum(worst, overs[z])
    over_ref[...] = worst[13:14, :].astype(F32)
    up.finish()
    down.finish()


def gather_attn(reps, shards, tokens, mask, pack, w_qkv, w_out, w_up, w_down):
    length, width = tokens.shape
    hidden = w_up.shape[1]
    sds = jax.ShapeDtypeStruct
    groups = width // LANES
    vmem = pl.BlockSpec(memory_space=pltpu.VMEM)
    hbm = pl.BlockSpec(memory_space=pl.ANY)
    dma = pltpu.SemaphoreType.DMA
    return pl.pallas_call(
        functools.partial(gather_attn_kernel, reps),
        in_specs=[vmem] * 3 + [hbm] * 4,
        out_specs=[vmem] * 12 + [hbm] * 2,
        out_shape=(
            sds((8, length), F32),
            sds((length, width), BF16),
            sds((length, width), BF16),
            sds((length, 3 * width), BF16),
            sds((length, width), BF16),
            sds((8 * groups, length), F32),
            sds((length, width), F32),
            sds((8, width), F32),
            sds((1, hidden), F32),
            sds((1, LANES), F32),
            sds((width, 3 * width), BF16),
            sds((width, width), BF16),
            sds((width, hidden), BF16),
            sds((hidden, width), BF16),
        ),
        scratch_shapes=[
            pltpu.VMEM((shards, 16, LANES), BF16),
            pltpu.VMEM((reps, 16, LANES), BF16),
            dma((4, 9)), dma((4, 9)), dma((4,)),
            dma((shards - 1,)), dma((shards - 1,)),
            dma((reps - 1,)), dma((reps - 1,)),
        ],
        compiler_params=pltpu.CompilerParams(
            vmem_limit_bytes=56 * MB, collective_id=0, has_side_effects=True
        ),
        name="gather_attn",
    )(tokens, mask, pack, w_qkv, w_out, w_up, w_down)


def attn_forward(tokens, mask, vecs, wqkv, wout):
    length, width = tokens.shape
    sds = jax.ShapeDtypeStruct
    groups = width // LANES
    return pl.pallas_call(
        attn_kernel,
        out_shape=(
            sds((8, length), F32),
            sds((length, width), BF16),
            sds((length, width), BF16),
            sds((length, 3 * width), BF16),
            sds((length, width), BF16),
            sds((8 * groups, length), F32),
            sds((length, width), F32),
        ),
        compiler_params=pltpu.CompilerParams(vmem_limit_bytes=56 * MB),
        name="attn_forward",
    )(tokens, mask, vecs, wqkv, wout)


def ffn_kernel(
    few,
    x1_ref, cot_ref, slot_ref, mask_ref, vec_ref, bup_ref, wup_ref, wdn_ref, wout_ref, o_ref,
    res_ref, gup_ref, gdn_ref, g1_ref, do_ref, gout_ref, small_ref,
    acc, h2, h2t, gy, gyt, dh2, outp,
):
    j = pl.program_id(0)
    last = pl.num_programs(0) - 1
    length, width = x1_ref.shape
    gain = vec_ref[5:6, :]
    shift = vec_ref[6:7, :]
    bdown = vec_ref[7:8, :]
    blocks = []
    start = 0
    part = few if few <= 384 else 256
    while start < few:
        blocks.append((start, part, True))
        start += part
    while start < length:
        size = min(320, length - start)
        blocks.append((start, size, False))
        start += size

    @pl.when(j == 0)
    def _():
        for start, size, back in blocks:
            rows = slice(start, start + size)
            x1 = x1_ref[rows, :]
            xhat, _ = norm_stats(x1)
            hidden = (xhat * gain + shift).astype(BF16)
            h2[rows, :] = hidden
            acc[rows, :] = x1 + bdown
            if back:
                h2t[:, rows] = jnp.transpose(hidden)
                pick = one_hot_rows(slot_ref[0:1, :], float(start), size) * mask_ref[...]
                g = dot(pick.astype(BF16), cot_ref[...])
                gy[rows, :] = g.astype(BF16)
                gyt[:, rows] = jnp.transpose(g.astype(BF16))
                dh2[rows, :] = jnp.zeros((size, width), F32)

    gup = gdn = gbup = None
    for start, size, back in blocks:
        rows = slice(start, start + size)
        u = dot(h2[rows, :], wup_ref[...]) + bup_ref[...]
        cdf, e = cdf_parts(u)
        a = (u * cdf).astype(BF16)
        acc[rows, :] += dot(a, wdn_ref[...])
        if back:
            da = dot(gy[rows, :], wdn_ref[...], NT)
            du = ((cdf + u * e * 0.3989422804014327) * da).astype(BF16)
            p_up = dot(h2t[:, rows], du)
            p_dn = dot(gyt[:, rows], a)
            p_b = jnp.sum(du.astype(F32), axis=0, keepdims=True)
            gup = p_up if gup is None else gup + p_up
            gdn = p_dn if gdn is None else gdn + p_dn
            gbup = p_b if gbup is None else gbup + p_b
            dh2[rows, :] += dot(du, wup_ref[...], NT)
    gup_ref[...] = gup.astype(BF16)
    for n in range(gdn_ref.shape[0]):
        cols = slice(n * width, (n + 1) * width)
        gdn_ref[n] = gdn[:, cols].astype(BF16)
        small_ref[pl.ds(j * gdn_ref.shape[0] + n, 1), :] = gbup[:, cols]

    @pl.when(j == last)
    def _():
        ggain = gshift = gbdown = gbout = gout = jnp.zeros((1, 1), F32)
        for start, size, back in blocks:
            rows = slice(start, start + size)
            outp[rows, :] = acc[rows, :].astype(BF16)
            if back:
                xhat, rstd = norm_stats(x1_ref[rows, :])
                d = dh2[rows, :]
                g = gy[rows, :].astype(F32)
                g1 = g + norm_back(d, xhat, rstd, gain)
                g1_ref[rows, :] = g1
                g1b = g1.astype(BF16)
                do_ref[rows, :] = dot(g1b, wout_ref[...], NT).astype(BF16)
                gout = gout + dot(jnp.transpose(o_ref[rows, :]), g1b)
                ggain = ggain + jnp.sum(d * xhat, axis=0, keepdims=True)
                gshift = gshift + jnp.sum(d, axis=0, keepdims=True)
                gbdown = gbdown + jnp.sum(g, axis=0, keepdims=True)
                gbout = gbout + jnp.sum(g1b.astype(F32), axis=0, keepdims=True)
        gout_ref[...] = gout.astype(BF16)
        small_ref[8:9, :] = gbout
        small_ref[9:10, :] = ggain
        small_ref[10:11, :] = gshift
        small_ref[11:12, :] = gbdown
        small_ref[12:16, :] = jnp.zeros((4, width), F32)
        unpermute(slot_ref[0:1, :], outp, res_ref)


def feed_forward(few, x1, cot, slot, mask, vecs, bup, wup, wdn, wout, o):
    length, width = x1.shape
    hidden = wup.shape[1]
    fc = 2 * width
    sds = jax.ShapeDtypeStruct
    whole = lambda *shape: pl.BlockSpec(shape, lambda j: (0,) * len(shape))
    return pl.pallas_call(
        functools.partial(ffn_kernel, few),
        grid=(hidden // fc,),
        in_specs=[
            whole(length, width),
            whole(length, width),
            whole(8, length),
            whole(1, length),
            whole(8, width),
            pl.BlockSpec((1, fc), lambda j: (0, j)),
            pl.BlockSpec((width, fc), lambda j: (0, j)),
            pl.BlockSpec((fc, width), lambda j: (j, 0)),
            whole(width, width),
            whole(few, width),
        ],
        out_specs=[
            whole(length, width),
            pl.BlockSpec((width, fc), lambda j: (0, j)),
            pl.BlockSpec((2, width, width), lambda j: (j, 0, 0)),
            whole(few, width),
            whole(few, width),
            whole(width, width),
            whole(16, width),
        ],
        out_shape=(
            sds((length, width), BF16),
            sds((width, hidden), BF16),
            sds((hidden // width, width, width), BF16),
            sds((few, width), F32),
            sds((few, width), BF16),
            sds((width, width), BF16),
            sds((16, width), F32),
        ),
        scratch_shapes=[
            pltpu.VMEM((length, width), F32),
            pltpu.VMEM((length, width), BF16),
            pltpu.VMEM((width, few), BF16),
            pltpu.VMEM((few, width), BF16),
            pltpu.VMEM((width, few), BF16),
            pltpu.VMEM((few, width), F32),
            pltpu.VMEM((length, width), BF16),
        ],
        compiler_params=pltpu.CompilerParams(vmem_limit_bytes=56 * MB),
        name="feed_forward",
    )(x1, cot, slot, mask, vecs, bup, wup, wdn, wout, o)


class Heads:
    step = 256

    def __init__(self, few, q_ref, k_ref, v_ref, do_ref, o_ref, lse_ref, dqt, dkv):
        self.k_ref, self.v_ref, self.lse_ref, self.dqt, self.dkv = k_ref, v_ref, lse_ref, dqt, dkv
        q = q_ref[...]
        do = do_ref[...]
        lane = lax.broadcasted_iota(jnp.int32, (few, LANES), 1)
        head = lax.broadcasted_iota(jnp.int32, (8, LANES), 0)
        lane8 = lax.broadcasted_iota(jnp.int32, (8, LANES), 1)
        pick = jnp.where(lane8 // HEAD_DIM == head, 1.0, 0.0)
        self.delta = lax.dot_general(
            pick, do.astype(F32) * o_ref[...].astype(F32), NT,
            precision=lax.Precision.HIGHEST, preferred_element_type=F32,
        )
        dqt[...] = jnp.zeros_like(dqt)
        zero = jnp.zeros_like(q)
        self.qs = [jnp.where(lane // HEAD_DIM == h, q, zero) for h in range(GROUP)]
        self.dos = [jnp.where(lane // HEAD_DIM == h, do, zero) for h in range(GROUP)]

    def keys(self, i):
        step = self.step
        rows = pl.ds(pl.multiple_of(i * step, step), step)
        k = self.k_ref[rows, :]
        v = self.v_ref[rows, :]
        kt = jnp.transpose(k)
        dk = jnp.zeros((step, LANES), F32)
        dv = jnp.zeros((step, LANES), F32)
        for h in range(GROUP):
            s = dot(k, self.qs[h], NT)
            p = jnp.exp2(s * (SCALE * LOG2E) - self.lse_ref[h : h + 1, :])
            dp = dot(v, self.dos[h], NT)
            ds = (p * (dp - self.delta[h : h + 1, :])).astype(BF16)
            dv = dv + dot(p.astype(BF16), self.dos[h])
            dk = dk + dot(ds, self.qs[h])
            part = slice(h * HEAD_DIM, (h + 1) * HEAD_DIM)
            self.dqt[part, :] += dot(kt[part, :], ds)
        self.dkv[rows, :LANES] = (dk * SCALE).astype(BF16)
        self.dkv[rows, LANES:] = dv.astype(BF16)


def transpose_rows(src_ref, out_ref):
    step = 256
    for start in range(0, src_ref.shape[0], step):
        out_ref[:, start : start + step] = jnp.transpose(src_ref[start : start + step, :])


def group_weights(few, dqt, dkv, h1t, small_ref, cols):
    dq = (jnp.transpose(dqt[...]) * SCALE).astype(BF16)
    gq = dot(h1t[:, :few], dq).astype(BF16)
    gkv = dot(h1t[...], dkv[...]).astype(BF16)
    small_ref[2:3, cols] = jnp.sum(dq.astype(F32), axis=0, keepdims=True)
    small_ref[3:4, cols] = jnp.sum(dkv[:, LANES:].astype(F32), axis=0, keepdims=True)
    return dq, gq, gkv[:, :LANES], gkv[:, LANES:]


def group_inputs(few, dq, dkv, wq_ref, wk_ref, wv_ref, dh1):
    step = 256
    wkv = jnp.concatenate([wk_ref[...], wv_ref[...]], axis=1)
    for start in range(0, dh1.shape[0], step):
        rows = slice(start, start + step)
        dh1[rows, :] += dot(dkv[rows, :], wkv, NT)
    dh1[:few, :] += dot(dq, wq_ref[...], NT)


def back_finish(few, dh1_ref, xp_ref, vec_ref, g1_ref, small_ref, gtp):
    length, width = xp_ref.shape
    gain = vec_ref[0:1, :]
    step = 128
    ggain = gshift = jnp.zeros((1, width), F32)
    for start in range(0, length, step):
        rows = slice(start, start + step)
        xhat, rstd = norm_stats(xp_ref[rows, :].astype(F32))
        d = dh1_ref[rows, :]
        g = norm_back(d, xhat, rstd, gain)
        if start < few:
            g = g + g1_ref[rows, :]
        gtp[rows, :] = g.astype(BF16)
        ggain = ggain + jnp.sum(d * xhat, axis=0, keepdims=True)
        gshift = gshift + jnp.sum(d, axis=0, keepdims=True)
    small_ref[0:1, :] = ggain
    small_ref[1:2, :] = gshift


def back_kernel(
    few,
    q, k, v, do, o, lse, h1, xp, vec, wq, wk, wv, g1, slot,
    gtok, gq_ref, gk_ref, gv_ref, small,
    h1t, dh1, dqt, dkv, gtp,
):
    t = pl.program_id(0)
    cols = pl.ds(pl.multiple_of(t * LANES, LANES), LANES)

    @pl.when(t == 0)
    def _():
        transpose_rows(h1, h1t)
        dh1[...] = jnp.zeros_like(dh1)
        small[...] = jnp.zeros_like(small)

    heads = Heads(few, q, k, v, do, o, lse, dqt, dkv)

    def body(i, _):
        heads.keys(i)
        return 0

    lax.fori_loop(0, h1.shape[0] // heads.step, body, 0)
    dq, gq, gk, gv = group_weights(few, dqt, dkv, h1t, small, cols)
    gq_ref[...] = gq
    gk_ref[...] = gk
    gv_ref[...] = gv
    group_inputs(few, dq, dkv, wq, wk, wv, dh1)

    @pl.when(t == pl.num_programs(0) - 1)
    def _():
        back_finish(few, dh1, xp, vec, g1, small, gtp)
        unpermute(slot[0:1, :], gtp, gtok)


def back_specs(few, length, width):
    groups = width // LANES
    whole = lambda *shape: pl.BlockSpec(shape, lambda t: (0,) * len(shape))
    cols = lambda rows, first: pl.BlockSpec((rows, LANES), lambda t: (0, first + t))
    in_specs = [
        cols(few, 0),
        cols(length, groups),
        cols(length, 2 * groups),
        cols(few, 0),
        cols(few, 0),
        pl.BlockSpec((8, few), lambda t: (t, 0)),
        whole(length, width),
        whole(length, width),
        whole(8, width),
        cols(width, 0),
        cols(width, groups),
        cols(width, 2 * groups),
        whole(few, width),
        whole(8, length),
    ]
    scratch = [
        pltpu.VMEM((width, length), BF16),
        pltpu.VMEM((length, width), F32),
        pltpu.VMEM((LANES, few), F32),
        pltpu.VMEM((length, 2 * LANES), BF16),
        pltpu.VMEM((length, width), BF16),
    ]
    return whole, cols, in_specs, scratch


def attn_backward(few, qkv, do, o, lse, h1, xp, vecs, wqkv, g1, slot):
    length, width = h1.shape
    sds = jax.ShapeDtypeStruct
    whole, cols, in_specs, scratch = back_specs(few, length, width)
    return pl.pallas_call(
        functools.partial(back_kernel, few),
        grid=(width // LANES,),
        in_specs=in_specs,
        out_specs=[whole(length, width), cols(width, 0), cols(width, 0), cols(width, 0), whole(8, width)],
        out_shape=(
            sds((length, width), BF16),
            sds((width, width), BF16),
            sds((width, width), BF16),
            sds((width, width), BF16),
            sds((8, width), F32),
        ),
        scratch_shapes=scratch,
        compiler_params=pltpu.CompilerParams(vmem_limit_bytes=56 * MB),
        name="attn_backward",
    )(qkv, qkv, qkv, do, o, lse, h1, xp, vecs, wqkv, wqkv, wqkv, g1, slot)


class Reduce:
    def __init__(self, place, rep, reps, mine, other, acc, near, side, last, depth, fin, sems):
        send, recv, local = sems
        self.rep, self.reps = rep, reps
        self.acc, self.near, self.side, self.last, self.depth, self.fin = acc, near, side, last, depth, fin
        chip = place.me // 2
        cx, cy, cd = place.xn // 2, place.yn // 2, place.dg // 2
        self.chip, self.cx, self.cy = chip, cx, cy
        fsdp = lambda d: {"fsdp": d}
        low, high = slice(0, 2), slice(2, 4)
        n = iter(range(100))
        def copy(src, dst, to):
            i = next(n)
            return remote(src, dst, send.at[i], recv.at[i], to)
        self.a = [copy(other[q], near.at[:, q], fsdp(place.sib)) for q in range(4)]
        self.own = [pltpu.make_async_copy(mine[q], acc.at[:, q], local.at[q]) for q in range(4)]
        self.b = [
            copy(acc.at[cx, low], side.at[0], fsdp(place.xn)),
            copy(acc.at[cy, high], side.at[2], fsdp(place.yn)),
            copy(acc.at[cd, low], side.at[1], fsdp(place.xn)),
            copy(acc.at[cd, high], side.at[3], fsdp(place.yn)),
        ]
        self.c = [
            copy(acc.at[cy, low], last.at[0], fsdp(place.yn)),
            copy(acc.at[cx, high], last.at[1], fsdp(place.xn)),
        ]
        peers = [(rep + d) % reps for d in range(1, reps)]
        self.d = [copy(acc.at[chip, z], depth.at[i], {"rep": z}) for i, z in enumerate(peers)]
        self.e = [copy(fin.at[rep], fin.at[rep], {"rep": z}) for z in peers]

    COPIES = 16

    def start(self):
        for x in self.a + self.own:
            x.start()

    def near_sum(self):
        for q in range(4):
            self.own[q].wait()
            self.a[q].wait_recv()
            for c in range(4):
                self.acc[c, q] = (self.acc[c, q].astype(F32) + self.near[c, q].astype(F32)).astype(BF16)
        for x in self.b:
            x.start()

    def add(self, c, half, part):
        for q in range(2):
            self.acc[c, half + q] = (self.acc[c, half + q].astype(F32) + part[q].astype(F32)).astype(BF16)

    def side_sum(self):
        for x in self.b:
            x.wait()
        self.add(self.cy, 0, self.side.at[1])
        self.c[0].start()
        self.add(self.cx, 2, self.side.at[3])
        self.c[1].start()
        self.add(self.chip, 0, self.side.at[0])
        self.add(self.chip, 2, self.side.at[2])

    def last_sum(self):
        for x in self.c:
            x.wait()
        self.add(self.chip, 0, self.last.at[0])
        self.add(self.chip, 2, self.last.at[1])
        for x in self.d:
            x.start()

    def depth_sum(self):
        total = self.acc[self.chip, self.rep].astype(F32)
        for i in range(self.reps - 1):
            self.d[i].wait()
            total = total + self.depth[i].astype(F32)
        self.fin[self.rep] = total.astype(BF16)
        for x in self.e:
            x.start()

    def finish(self):
        for x in self.e:
            x.wait()
        for x in self.a:
            x.wait_send()


class Small:
    def __init__(self, me, shards, rep, reps, rows, beside, depth, out, sems):
        psend, precv, rsend, rrecv = sems
        self.me, self.rep, self.rows, self.near, self.depth, self.out = me, rep, rows, beside, depth, out
        self.first = [
            remote(beside.at[me], beside.at[me], psend.at[d - 1], precv.at[d - 1], {"fsdp": (me + d) % shards})
            for d in range(1, shards)
        ]
        self.second = [
            remote(depth.at[rep], depth.at[rep], rsend.at[d - 1], rrecv.at[d - 1], {"rep": (rep + d) % reps})
            for d in range(1, reps)
        ]

    def start(self):
        self.near[self.me] = self.rows[...]
        for x in self.first:
            x.start()

    def middle(self):
        for x in self.first:
            x.wait()
        total = self.near[0]
        for s in range(1, self.near.shape[0]):
            total = total + self.near[s]
        self.depth[self.rep] = total
        for x in self.second:
            x.start()

    def finish(self):
        for x in self.second:
            x.wait()
        total = self.depth[0]
        for z in range(1, self.depth.shape[0]):
            total = total + self.depth[z]
        self.out[...] = total


def reduce_back_kernel(
    few, shards, reps,
    q, k, v, do, o, lse, h1, xp, vec, wq, wk, wv, g1, slot, early_ref, gout_ref, gup_ref, gdn_ref,
    gtok, gup_out, gdn_out, gqkv_out, gout_out, early_out, late_out,
    h1t, dh1, dqt, dkv, gtp, late, gqkv, fin, acc, near, side, last, depth, send, recv, local,
    enear, edepth, lnear, ldepth, es1, er1, es2, er2, ls1, lr1, ls2, lr2,
):
    t = pl.program_id(0)
    cols = pl.ds(pl.multiple_of(t * LANES, LANES), LANES)
    share = h1.shape[1] // shards
    width = h1.shape[1]
    place = Place()
    rep = lax.axis_index("rep")
    core = place.me % 2

    def quarter(n, side):
        u = n // 4
        if u < 2:
            return gup_ref.at[:, side, :, n * width : (n + 1) * width]
        if u < 4:
            return gdn_ref.at[:, side, (n - 8) * share : (n - 7) * share, :]
        return gout_ref.at[:, side] if n == 16 else gqkv.at[n - 17, :, side]

    units = []
    for u in range(5):
        sems = (send.at[u], recv.at[u], local.at[u])
        units.append(
            Reduce(
                place, rep, reps,
                [quarter(4 * u + n, core) for n in range(4)],
                [quarter(4 * u + n, 1 - core) for n in range(4)],
                acc.at[u], near.at[u], side.at[u], last.at[u], depth.at[u], fin.at[u], sems,
            )
        )
    early = Small(place.me, shards, rep, reps, early_ref, enear, edepth, early_out, (es1, er1, es2, er2))
    later = Small(place.me, shards, rep, reps, late, lnear, ldepth, late_out, (ls1, lr1, ls2, lr2))

    @pl.when(t == 0)
    def _():
        barrier = pltpu.get_barrier_semaphore()
        for d in range(1, shards):
            pl.semaphore_signal(
                barrier, inc=1, device_id={"fsdp": (place.me + d) % shards},
                device_id_type=pl.DeviceIdType.MESH,
            )
        for d in range(1, reps):
            pl.semaphore_signal(
                barrier, inc=1, device_id={"rep": (rep + d) % reps}, device_id_type=pl.DeviceIdType.MESH
            )
        pl.semaphore_wait(barrier, shards + reps - 2)
        for u in range(4):
            units[u].start()
        early.start()
        transpose_rows(h1, h1t)
        dh1[...] = jnp.zeros_like(dh1)
        late[...] = jnp.zeros_like(late)

    heads = Heads(few, q, k, v, do, o, lse, dqt, dkv)
    blocks = h1.shape[0] // heads.step

    plan = [
        (1, units[0].near_sum), (2, units[1].near_sum), (3, units[2].near_sum), (4, units[3].near_sum),
        (5, early.middle), (6, units[0].side_sum), (9, units[1].side_sum), (10, units[0].last_sum),
        (11, early.finish), (13, units[2].side_sum), (14, units[1].last_sum), (15, units[0].depth_sum),
        (17, units[3].side_sum), (18, units[2].last_sum), (19, units[1].depth_sum),
    ]

    def body(i, _):
        for at, step in plan:
            pl.when(t * blocks + i == at)(step)
        heads.keys(i)
        return 0

    lax.fori_loop(0, blocks, body, 0)
    dq, gq, gk, gv = group_weights(few, dqt, dkv, h1t, late, cols)
    chips = shards // 2
    for n, g in enumerate((gq, gk, gv)):
        gqkv[n, :, :, :, cols] = g.reshape(chips, 2, share, LANES)
    final = t == pl.num_programs(0) - 1
    pl.when(final)(units[4].start)
    group_inputs(few, dq, dkv, wq, wk, wv, dh1)

    @pl.when(final)
    def _():
        units[4].near_sum()
        units[3].last_sum()
        units[2].depth_sum()
        back_finish(few, dh1, xp, vec, g1, late, gtp)
        later.start()
        units[4].side_sum()
        units[3].depth_sum()
        units[4].last_sum()
        later.middle()
        unpermute(slot[0:1, :], gtp, gtok)
        units[4].depth_sum()
        for n in range(16):
            if n % 4 == 0:
                units[n // 4].finish()
            part = fin[n // 4, n % 4].astype(F32)
            if n < 8:
                gup_out[:, n * width : (n + 1) * width] = part
            else:
                gdn_out[:, (n - 8) * share : (n - 7) * share] = jnp.transpose(part)
        later.finish()
        units[4].finish()
        gout_out[...] = fin[4, 0].astype(F32)
        for n in range(3):
            gqkv_out[:, n * width : (n + 1) * width] = fin[4, 1 + n].astype(F32)


def reduce_backward(few, shards, reps, ident, qkv, do, o, lse, h1, xp, vecs, wqkv, g1, slot, early, gout, gup, gdn):
    length, width = h1.shape
    share = width // shards
    chips = shards // 2
    sds = jax.ShapeDtypeStruct
    whole, cols, in_specs, scratch = back_specs(few, length, width)
    hbm = pl.BlockSpec(memory_space=pl.ANY)
    dma = pltpu.SemaphoreType.DMA
    block = (share, width)
    copies = Reduce.COPIES
    hidden = gup.shape[1]
    return pl.pallas_call(
        functools.partial(reduce_back_kernel, few, shards, reps),
        grid=(width // LANES,),
        in_specs=in_specs + [whole(16, width), hbm, hbm, hbm],
        out_specs=[
            whole(length, width), whole(share, hidden), whole(width, width), whole(share, 3 * width),
            whole(share, width), whole(16, width), whole(8, width),
        ],
        out_shape=(
            sds((length, width), BF16),
            sds((share, hidden), F32),
            sds((width, width), F32),
            sds((share, 3 * width), F32),
            sds((share, width), F32),
            sds((16, width), F32),
            sds((8, width), F32),
        ),
        scratch_shapes=scratch
        + [
            pltpu.VMEM((8, width), F32),
            pltpu.VMEM((3, chips, 2) + block, BF16),
            pltpu.VMEM((5, 4) + block, BF16),
            pltpu.VMEM((5, chips, 4) + block, BF16),
            pltpu.VMEM((5, chips, 4) + block, BF16),
            pltpu.VMEM((5, 4, 2) + block, BF16),
            pltpu.VMEM((5, 2, 2) + block, BF16),
            pltpu.VMEM((5, reps - 1) + block, BF16),
            dma((5, copies)), dma((5, copies)), dma((5, 4)),
            pltpu.VMEM((shards, 16, width), F32),
            pltpu.VMEM((reps, 16, width), F32),
            pltpu.VMEM((shards, 8, width), F32),
            pltpu.VMEM((reps, 8, width), F32),
            dma((shards - 1,)), dma((shards - 1,)), dma((reps - 1,)), dma((reps - 1,)),
            dma((shards - 1,)), dma((shards - 1,)), dma((reps - 1,)), dma((reps - 1,)),
        ],
        compiler_params=pltpu.CompilerParams(
            vmem_limit_bytes=60 * MB, collective_id=ident, has_side_effects=True
        ),
        name="reduce_backward",
    )(
        qkv, qkv, qkv, do, o, lse, h1, xp, vecs, wqkv, wqkv, wqkv, g1, slot, early,
        gout.reshape(chips, 2, share, width),
        gup.reshape(chips, 2, share, hidden),
        gdn.reshape(chips, 2, width, width),
    )


def local(
    reps, shards,
    tokens, masked, cotangent, norm1_gain, norm1_shift, w_qkv, bias_query, bias_value, w_out,
    bias_out, norm2_gain, norm2_shift, w_up, bias_up, w_down, bias_down,
):
    seqs, length, width = tokens.shape
    hidden = w_up.shape[1]
    share = w_qkv.shape[0]
    close = shards == 8 and share % 16 == 0 and share <= LANES and w_down.shape[0] == width
    x = tokens.reshape(seqs * length, width)
    cot = cotangent.reshape(seqs * length, width)
    mask = masked.astype(F32)
    if close:
        pack = jnp.concatenate(
            [
                jnp.pad(
                    jnp.stack(
                        [norm1_gain, norm1_shift, bias_query, bias_value, bias_out, norm2_gain, norm2_shift, bias_down]
                    ),
                    ((0, 0), (0, LANES - share)),
                ),
                jnp.pad(bias_up.reshape(-1, LANES), ((0, 3), (0, 0))),
            ]
        )
        slot, xp, h1, qkv, o, lse, x1, vecs, bup, over, wqkv, wout, wup, wdn = gather_attn(
            reps, shards, x, mask, pack, w_qkv, w_out, w_up, w_down
        )
        small_enough = over[0, 0] < 0.5
    else:
        small_enough = lax.pmax(jnp.sum(masked), ("rep", "fsdp")) <= FEW
        packed = jnp.stack(
            [norm1_gain, norm1_shift, bias_query, bias_value, bias_out, norm2_gain, norm2_shift, bias_down]
        )
        vecs = lax.all_gather(packed, "fsdp", axis=1, tiled=True).astype(F32)
        bup = lax.all_gather(bias_up, "fsdp", axis=0, tiled=True).astype(F32).reshape(1, hidden)
        gather = lambda w: lax.all_gather(w, "fsdp", axis=0, tiled=True)
        wqkv, wout, wup, wdn = gather(w_qkv), gather(w_out), gather(w_up), gather(w_down)
        slot, xp, h1, qkv, o, lse, x1 = attn_forward(x, mask, vecs, wqkv, wout)

    def backward(few):
        def run():
            res, gup, gdn, g1, do, gout, early = feed_forward(
                few, x1, cot, slot, mask, vecs, bup, wup, wdn, wout, o
            )
            if close:
                gtok, gup, gdn, gqkv, gout, early, late = reduce_backward(
                    few, shards, reps, 1 if few == FEW else 2,
                    qkv, do, o, lse, h1, xp, vecs, wqkv, g1, slot, early, gout, gup, gdn,
                )
                return res, gtok, gup, gdn, gqkv, gout, early, late
            gtok, gq, gk, gv, late = attn_backward(
                few, qkv, do, o, lse, h1, xp, vecs, wqkv, g1, slot
            )
            return res, gtok, gup, gdn, jnp.concatenate([gout, gq, gk, gv], axis=1), early, late

        return run

    res, gtok, *grads, early, late = lax.cond(small_enough, backward(FEW), backward(length))

    if close:
        gup, gdn, gqkv, gout = grads
    else:
        def scatter(g, dim):
            part = lax.psum_scatter(g, "fsdp", scatter_dimension=dim, tiled=True)
            return lax.psum(part, "rep").astype(F32)

        gup, gdn, gattn = grads
        gup = scatter(gup, 0)
        gdn = scatter(gdn.transpose(0, 2, 1).reshape(hidden, width), 0)
        gattn = scatter(gattn, 0)
        gout, gqkv = gattn[:, :width], gattn[:, width:]
        early = lax.psum(early, ("rep", "fsdp"))
        late = lax.psum(late, ("rep", "fsdp"))
    me = lax.axis_index("fsdp")
    own = bias_up.shape[0]
    gbup = lax.dynamic_slice_in_dim(early[:8].reshape(hidden), me * own, own)
    mine = lax.dynamic_slice_in_dim(jnp.concatenate([late[:4], early[8:12]]), me * share, share, axis=1)
    return (
        res.reshape(seqs, length, width),
        gtok.reshape(seqs, length, width),
        mine[0], mine[1], gqkv, mine[2], mine[3], gout, mine[4], mine[5], mine[6],
        gup, gbup, gdn, mine[7],
    )


def solution(mesh):
    rows3 = P(("rep", "fsdp"), None, None)
    vec = P("fsdp")
    mat = P("fsdp", None)
    in_specs = (
        rows3, P(("rep", "fsdp"), None), rows3,
        vec, vec, mat, vec, vec, mat, vec, vec, vec, mat, vec, mat, vec,
    )
    out_specs = (rows3, rows3, vec, vec, mat, vec, vec, mat, vec, vec, vec, mat, vec, mat, vec)
    body = functools.partial(local, mesh.shape["rep"], mesh.shape["fsdp"])
    return jax.shard_map(body, mesh=mesh, in_specs=in_specs, out_specs=out_specs, check_vma=False)
```

```python
import functools

import jax
import jax.numpy as jnp
from jax import lax
from jax.experimental import pallas as pl
from jax.experimental.pallas import tpu as pltpu
from jax.sharding import PartitionSpec as P

HEADS = 20
HEAD_DIM = 32
GROUP = 4
LANES = 128
SCALE = HEAD_DIM ** (-0.5)
LOG2E = 1.4426950408889634
FEW = 384
F32 = jnp.float32
BF16 = jnp.bfloat16
MB = 1024 * 1024

NN = (((1,), (0,)), ((), ()))
NT = (((1,), (1,)), ((), ()))


def dot(a, b, dims=NN):
    return lax.dot_general(a, b, dims, preferred_element_type=F32)


def norm_stats(x):
    mean = jnp.mean(x, axis=-1, keepdims=True)
    centred = x - mean
    variance = jnp.mean(centred * centred, axis=-1, keepdims=True)
    rstd = lax.rsqrt(variance + 1e-05)
    return centred * rstd, rstd


def norm_back(grad, xhat, rstd, gain):
    dxhat = grad * gain
    first = jnp.mean(dxhat, axis=-1, keepdims=True)
    second = jnp.mean(dxhat * xhat, axis=-1, keepdims=True)
    return rstd * (dxhat - first - xhat * second)


def cdf_parts(u):
    z = jnp.abs(u)
    t = 1.0 / (1.0 + 0.23164189 * z)
    e = jnp.exp2(u * u * (-0.5 * LOG2E))
    poly = t * (
        0.127414796 + t * (-0.142248368 + t * (0.7107068705 + t * (-0.7265760135 + t * 0.5307027145)))
    )
    tail = poly * e
    return jnp.where(u < 0, tail, 1.0 - tail), e


def one_hot_rows(slot, start, size):
    length = slot.shape[1]
    rows = lax.broadcasted_iota(jnp.int32, (size, length), 0).astype(F32) + start
    return jnp.where(rows == slot, 1.0, 0.0)


def unpermute(slot, src_ref, out_ref):
    length = slot.shape[1]
    wide = jnp.transpose(jnp.broadcast_to(slot, (LANES, length)))
    step = 256
    for start in range(0, length, step):
        col = wide[start : start + step, :1]
        cols = lax.broadcasted_iota(jnp.int32, (step, length), 1).astype(F32)
        pick = jnp.where(cols == col, 1.0, 0.0).astype(BF16)
        out_ref[start : start + step, :] = dot(pick, src_ref[...]).astype(BF16)


def slots_of(mask_ref):
    length = mask_ref.shape[1]
    step = 256
    mask8 = jnp.broadcast_to(mask_ref[...], (8, length))
    cum = []
    for start in range(0, length, step):
        up = lax.broadcasted_iota(jnp.int32, (length, step), 0)
        to = lax.broadcasted_iota(jnp.int32, (length, step), 1) + start
        cum.append(dot(mask8.astype(BF16), jnp.where(up <= to, 1.0, 0.0).astype(BF16)))
    cum = jnp.concatenate(cum, axis=1)
    count = jnp.sum(mask8, axis=1, keepdims=True)
    pos = lax.broadcasted_iota(jnp.int32, (8, length), 1).astype(F32)
    return jnp.where(mask8 > 0.5, cum - 1.0, count + pos - cum), count


def permute_rows(tokens_ref, slot, xp_ref):
    step = 256

    def body(i, _):
        rows = pl.ds(pl.multiple_of(i * step, step), step)
        pick = one_hot_rows(slot[:1], (i * step).astype(F32), step).astype(BF16)
        xp_ref[rows, :] = dot(pick, tokens_ref[...]).astype(BF16)
        return 0

    lax.fori_loop(0, tokens_ref.shape[0] // step, body, 0)


def first_norm(xp_ref, vec_ref, h1_ref):
    step = 128
    gain = vec_ref[0:1, :]
    shift = vec_ref[1:2, :]

    def body(i, _):
        rows = pl.ds(pl.multiple_of(i * step, step), step)
        xhat, _ = norm_stats(xp_ref[rows, :].astype(F32))
        h1_ref[rows, :] = (xhat * gain + shift).astype(BF16)
        return 0

    lax.fori_loop(0, xp_ref.shape[0] // step, body, 0)


def project(h1_ref, vec_ref, wqkv_ref, qkv_ref):
    length, width = h1_ref.shape
    step = 256
    bq = vec_ref[2:3, :]
    bv = vec_ref[3:4, :]

    def body(i, _):
        rows = pl.ds(pl.multiple_of(i * step, step), step)
        h1 = h1_ref[rows, :]
        qkv_ref[rows, :width] = (dot(h1, wqkv_ref[:, :width]) + bq).astype(BF16)
        qkv_ref[rows, width : 2 * width] = dot(h1, wqkv_ref[:, width : 2 * width]).astype(BF16)
        qkv_ref[rows, 2 * width :] = (dot(h1, wqkv_ref[:, 2 * width :]) + bv).astype(BF16)
        return 0

    lax.fori_loop(0, length // step, body, 0)


def attend(qkv_ref, o_ref, lse_ref, beside):
    length, width = o_ref.shape
    step = 256
    c = SCALE * LOG2E
    lane = lax.broadcasted_iota(jnp.int32, (step, LANES), 1)

    def body(n, _):
        beside(n)
        t = n // (length // step)
        i = n % (length // step)
        rows = pl.ds(pl.multiple_of(i * step, step), step)
        q = qkv_ref[rows, pl.ds(pl.multiple_of(t * LANES, LANES), LANES)]
        k = qkv_ref[:, pl.ds(pl.multiple_of(width + t * LANES, LANES), LANES)]
        v = qkv_ref[:, pl.ds(pl.multiple_of(2 * width + t * LANES, LANES), LANES)]
        vo = jnp.concatenate([v, jnp.ones_like(v)], axis=1)
        out = jnp.zeros((step, LANES), F32)
        lses = jnp.zeros((step, LANES), F32)
        for h in range(GROUP):
            mine = lane // HEAD_DIM == h
            s = dot(jnp.where(mine, q, jnp.zeros_like(q)), k, NT)
            top = jnp.max(s, axis=-1, keepdims=True)
            p = jnp.exp2((s - top) * c).astype(BF16)
            ov = dot(p, vo)
            total = ov[:, LANES:]
            out = jnp.where(mine, ov[:, :LANES] / total, out)
            lses = jnp.where(lane == h, top * c + jnp.log2(total), lses)
        o_ref[rows, pl.ds(pl.multiple_of(t * LANES, LANES), LANES)] = out.astype(BF16)
        lse_ref[pl.ds(pl.multiple_of(t * 8, 8), 8), rows] = jnp.transpose(lses)[:8, :]
        return 0

    lax.fori_loop(0, (width // LANES) * (length // step), body, 0)


def join(xp_ref, o_ref, wout_ref, vec_ref, x1_ref):
    step = 256
    bout = vec_ref[4:5, :]

    def body(i, _):
        rows = pl.ds(pl.multiple_of(i * step, step), step)
        x1_ref[rows, :] = xp_ref[rows, :].astype(F32) + dot(o_ref[rows, :], wout_ref[...]) + bout
        return 0

    lax.fori_loop(0, xp_ref.shape[0] // step, body, 0)


def attn_kernel(
    tokens_ref, mask_ref, vec_ref, wqkv_ref, wout_ref,
    slot_ref, xp_ref, h1_ref, qkv_ref, o_ref, lse_ref, x1_ref,
):
    slot, _ = slots_of(mask_ref)
    slot_ref[...] = slot
    permute_rows(tokens_ref, slot, xp_ref)
    first_norm(xp_ref, vec_ref, h1_ref)
    project(h1_ref, vec_ref, wqkv_ref, qkv_ref)
    attend(qkv_ref, o_ref, lse_ref, lambda n: None)
    join(xp_ref, o_ref, wout_ref, vec_ref, x1_ref)


class Place:
    def __init__(self):
        self.me = me = lax.axis_index("fsdp")
        core = me % 2
        x = me // 2 % 2
        y = me // 4
        self.sib = me + 1 - 2 * core
        self.xn = me + 2 - 4 * x
        self.yn = me + 4 - 8 * y
        self.dg = me + 6 - 4 * x - 8 * y


def remote(src, dst, send, recv, to):
    return pltpu.make_async_remote_copy(
        src_ref=src, dst_ref=dst, send_sem=send, recv_sem=recv,
        device_id=to, device_id_type=pl.DeviceIdType.MESH,
    )


class Gather:
    def __init__(self, place, own, full, cut, send, recv, local):
        self.place = place
        rows = own.shape[0]
        at = lambda s, lo=0, hi=rows: full.at[pl.ds(pl.multiple_of(s * rows + lo, 16), hi - lo), :]
        me, sib, xn, yn, dg = place.me, place.sib, place.xn, place.yn, place.dg
        moves = [
            (own, at(me), sib), (own, at(me), xn), (own, at(me), yn),
            (at(xn), at(xn), sib), (at(yn), at(yn), sib),
            (at(xn, 0, cut), at(xn, 0, cut), yn), (at(yn, cut), at(yn, cut), xn),
            (at(dg, 0, cut), at(dg, 0, cut), sib), (at(dg, cut), at(dg, cut), sib),
        ]
        self.copies = [
            remote(src, dst, send.at[i], recv.at[i], {"fsdp": to}) for i, (src, dst, to) in enumerate(moves)
        ]
        self.local = pltpu.make_async_copy(own, at(me), local)

    def first(self):
        self.copies[1].start()
        self.copies[2].start()
        self.copies[0].start()
        self.local.start()

    def second(self):
        self.copies[1].wait_recv()
        self.copies[5].start()
        self.copies[3].start()
        self.copies[2].wait_recv()
        self.copies[6].start()
        self.copies[4].start()

    def third(self):
        self.copies[5].wait_recv()
        self.copies[7].start()
        self.copies[6].wait_recv()
        self.copies[8].start()

    def finish(self):
        for i in (0, 3, 4, 7, 8):
            self.copies[i].wait_recv()
        self.local.wait()
        for copy in self.copies:
            copy.wait_send()


def gather_attn_kernel(
    reps,
    tokens_ref, mask_ref, pack_ref, wqkv_in, wout_in, wup_in, wdn_in,
    slot_ref, xp_ref, h1_ref, qkv_ref, o_ref, lse_ref, x1_ref, vec_ref, bup_ref, over_ref,
    wqkv_ref, wout_ref, wup_ref, wdn_ref,
    packs, overs, send, recv, local, psend, precv, rsend, rrecv,
):
    width = tokens_ref.shape[1]
    share = wqkv_in.shape[0]
    place = Place()
    me = place.me
    rep = lax.axis_index("rep")
    shards = packs.shape[0]
    barrier = pltpu.get_barrier_semaphore()
    for d in range(1, shards):
        pl.semaphore_signal(
            barrier, inc=1, device_id={"fsdp": (me + d) % shards}, device_id_type=pl.DeviceIdType.MESH
        )
    for d in range(1, reps):
        pl.semaphore_signal(
            barrier, inc=1, device_id={"rep": (rep + d) % reps}, device_id_type=pl.DeviceIdType.MESH
        )
    slot, count = slots_of(mask_ref)
    slot_ref[...] = slot
    row = lax.broadcasted_iota(jnp.int32, (16, LANES), 0)
    over = jnp.where(count[:1] > FEW, 1.0, 0.0)
    packs[me] = jnp.where(row == 13, over, pack_ref[...].astype(F32)).astype(BF16)
    pl.semaphore_wait(barrier, shards + reps - 2)

    gathers = []
    for n, (own, full, cut) in enumerate(
        ((wqkv_in, wqkv_ref, 48), (wout_in, wout_ref, 32), (wup_in, wup_ref, 48), (wdn_in, wdn_ref, 320))
    ):
        gathers.append(Gather(place, own, full, cut, send.at[n], recv.at[n], local.at[n]))
    qkv, out, up, down = gathers
    vectors = []
    for d in range(1, shards):
        copy = remote(
            packs.at[me], packs.at[me], psend.at[d - 1], precv.at[d - 1], {"fsdp": (me + d) % shards}
        )
        copy.start()
        vectors.append(copy)
    qkv.first()
    permute_rows(tokens_ref, slot, xp_ref)
    for copy in vectors:
        copy.wait_recv()
    all_over = packs[0]
    for s in range(1, shards):
        all_over = jnp.maximum(all_over, packs[s])
    overs[rep] = all_over
    flags = []
    for d in range(1, reps):
        copy = remote(overs.at[rep], overs.at[rep], rsend.at[d - 1], rrecv.at[d - 1], {"rep": (rep + d) % reps})
        copy.start()
        flags.append(copy)
    qkv.second()
    out.first()
    up.first()
    vecs = jnp.zeros((16, width), F32)
    for s in range(shards):
        pack = packs[s]
        lane = lax.broadcasted_iota(jnp.int32, (LANES, width), 0)
        col = lax.broadcasted_iota(jnp.int32, (LANES, width), 1) - s * share
        spot = jnp.where((lane == col) & (lane < share), 1.0, 0.0).astype(BF16)
        vecs = vecs + dot(pack, spot)
        wide = pack.astype(F32)
        for r in range(width // LANES):
            bup_ref[0:1, s * width + r * LANES : s * width + (r + 1) * LANES] = wide[8 + r : 9 + r, :]
    vec_ref[...] = vecs[:8]
    first_norm(xp_ref, vec_ref, h1_ref)
    qkv.third()
    qkv.finish()
    project(h1_ref, vec_ref, wqkv_ref, qkv_ref)

    def beside(n):
        for at, step in (
            (0, out.second), (2, out.third), (4, up.second), (5, down.first), (9, up.third), (14, down.second),
            (18, down.third),
        ):
            pl.when(n == at)(step)

    attend(qkv_ref, o_ref, lse_ref, beside)
    out.finish()
    join(xp_ref, o_ref, wout_ref, vec_ref, x1_ref)
    for copy in flags:
        copy.wait()
    for copy in vectors:
        copy.wait_send()
    worst = overs[0]
    for z in range(1, reps):
        worst = jnp.maximum(worst, overs[z])
    over_ref[...] = worst[13:14, :].astype(F32)
    up.finish()
    down.finish()


def gather_attn(reps, shards, tokens, mask, pack, w_qkv, w_out, w_up, w_down):
    length, width = tokens.shape
    hidden = w_up.shape[1]
    sds = jax.ShapeDtypeStruct
    groups = width // LANES
    vmem = pl.BlockSpec(memory_space=pltpu.VMEM)
    hbm = pl.BlockSpec(memory_space=pl.ANY)
    dma = pltpu.SemaphoreType.DMA
    return pl.pallas_call(
        functools.partial(gather_attn_kernel, reps),
        in_specs=[vmem] * 3 + [hbm] * 4,
        out_specs=[vmem] * 12 + [hbm] * 2,
        out_shape=(
            sds((8, length), F32),
            sds((length, width), BF16),
            sds((length, width), BF16),
            sds((length, 3 * width), BF16),
            sds((length, width), BF16),
            sds((8 * groups, length), F32),
            sds((length, width), F32),
            sds((8, width), F32),
            sds((1, hidden), F32),
            sds((1, LANES), F32),
            sds((width, 3 * width), BF16),
            sds((width, width), BF16),
            sds((width, hidden), BF16),
            sds((hidden, width), BF16),
        ),
        scratch_shapes=[
            pltpu.VMEM((shards, 16, LANES), BF16),
            pltpu.VMEM((reps, 16, LANES), BF16),
            dma((4, 9)), dma((4, 9)), dma((4,)),
            dma((shards - 1,)), dma((shards - 1,)),
            dma((reps - 1,)), dma((reps - 1,)),
        ],
        compiler_params=pltpu.CompilerParams(
            vmem_limit_bytes=56 * MB, collective_id=0, has_side_effects=True
        ),
        name="gather_attn",
    )(tokens, mask, pack, w_qkv, w_out, w_up, w_down)


def attn_forward(tokens, mask, vecs, wqkv, wout):
    length, width = tokens.shape
    sds = jax.ShapeDtypeStruct
    groups = width // LANES
    return pl.pallas_call(
        attn_kernel,
        out_shape=(
            sds((8, length), F32),
            sds((length, width), BF16),
            sds((length, width), BF16),
            sds((length, 3 * width), BF16),
            sds((length, width), BF16),
            sds((8 * groups, length), F32),
            sds((length, width), F32),
        ),
        compiler_params=pltpu.CompilerParams(vmem_limit_bytes=56 * MB),
        name="attn_forward",
    )(tokens, mask, vecs, wqkv, wout)


def ffn_blocks(few, length):
    part = few if few <= 384 else 256
    blocks = [(start, part, True) for start in range(0, few, part)]
    start = few
    while start < length:
        size = min(320, length - start)
        blocks.append((start, size, False))
        start += size
    return blocks


def ffn_start(blocks, x1_ref, cot_ref, slot_ref, mask_ref, vec_ref, acc, h2, h2t, gy, gyt, dh2):
    gain = vec_ref[5:6, :]
    shift = vec_ref[6:7, :]
    bdown = vec_ref[7:8, :]
    for start, size, back in blocks:
        rows = slice(start, start + size)
        x1 = x1_ref[rows, :]
        xhat, _ = norm_stats(x1)
        hidden = (xhat * gain + shift).astype(BF16)
        h2[rows, :] = hidden
        acc[rows, :] = x1 + bdown
        if back:
            h2t[:, rows] = jnp.transpose(hidden)
            pick = one_hot_rows(slot_ref[0:1, :], float(start), size) * mask_ref[...]
            g = dot(pick.astype(BF16), cot_ref[...])
            gy[rows, :] = g.astype(BF16)
            gyt[:, rows] = jnp.transpose(g.astype(BF16))
            dh2[rows, :] = jnp.zeros_like(g)


def ffn_block(block, wup, wdn, bup, acc, h2, h2t, gy, gyt, dh2):
    start, size, back = block
    rows = slice(start, start + size)
    u = dot(h2[rows, :], wup) + bup
    cdf, e = cdf_parts(u)
    a = (u * cdf).astype(BF16)
    acc[rows, :] += dot(a, wdn)
    if not back:
        return None
    da = dot(gy[rows, :], wdn, NT)
    du = ((cdf + u * e * 0.3989422804014327) * da).astype(BF16)
    dh2[rows, :] += dot(du, wup, NT)
    return (
        dot(h2t[:, rows], du),
        dot(gyt[:, rows], a),
        jnp.sum(du.astype(F32), axis=0, keepdims=True),
    )


def ffn_end(blocks, x1_ref, slot_ref, vec_ref, wout_ref, o_ref, acc, gy, dh2, outp, res_ref, g1_ref, do_ref, small_ref):
    gain = vec_ref[5:6, :]
    ggain = gshift = gbdown = gbout = gout = None
    plus = lambda a, b: b if a is None else a + b
    for start, size, back in blocks:
        rows = slice(start, start + size)
        outp[rows, :] = acc[rows, :].astype(BF16)
        if back:
            xhat, rstd = norm_stats(x1_ref[rows, :])
            d = dh2[rows, :]
            g = gy[rows, :].astype(F32)
            g1 = g + norm_back(d, xhat, rstd, gain)
            g1_ref[rows, :] = g1
            g1b = g1.astype(BF16)
            do_ref[rows, :] = dot(g1b, wout_ref[...], NT).astype(BF16)
            gout = plus(gout, dot(jnp.transpose(o_ref[rows, :]), g1b))
            ggain = plus(ggain, jnp.sum(d * xhat, axis=0, keepdims=True))
            gshift = plus(gshift, jnp.sum(d, axis=0, keepdims=True))
            gbdown = plus(gbdown, jnp.sum(g, axis=0, keepdims=True))
            gbout = plus(gbout, jnp.sum(g1b.astype(F32), axis=0, keepdims=True))
    small_ref[8:9, :] = gbout
    small_ref[9:10, :] = ggain
    small_ref[10:11, :] = gshift
    small_ref[11:12, :] = gbdown
    small_ref[12:16, :] = jnp.zeros((4, outp.shape[1]), F32)
    unpermute(slot_ref[0:1, :], outp, res_ref)
    return gout


def ffn_kernel(
    few,
    x1_ref, cot_ref, slot_ref, mask_ref, vec_ref, bup_ref, wup_ref, wdn_ref, wout_ref, o_ref,
    res_ref, gup_ref, gdn_ref, g1_ref, do_ref, gout_ref, small_ref,
    acc, h2, h2t, gy, gyt, dh2, outp,
):
    j = pl.program_id(0)
    length, width = x1_ref.shape
    blocks = ffn_blocks(few, length)

    @pl.when(j == 0)
    def _():
        ffn_start(blocks, x1_ref, cot_ref, slot_ref, mask_ref, vec_ref, acc, h2, h2t, gy, gyt, dh2)

    total = None
    for block in blocks:
        part = ffn_block(block, wup_ref[...], wdn_ref[...], bup_ref[...], acc, h2, h2t, gy, gyt, dh2)
        if part is not None:
            total = part if total is None else [x + y for x, y in zip(total, part)]
    gup, gdn, gbup = total
    gup_ref[...] = gup.astype(BF16)
    for n in range(gdn_ref.shape[0]):
        cols = slice(n * width, (n + 1) * width)
        gdn_ref[n] = gdn[:, cols].astype(BF16)
        small_ref[pl.ds(j * gdn_ref.shape[0] + n, 1), :] = gbup[:, cols]

    @pl.when(j == pl.num_programs(0) - 1)
    def _():
        gout = ffn_end(
            blocks, x1_ref, slot_ref, vec_ref, wout_ref, o_ref, acc, gy, dh2, outp, res_ref, g1_ref, do_ref, small_ref
        )
        gout_ref[...] = gout.astype(BF16)


def feed_forward(few, x1, cot, slot, mask, vecs, bup, wup, wdn, wout, o):
    length, width = x1.shape
    hidden = wup.shape[1]
    fc = 2 * width
    sds = jax.ShapeDtypeStruct
    whole = lambda *shape: pl.BlockSpec(shape, lambda j: (0,) * len(shape))
    return pl.pallas_call(
        functools.partial(ffn_kernel, few),
        grid=(hidden // fc,),
        in_specs=[
            whole(length, width),
            whole(length, width),
            whole(8, length),
            whole(1, length),
            whole(8, width),
            pl.BlockSpec((1, fc), lambda j: (0, j)),
            pl.BlockSpec((width, fc), lambda j: (0, j)),
            pl.BlockSpec((fc, width), lambda j: (j, 0)),
            whole(width, width),
            whole(few, width),
        ],
        out_specs=[
            whole(length, width),
            pl.BlockSpec((width, fc), lambda j: (0, j)),
            pl.BlockSpec((2, width, width), lambda j: (j, 0, 0)),
            whole(few, width),
            whole(few, width),
            whole(width, width),
            whole(16, width),
        ],
        out_shape=(
            sds((length, width), BF16),
            sds((width, hidden), BF16),
            sds((hidden // width, width, width), BF16),
            sds((few, width), F32),
            sds((few, width), BF16),
            sds((width, width), BF16),
            sds((16, width), F32),
        ),
        scratch_shapes=[
            pltpu.VMEM((length, width), F32),
            pltpu.VMEM((length, width), BF16),
            pltpu.VMEM((width, few), BF16),
            pltpu.VMEM((few, width), BF16),
            pltpu.VMEM((width, few), BF16),
            pltpu.VMEM((few, width), F32),
            pltpu.VMEM((length, width), BF16),
        ],
        compiler_params=pltpu.CompilerParams(vmem_limit_bytes=56 * MB),
        name="feed_forward",
    )(x1, cot, slot, mask, vecs, bup, wup, wdn, wout, o)


class Heads:
    step = 256

    def __init__(self, few, q_ref, k_ref, v_ref, do_ref, o_ref, lse_ref, dqt, dkv):
        self.k_ref, self.v_ref, self.lse_ref, self.dqt, self.dkv = k_ref, v_ref, lse_ref, dqt, dkv
        q = q_ref[...]
        do = do_ref[...]
        lane = lax.broadcasted_iota(jnp.int32, (few, LANES), 1)
        head = lax.broadcasted_iota(jnp.int32, (8, LANES), 0)
        lane8 = lax.broadcasted_iota(jnp.int32, (8, LANES), 1)
        pick = jnp.where(lane8 // HEAD_DIM == head, 1.0, 0.0)
        self.delta = lax.dot_general(
            pick, do.astype(F32) * o_ref[...].astype(F32), NT,
            precision=lax.Precision.HIGHEST, preferred_element_type=F32,
        )
        dqt[...] = jnp.zeros_like(dqt)
        zero = jnp.zeros_like(q)
        self.qs = [jnp.where(lane // HEAD_DIM == h, q, zero) for h in range(GROUP)]
        self.dos = [jnp.where(lane // HEAD_DIM == h, do, zero) for h in range(GROUP)]

    def keys(self, i):
        step = self.step
        rows = pl.ds(pl.multiple_of(i * step, step), step)
        k = self.k_ref[rows, :]
        v = self.v_ref[rows, :]
        kt = jnp.transpose(k)
        dk = jnp.zeros((step, LANES), F32)
        dv = jnp.zeros((step, LANES), F32)
        for h in range(GROUP):
            s = dot(k, self.qs[h], NT)
            p = jnp.exp2(s * (SCALE * LOG2E) - self.lse_ref[h : h + 1, :])
            dp = dot(v, self.dos[h], NT)
            ds = (p * (dp - self.delta[h : h + 1, :])).astype(BF16)
            dv = dv + dot(p.astype(BF16), self.dos[h])
            dk = dk + dot(ds, self.qs[h])
            part = slice(h * HEAD_DIM, (h + 1) * HEAD_DIM)
            self.dqt[part, :] += dot(kt[part, :], ds)
        self.dkv[rows, :LANES] = (dk * SCALE).astype(BF16)
        self.dkv[rows, LANES:] = dv.astype(BF16)


def transpose_rows(src_ref, out_ref):
    step = 256
    for start in range(0, src_ref.shape[0], step):
        out_ref[:, start : start + step] = jnp.transpose(src_ref[start : start + step, :])


def group_weights(few, dqt, dkv, h1t, small_ref, cols):
    dq = (jnp.transpose(dqt[...]) * SCALE).astype(BF16)
    gq = dot(h1t[:, :few], dq).astype(BF16)
    gkv = dot(h1t[...], dkv[...]).astype(BF16)
    small_ref[2:3, cols] = jnp.sum(dq.astype(F32), axis=0, keepdims=True)
    small_ref[3:4, cols] = jnp.sum(dkv[:, LANES:].astype(F32), axis=0, keepdims=True)
    return dq, gq, gkv[:, :LANES], gkv[:, LANES:]


def group_inputs(few, dq, dkv, wq_ref, wk_ref, wv_ref, dh1):
    step = 256
    wkv = jnp.concatenate([wk_ref[...], wv_ref[...]], axis=1)
    for start in range(0, dh1.shape[0], step):
        rows = slice(start, start + step)
        dh1[rows, :] += dot(dkv[rows, :], wkv, NT)
    dh1[:few, :] += dot(dq, wq_ref[...], NT)


def back_finish(few, dh1_ref, xp_ref, vec_ref, g1_ref, small_ref, gtp):
    length, width = xp_ref.shape
    gain = vec_ref[0:1, :]
    step = 128
    ggain = gshift = jnp.zeros((1, width), F32)
    for start in range(0, length, step):
        rows = slice(start, start + step)
        xhat, rstd = norm_stats(xp_ref[rows, :].astype(F32))
        d = dh1_ref[rows, :]
        g = norm_back(d, xhat, rstd, gain)
        if start < few:
            g = g + g1_ref[rows, :]
        gtp[rows, :] = g.astype(BF16)
        ggain = ggain + jnp.sum(d * xhat, axis=0, keepdims=True)
        gshift = gshift + jnp.sum(d, axis=0, keepdims=True)
    small_ref[0:1, :] = ggain
    small_ref[1:2, :] = gshift


def back_kernel(
    few,
    q, k, v, do, o, lse, h1, xp, vec, wq, wk, wv, g1, slot,
    gtok, gq_ref, gk_ref, gv_ref, small,
    h1t, dh1, dqt, dkv, gtp,
):
    t = pl.program_id(0)
    cols = pl.ds(pl.multiple_of(t * LANES, LANES), LANES)

    @pl.when(t == 0)
    def _():
        transpose_rows(h1, h1t)
        dh1[...] = jnp.zeros_like(dh1)
        small[...] = jnp.zeros_like(small)

    heads = Heads(few, q, k, v, do, o, lse, dqt, dkv)

    def body(i, _):
        heads.keys(i)
        return 0

    lax.fori_loop(0, h1.shape[0] // heads.step, body, 0)
    dq, gq, gk, gv = group_weights(few, dqt, dkv, h1t, small, cols)
    gq_ref[...] = gq
    gk_ref[...] = gk
    gv_ref[...] = gv
    group_inputs(few, dq, dkv, wq, wk, wv, dh1)

    @pl.when(t == pl.num_programs(0) - 1)
    def _():
        back_finish(few, dh1, xp, vec, g1, small, gtp)
        unpermute(slot[0:1, :], gtp, gtok)


def back_specs(few, length, width):
    groups = width // LANES
    whole = lambda *shape: pl.BlockSpec(shape, lambda t: (0,) * len(shape))
    cols = lambda rows, first: pl.BlockSpec((rows, LANES), lambda t: (0, first + t))
    in_specs = [
        cols(few, 0),
        cols(length, groups),
        cols(length, 2 * groups),
        cols(few, 0),
        cols(few, 0),
        pl.BlockSpec((8, few), lambda t: (t, 0)),
        whole(length, width),
        whole(length, width),
        whole(8, width),
        cols(width, 0),
        cols(width, groups),
        cols(width, 2 * groups),
        whole(few, width),
        whole(8, length),
    ]
    scratch = [
        pltpu.VMEM((width, length), BF16),
        pltpu.VMEM((length, width), F32),
        pltpu.VMEM((LANES, few), F32),
        pltpu.VMEM((length, 2 * LANES), BF16),
        pltpu.VMEM((length, width), BF16),
    ]
    return whole, cols, in_specs, scratch


def attn_backward(few, qkv, do, o, lse, h1, xp, vecs, wqkv, g1, slot):
    length, width = h1.shape
    sds = jax.ShapeDtypeStruct
    whole, cols, in_specs, scratch = back_specs(few, length, width)
    return pl.pallas_call(
        functools.partial(back_kernel, few),
        grid=(width // LANES,),
        in_specs=in_specs,
        out_specs=[whole(length, width), cols(width, 0), cols(width, 0), cols(width, 0), whole(8, width)],
        out_shape=(
            sds((length, width), BF16),
            sds((width, width), BF16),
            sds((width, width), BF16),
            sds((width, width), BF16),
            sds((8, width), F32),
        ),
        scratch_shapes=scratch,
        compiler_params=pltpu.CompilerParams(vmem_limit_bytes=56 * MB),
        name="attn_backward",
    )(qkv, qkv, qkv, do, o, lse, h1, xp, vecs, wqkv, wqkv, wqkv, g1, slot)


class Reduce:
    def __init__(self, place, rep, reps, mine, other, acc, near, side, last, depth, fin, sems):
        send, recv, local = sems
        self.rep, self.reps = rep, reps
        self.acc, self.near, self.side, self.last, self.depth, self.fin = acc, near, side, last, depth, fin
        chip = place.me // 2
        cx, cy, cd = place.xn // 2, place.yn // 2, place.dg // 2
        self.chip, self.cx, self.cy = chip, cx, cy
        fsdp = lambda d: {"fsdp": d}
        low, high = slice(0, 2), slice(2, 4)
        n = iter(range(100))
        def copy(src, dst, to):
            i = next(n)
            return remote(src, dst, send.at[i], recv.at[i], to)
        self.a = [copy(other[q], near.at[:, q], fsdp(place.sib)) for q in range(4)]
        self.own = [pltpu.make_async_copy(mine[q], acc.at[:, q], local.at[q]) for q in range(4)]
        self.b = [
            copy(acc.at[cx, low], side.at[0], fsdp(place.xn)),
            copy(acc.at[cy, high], side.at[2], fsdp(place.yn)),
            copy(acc.at[cd, low], side.at[1], fsdp(place.xn)),
            copy(acc.at[cd, high], side.at[3], fsdp(place.yn)),
        ]
        self.c = [
            copy(acc.at[cy, low], last.at[0], fsdp(place.yn)),
            copy(acc.at[cx, high], last.at[1], fsdp(place.xn)),
        ]
        peers = [(rep + d) % reps for d in range(1, reps)]
        self.d = [copy(acc.at[chip, z], depth.at[i], {"rep": z}) for i, z in enumerate(peers)]
        self.e = [copy(fin.at[rep], fin.at[rep], {"rep": z}) for z in peers]

    COPIES = 16

    def start(self):
        for x in self.a + self.own:
            x.start()

    def near_sum(self):
        for q in range(4):
            self.own[q].wait()
            self.a[q].wait_recv()
            for c in range(4):
                self.acc[c, q] = (self.acc[c, q].astype(F32) + self.near[c, q].astype(F32)).astype(BF16)
        for x in self.b:
            x.start()

    def add(self, c, half, part):
        for q in range(2):
            self.acc[c, half + q] = (self.acc[c, half + q].astype(F32) + part[q].astype(F32)).astype(BF16)

    def side_sum(self):
        for x in self.b:
            x.wait()
        self.add(self.cy, 0, self.side.at[1])
        self.c[0].start()
        self.add(self.cx, 2, self.side.at[3])
        self.c[1].start()
        self.add(self.chip, 0, self.side.at[0])
        self.add(self.chip, 2, self.side.at[2])

    def last_sum(self):
        for x in self.c:
            x.wait()
        self.add(self.chip, 0, self.last.at[0])
        self.add(self.chip, 2, self.last.at[1])
        for x in self.d:
            x.start()

    def depth_sum(self):
        total = self.acc[self.chip, self.rep].astype(F32)
        for i in range(self.reps - 1):
            self.d[i].wait()
            total = total + self.depth[i].astype(F32)
        self.fin[self.rep] = total.astype(BF16)
        for x in self.e:
            x.start()

    def finish(self):
        for x in self.e:
            x.wait()
        for x in self.a:
            x.wait_send()


class Small:
    def __init__(self, me, shards, rep, reps, rows, beside, depth, out, sems):
        psend, precv, rsend, rrecv = sems
        self.me, self.rep, self.rows, self.near, self.depth, self.out = me, rep, rows, beside, depth, out
        self.first = [
            remote(beside.at[me], beside.at[me], psend.at[d - 1], precv.at[d - 1], {"fsdp": (me + d) % shards})
            for d in range(1, shards)
        ]
        self.second = [
            remote(depth.at[rep], depth.at[rep], rsend.at[d - 1], rrecv.at[d - 1], {"rep": (rep + d) % reps})
            for d in range(1, reps)
        ]

    def start(self):
        self.near[self.me] = self.rows[...]
        for x in self.first:
            x.start()

    def middle(self):
        for x in self.first:
            x.wait()
        total = self.near[0]
        for s in range(1, self.near.shape[0]):
            total = total + self.near[s]
        self.depth[self.rep] = total
        for x in self.second:
            x.start()

    def finish(self):
        for x in self.second:
            x.wait()
        total = self.depth[0]
        for z in range(1, self.depth.shape[0]):
            total = total + self.depth[z]
        self.out[...] = total


def reduce_back_kernel(
    few, shards, reps,
    q, k, v, do, o, lse, h1, xp, vec, wq, wk, wv, g1, slot, early_ref, gout_ref, gup_ref, gdn_ref,
    gtok, gup_out, gdn_out, gqkv_out, gout_out, early_out, late_out,
    h1t, dh1, dqt, dkv, gtp, late, gqkv, fin, acc, near, side, last, depth, send, recv, local,
    enear, edepth, lnear, ldepth, es1, er1, es2, er2, ls1, lr1, ls2, lr2,
):
    t = pl.program_id(0)
    cols = pl.ds(pl.multiple_of(t * LANES, LANES), LANES)
    share = h1.shape[1] // shards
    width = h1.shape[1]
    place = Place()
    rep = lax.axis_index("rep")
    core = place.me % 2

    def quarter(n, side):
        u = n // 4
        if u < 2:
            return gup_ref.at[:, side, :, n * width : (n + 1) * width]
        if u < 4:
            return gdn_ref.at[:, side, (n - 8) * share : (n - 7) * share, :]
        return gout_ref.at[:, side] if n == 16 else gqkv.at[n - 17, :, side]

    units = []
    for u in range(5):
        sems = (send.at[u], recv.at[u], local.at[u])
        units.append(
            Reduce(
                place, rep, reps,
                [quarter(4 * u + n, core) for n in range(4)],
                [quarter(4 * u + n, 1 - core) for n in range(4)],
                acc.at[u], near.at[u], side.at[u], last.at[u], depth.at[u], fin.at[u], sems,
            )
        )
    early = Small(place.me, shards, rep, reps, early_ref, enear, edepth, early_out, (es1, er1, es2, er2))
    later = Small(place.me, shards, rep, reps, late, lnear, ldepth, late_out, (ls1, lr1, ls2, lr2))

    @pl.when(t == 0)
    def _():
        barrier = pltpu.get_barrier_semaphore()
        for d in range(1, shards):
            pl.semaphore_signal(
                barrier, inc=1, device_id={"fsdp": (place.me + d) % shards},
                device_id_type=pl.DeviceIdType.MESH,
            )
        for d in range(1, reps):
            pl.semaphore_signal(
                barrier, inc=1, device_id={"rep": (rep + d) % reps}, device_id_type=pl.DeviceIdType.MESH
            )
        pl.semaphore_wait(barrier, shards + reps - 2)
        for u in range(4):
            units[u].start()
        early.start()
        transpose_rows(h1, h1t)
        dh1[...] = jnp.zeros_like(dh1)
        late[...] = jnp.zeros_like(late)

    heads = Heads(few, q, k, v, do, o, lse, dqt, dkv)
    blocks = h1.shape[0] // heads.step

    plan = [
        (1, units[0].near_sum), (2, units[1].near_sum), (3, units[2].near_sum), (4, units[3].near_sum),
        (5, early.middle), (6, units[0].side_sum), (9, units[1].side_sum), (10, units[0].last_sum),
        (11, early.finish), (13, units[2].side_sum), (14, units[1].last_sum), (15, units[0].depth_sum),
        (17, units[3].side_sum), (18, units[2].last_sum), (19, units[1].depth_sum),
    ]

    def body(i, _):
        for at, step in plan:
            pl.when(t * blocks + i == at)(step)
        heads.keys(i)
        return 0

    lax.fori_loop(0, blocks, body, 0)
    dq, gq, gk, gv = group_weights(few, dqt, dkv, h1t, late, cols)
    chips = shards // 2
    for n, g in enumerate((gq, gk, gv)):
        gqkv[n, :, :, :, cols] = g.reshape(chips, 2, share, LANES)
    final = t == pl.num_programs(0) - 1
    pl.when(final)(units[4].start)
    group_inputs(few, dq, dkv, wq, wk, wv, dh1)

    @pl.when(final)
    def _():
        units[4].near_sum()
        units[3].last_sum()
        units[2].depth_sum()
        back_finish(few, dh1, xp, vec, g1, late, gtp)
        later.start()
        units[4].side_sum()
        units[3].depth_sum()
        units[4].last_sum()
        later.middle()
        unpermute(slot[0:1, :], gtp, gtok)
        units[4].depth_sum()
        for n in range(16):
            if n % 4 == 0:
                units[n // 4].finish()
            part = fin[n // 4, n % 4].astype(F32)
            if n < 8:
                gup_out[:, n * width : (n + 1) * width] = part
            else:
                gdn_out[:, (n - 8) * share : (n - 7) * share] = jnp.transpose(part)
        later.finish()
        units[4].finish()
        gout_out[...] = fin[4, 0].astype(F32)
        for n in range(3):
            gqkv_out[:, n * width : (n + 1) * width] = fin[4, 1 + n].astype(F32)


def reduce_backward(few, shards, reps, ident, qkv, do, o, lse, h1, xp, vecs, wqkv, g1, slot, early, gout, gup, gdn):
    length, width = h1.shape
    share = width // shards
    chips = shards // 2
    sds = jax.ShapeDtypeStruct
    whole, cols, in_specs, scratch = back_specs(few, length, width)
    hbm = pl.BlockSpec(memory_space=pl.ANY)
    dma = pltpu.SemaphoreType.DMA
    block = (share, width)
    copies = Reduce.COPIES
    hidden = gup.shape[1]
    return pl.pallas_call(
        functools.partial(reduce_back_kernel, few, shards, reps),
        grid=(width // LANES,),
        in_specs=in_specs + [whole(16, width), hbm, hbm, hbm],
        out_specs=[
            whole(length, width), whole(share, hidden), whole(width, width), whole(share, 3 * width),
            whole(share, width), whole(16, width), whole(8, width),
        ],
        out_shape=(
            sds((length, width), BF16),
            sds((share, hidden), F32),
            sds((width, width), F32),
            sds((share, 3 * width), F32),
            sds((share, width), F32),
            sds((16, width), F32),
            sds((8, width), F32),
        ),
        scratch_shapes=scratch
        + [
            pltpu.VMEM((8, width), F32),
            pltpu.VMEM((3, chips, 2) + block, BF16),
            pltpu.VMEM((5, 4) + block, BF16),
            pltpu.VMEM((5, chips, 4) + block, BF16),
            pltpu.VMEM((5, chips, 4) + block, BF16),
            pltpu.VMEM((5, 4, 2) + block, BF16),
            pltpu.VMEM((5, 2, 2) + block, BF16),
            pltpu.VMEM((5, reps - 1) + block, BF16),
            dma((5, copies)), dma((5, copies)), dma((5, 4)),
            pltpu.VMEM((shards, 16, width), F32),
            pltpu.VMEM((reps, 16, width), F32),
            pltpu.VMEM((shards, 8, width), F32),
            pltpu.VMEM((reps, 8, width), F32),
            dma((shards - 1,)), dma((shards - 1,)), dma((reps - 1,)), dma((reps - 1,)),
            dma((shards - 1,)), dma((shards - 1,)), dma((reps - 1,)), dma((reps - 1,)),
        ],
        compiler_params=pltpu.CompilerParams(
            vmem_limit_bytes=60 * MB, collective_id=ident, has_side_effects=True
        ),
        name="reduce_backward",
    )(
        qkv, qkv, qkv, do, o, lse, h1, xp, vecs, wqkv, wqkv, wqkv, g1, slot, early,
        gout.reshape(chips, 2, share, width),
        gup.reshape(chips, 2, share, hidden),
        gdn.reshape(chips, 2, width, width),
    )


class Unit:
    COPIES = 13

    def __init__(self, place, rep, reps, other, acc, near, side, last, depth, fin, send, recv):
        self.rep, self.reps = rep, reps
        self.acc, self.near, self.side, self.last, self.depth, self.fin = acc, near, side, last, depth, fin
        chip = place.me // 2
        cx, cy, cd = place.xn // 2, place.yn // 2, place.dg // 2
        self.chip, self.cx, self.cy = chip, cx, cy
        self.rows = rows = acc.shape[1]
        half, self.quarter = rows // 2, rows // 4
        low, high = pl.ds(0, half), pl.ds(half, half)
        self.low, self.high = low, high
        fsdp = lambda d: {"fsdp": d}

        def copy(i, src, dst, to):
            return remote(src, dst, send.at[i], recv.at[i], to)

        if other is not None:
            self.a = copy(0, other, near, fsdp(place.sib))
        if side is not None:
            self.b = [
                copy(1, acc.at[cd, low], side.at[1], fsdp(place.xn)),
                copy(2, acc.at[cd, high], side.at[3], fsdp(place.yn)),
                copy(3, acc.at[cx, low], side.at[0], fsdp(place.xn)),
                copy(4, acc.at[cy, high], side.at[2], fsdp(place.yn)),
            ]
            self.c = [
                copy(5, acc.at[cy, low], last.at[0], fsdp(place.yn)),
                copy(6, acc.at[cx, high], last.at[1], fsdp(place.xn)),
            ]
        if depth is not None:
            peers = [(rep + d) % reps for d in range(1, reps)]
            own = acc.at[chip] if other is not None or side is not None else acc.at[0]
            self.own = own
            self.d = [copy(7 + i, own.at[self.part(z)], depth.at[i], {"rep": z}) for i, z in enumerate(peers)]
            self.e = [
                copy(10 + i, fin.at[self.part(rep)], fin.at[self.part(rep)], {"rep": z})
                for i, z in enumerate(peers)
            ]

    def part(self, z):
        return pl.ds(pl.multiple_of(z * self.quarter, 16), self.quarter)

    def near_start(self):
        self.a.start()

    def near_add(self):
        self.a.wait_recv()
        for c in range(self.acc.shape[0]):
            self.acc[c] = self.acc[c] + self.near[c]

    def side_start(self):
        for x in self.b:
            x.start()

    def near_sum(self):
        self.near_add()
        self.side_start()

    def add(self, c, half, ref):
        self.acc[c, half, :] = self.acc[c, half, :] + ref[...]

    def side_sum(self):
        self.b[0].wait()
        self.add(self.cy, self.low, self.side.at[1])
        self.c[0].start()
        self.b[1].wait()
        self.add(self.cx, self.high, self.side.at[3])
        self.c[1].start()
        self.b[2].wait()
        self.add(self.chip, self.low, self.side.at[0])
        self.b[3].wait()
        self.add(self.chip, self.high, self.side.at[2])

    def last_add(self):
        for x in self.c:
            x.wait()
        self.add(self.chip, self.low, self.last.at[0])
        self.add(self.chip, self.high, self.last.at[1])

    def depth_start(self):
        for x in self.d:
            x.start()

    def last_sum(self):
        self.last_add()
        self.depth_start()

    def depth_sum(self):
        mine = self.part(self.rep)
        total = self.own[mine, :].astype(F32)
        for i in range(self.reps - 1):
            self.d[i].wait()
            total = total + self.depth[i].astype(F32)
        self.fin[mine, :] = total.astype(BF16)
        for x in self.e:
            x.start()

    def finish(self):
        for x in self.e:
            x.wait()


def greet(me, shards, rep, reps):
    barrier = pltpu.get_barrier_semaphore()
    mesh = pl.DeviceIdType.MESH
    for d in range(1, shards):
        pl.semaphore_signal(barrier, inc=1, device_id={"fsdp": (me + d) % shards}, device_id_type=mesh)
    for d in range(1, reps):
        pl.semaphore_signal(barrier, inc=1, device_id={"rep": (rep + d) % reps}, device_id_type=mesh)
    pl.semaphore_wait(barrier, shards + reps - 2)


CHUNKS = 5


def ffn_reduce_kernel(
    few, shards, reps,
    x1_ref, cot_ref, slot_ref, mask_ref, vec_ref, wout_ref, o_ref, *refs,
):
    bups, wups, wdns = refs[:shards], refs[shards : 2 * shards], refs[2 * shards : 3 * shards]
    (
        res_ref, g1_ref, do_ref, gout_ref, small_ref, fin_ref, own_ref, plane_ref,
        acc, h2, h2t, gy, gyt, dh2, outp, g, near, side, last, depth, fin, send, recv,
    ) = refs[3 * shards :]
    j = pl.program_id(0)
    length, width = x1_ref.shape
    share = width // shards
    blocks = ffn_blocks(few, length)
    place = Place()
    rep = lax.axis_index("rep")
    core = place.me % 2
    units = []
    for u in range(CHUNKS):
        z = u < 2
        xy = u < 4
        units.append(
            Unit(
                place, rep, reps, g.at[u, 1 - core], g.at[u, core], near.at[u],
                side.at[u] if xy else None, last.at[u] if xy else None,
                depth.at[u] if z else None, fin.at[u] if z else None, send.at[u], recv.at[u],
            )
        )

    def at(step, *acts):
        @pl.when(j == step)
        def _():
            for act in acts:
                act()

    @pl.when(j == 0)
    def _():
        greet(place.me, shards, rep, reps)
        ffn_start(blocks, x1_ref, cot_ref, slot_ref, mask_ref, vec_ref, acc, h2, h2t, gy, gyt, dh2)

    at(2, units[0].last_sum)
    at(3, units[1].last_sum, units[0].depth_sum)
    at(4, units[2].last_add, units[1].depth_sum)
    wup = jnp.concatenate([w[...] for w in wups], axis=1)
    wdn = jnp.concatenate([w[...] for w in wdns], axis=0)
    bup = jnp.concatenate([b[...] for b in bups], axis=1)
    cols = pl.ds(pl.multiple_of(j * LANES, LANES), LANES)
    for n, block in enumerate(blocks):
        part = ffn_block(block, wup, wdn, bup, acc, h2, h2t, gy, gyt, dh2)
        if n == 0:
            gup, gdn, gbup = part
            for s in range(shards):
                mine = slice(s * share, (s + 1) * share)
                lanes = slice(s * LANES, (s + 1) * LANES)
                for b in range(shards):
                    g[j, s % 2, s // 2, b * share : (b + 1) * share, :] = gup[
                        mine, b * LANES : (b + 1) * LANES
                    ].astype(BF16)
                g[j, s % 2, s // 2, width:, :] = gdn[:, lanes].astype(BF16)
                small_ref[s : s + 1, cols] = gbup[:, lanes]
            for u in range(CHUNKS):
                at(u, units[u].near_start)
        if n == 1:
            for u in range(4):
                at(u + 1, units[u].side_sum)
        if n == 2:
            for u in range(4):
                at(u, units[u].near_sum)

    @pl.when(j == CHUNKS - 1)
    def _():
        gout = ffn_end(
            blocks, x1_ref, slot_ref, vec_ref, wout_ref, o_ref, acc, gy, dh2, outp, res_ref, g1_ref, do_ref, small_ref
        )
        for s in range(shards):
            for b in range(CHUNKS):
                gout_ref[s % 2, s // 2, b * share : (b + 1) * share, :] = gout[
                    s * share : (s + 1) * share, b * LANES : (b + 1) * LANES
                ].astype(BF16)
            spare = gout_ref.shape[2] - CHUNKS * share
            gout_ref[s % 2, s // 2, CHUNKS * share :, :] = jnp.zeros((spare, LANES), BF16)
        units[4].near_add()
        plane_ref[...] = g[4, core]
        units[3].last_add()
        for n, u in enumerate((2, 3)):
            own_ref[n] = g[u, core, units[u].chip]
        for u in range(2):
            units[u].finish()
            fin_ref[u] = fin[u]
        for u in range(CHUNKS):
            units[u].a.wait_send()


def ffn_reduce(few, shards, reps, x1, cot, slot, mask, vecs, bup, wup, wdn, wout, o):
    length, width = x1.shape
    share = width // shards
    chips = shards // 2
    rows = 2 * width
    spare = 448
    sds = jax.ShapeDtypeStruct
    whole = lambda *shape: pl.BlockSpec(shape, lambda j: (0,) * len(shape))
    pick = lambda s, shape, across: pl.BlockSpec(
        shape, lambda j: (0, s * CHUNKS + j) if across else (s * CHUNKS + j, 0)
    )
    dma = pltpu.SemaphoreType.DMA
    return pl.pallas_call(
        functools.partial(ffn_reduce_kernel, few, shards, reps),
        grid=(CHUNKS,),
        in_specs=[
            whole(length, width), whole(length, width), whole(8, length), whole(1, length), whole(8, width),
            whole(width, width), whole(few, width),
        ]
        + [pick(s, (1, LANES), True) for s in range(shards)]
        + [pick(s, (width, LANES), True) for s in range(shards)]
        + [pick(s, (LANES, width), False) for s in range(shards)],
        out_specs=[
            whole(length, width), whole(few, width), whole(few, width), whole(2, chips, spare, LANES),
            whole(16, width), whole(2, rows, LANES), whole(2, rows, LANES), whole(chips, rows, LANES),
        ],
        out_shape=(
            sds((length, width), BF16),
            sds((few, width), F32),
            sds((few, width), BF16),
            sds((2, chips, spare, LANES), BF16),
            sds((16, width), F32),
            sds((2, rows, LANES), BF16),
            sds((2, rows, LANES), BF16),
            sds((chips, rows, LANES), BF16),
        ),
        scratch_shapes=[
            pltpu.VMEM((length, width), F32),
            pltpu.VMEM((length, width), BF16),
            pltpu.VMEM((width, few), BF16),
            pltpu.VMEM((few, width), BF16),
            pltpu.VMEM((width, few), BF16),
            pltpu.VMEM((few, width), F32),
            pltpu.VMEM((length, width), BF16),
            pltpu.VMEM((CHUNKS, 2, chips, rows, LANES), BF16),
            pltpu.VMEM((CHUNKS, chips, rows, LANES), BF16),
            pltpu.VMEM((4, 4, rows // 2, LANES), BF16),
            pltpu.VMEM((4, 2, rows // 2, LANES), BF16),
            pltpu.VMEM((2, reps - 1, rows // 4, LANES), BF16),
            pltpu.VMEM((2, rows, LANES), BF16),
            dma((CHUNKS, Unit.COPIES)), dma((CHUNKS, Unit.COPIES)),
        ],
        compiler_params=pltpu.CompilerParams(
            vmem_limit_bytes=60 * MB, collective_id=3, has_side_effects=True
        ),
        name="ffn_reduce",
    )(x1, cot, slot, mask, vecs, wout, o, *[bup] * shards, *[wup] * shards, *[wdn] * shards)


GROUP_ROWS = 256


def back_reduce_kernel(
    few, shards, reps,
    q, k, v, do, o, lse, h1, xp, vec, wq, wk, wv, g1, slot, early_ref, done_ref, own_in, plane_in, gout_in,
    gtok, gup_out, gdn_out, gqkv_out, gout_out, early_out, late_out,
    h1t, dh1, dqt, dkv, gtp, late,
    own, plane, fside, flast, fdepth, ffin,
    onear, oacc, oside, olast, odepth, ofin,
    gg, gnear, gside, glast, gdepth, gfin,
    send, recv, local,
    enear, edepth, lnear, ldepth, es1, er1, es2, er2, ls1, lr1, ls2, lr2,
):
    t = pl.program_id(0)
    groups = pl.num_programs(0)
    length, width = h1.shape
    share = width // shards
    chips = shards // 2
    cols = pl.ds(pl.multiple_of(t * LANES, LANES), LANES)
    place = Place()
    rep = lax.axis_index("rep")
    core = place.me % 2
    sems = lambda n: (send.at[n], recv.at[n])
    make = functools.partial(Unit, place, rep, reps)
    u2 = make(None, own.at[pl.ds(0, 1)], None, None, None, fdepth.at[0], ffin.at[0], *sems(0))
    u3 = make(None, own.at[pl.ds(1, 1)], None, None, None, fdepth.at[1], ffin.at[1], *sems(1))
    u4 = make(None, plane, None, fside, flast, fdepth.at[2], ffin.at[2], *sems(2))
    uo = make(gout_in.at[1 - core], oacc, onear, oside, olast, odepth, ofin, *sems(3))
    parts = []
    for n in range(5):
        parts.append(
            make(
                gg.at[n, 1 - core], gg.at[n, core], gnear.at[n], gside.at[n], glast.at[n], gdepth.at[n],
                gfin.at[n], *sems(4 + n)
            )
        )
    loads = [
        pltpu.make_async_copy(own_in, own, local.at[0]),
        pltpu.make_async_copy(plane_in, plane, local.at[1]),
        pltpu.make_async_copy(gout_in.at[core], oacc, local.at[2]),
    ]
    early = Small(place.me, shards, rep, reps, early_ref, enear, edepth, early_out, (es1, er1, es2, er2))
    later = Small(place.me, shards, rep, reps, late, lnear, ldepth, late_out, (ls1, lr1, ls2, lr2))

    @pl.when(t == 0)
    def _():
        for x in loads:
            x.start()
        transpose_rows(h1, h1t)
        dh1[...] = jnp.zeros_like(dh1)
        late[...] = jnp.zeros_like(late)
        greet(place.me, shards, rep, reps)
        loads[0].wait()
        u2.depth_start()
        loads[1].wait()
        u4.side_start()
        uo.near_start()
        loads[2].wait()
        early.start()

    heads = Heads(few, q, k, v, do, o, lse, dqt, dkv)
    blocks = length // heads.step

    plan = [
        (1, uo.near_sum), (2, early.middle), (4, u2.depth_sum), (4, u3.depth_start), (4, u4.side_sum),
        (6, early.finish), (6, uo.side_sum), (7, u4.last_sum), (8, u3.depth_sum), (9, uo.last_sum),
        (12, u4.depth_sum), (13, uo.depth_sum),
    ]
    for n in range(4):
        first = 4 * (n + 1)
        plan += [(first + 1, parts[n].near_sum), (first + 3, parts[n].side_sum)]
        if n < 3:
            plan += [(first + 5, parts[n].last_sum)]
        if n < 2:
            plan += [(first + 7, parts[n].depth_sum)]

    def body(i, _):
        for at, step in plan:
            pl.when(t * blocks + i == at)(step)
        heads.keys(i)
        return 0

    lax.fori_loop(0, blocks, body, 0)
    dq, gq, gk, gv = group_weights(few, dqt, dkv, h1t, late, cols)
    for n, part in enumerate((gq, gk, gv)):
        for s in range(shards):
            gg[t, s % 2, s // 2, n * share : (n + 1) * share, :] = part[s * share : (s + 1) * share, :]
    for s in range(shards):
        gg[t, s % 2, s // 2, 3 * share :, :] = jnp.zeros((GROUP_ROWS - 3 * share, LANES), BF16)
    for n in range(5):
        pl.when(t == n)(parts[n].near_start)
    group_inputs(few, dq, dkv, wq, wk, wv, dh1)

    @pl.when(t == groups - 1)
    def _():
        parts[4].near_sum()
        parts[3].last_sum()
        parts[2].depth_sum()
        back_finish(few, dh1, xp, vec, g1, late, gtp)
        later.start()
        parts[4].side_sum()
        parts[3].depth_sum()
        unpermute(slot[0:1, :], gtp, gtok)
        parts[4].last_sum()
        later.middle()
        for n in range(CHUNKS):
            if n >= 2:
                (u2, u3, u4)[n - 2].finish()
            src = done_ref.at[n] if n < 2 else ffin.at[n - 2]
            for b in range(shards):
                gup_out[:, b * width + n * LANES : b * width + (n + 1) * LANES] = src[
                    b * share : (b + 1) * share, :
                ].astype(F32)
            gdn_out[n * LANES : (n + 1) * LANES, :] = jnp.transpose(src[width:, :].astype(F32))
        uo.finish()
        for b in range(CHUNKS):
            gout_out[:, b * LANES : (b + 1) * LANES] = ofin[b * share : (b + 1) * share, :].astype(F32)
        parts[4].depth_sum()
        later.finish()
        for n in range(5):
            parts[n].finish()
            for m in range(3):
                gqkv_out[:, m * width + n * LANES : m * width + (n + 1) * LANES] = gfin[
                    n, m * share : (m + 1) * share, :
                ].astype(F32)
            parts[n].a.wait_send()
        uo.a.wait_send()


def back_reduce(few, shards, reps, qkv, do, o, lse, h1, xp, vecs, wqkv, g1, slot, early, done, own, plane, gout):
    length, width = h1.shape
    share = width // shards
    chips = shards // 2
    rows = 2 * width
    groups = width // LANES
    hidden = shards * width
    sds = jax.ShapeDtypeStruct
    whole, cols, in_specs, scratch = back_specs(few, length, width)
    hbm = pl.BlockSpec(memory_space=pl.ANY)
    dma = pltpu.SemaphoreType.DMA
    vm = lambda *shape: pltpu.VMEM(shape + (LANES,), BF16)
    spare = gout.shape[2]

    def buffers(rows):
        return [vm(4, rows // 2), vm(2, rows // 2), vm(reps - 1, rows // 4), vm(rows)]

    many = lambda n, refs: [pltpu.VMEM((n,) + r.shape, BF16) for r in refs]
    fside, flast, fdepth, ffin = buffers(rows)
    return pl.pallas_call(
        functools.partial(back_reduce_kernel, few, shards, reps),
        grid=(groups,),
        in_specs=in_specs + [whole(16, width), whole(2, rows, LANES), hbm, hbm, hbm],
        out_specs=[
            whole(length, width), whole(share, hidden), whole(width, width), whole(share, 3 * width),
            whole(share, width), whole(16, width), whole(8, width),
        ],
        out_shape=(
            sds((length, width), BF16),
            sds((share, hidden), F32),
            sds((width, width), F32),
            sds((share, 3 * width), F32),
            sds((share, width), F32),
            sds((16, width), F32),
            sds((8, width), F32),
        ),
        scratch_shapes=scratch
        + [
            pltpu.VMEM((8, width), F32),
            vm(2, rows), vm(chips, rows), fside, flast,
        ]
        + many(3, [fdepth, ffin])
        + [vm(chips, spare), vm(chips, spare)] + buffers(spare)
        + [vm(5, 2, chips, GROUP_ROWS), vm(5, chips, GROUP_ROWS)] + many(5, buffers(GROUP_ROWS))
        + [
            dma((9, Unit.COPIES)), dma((9, Unit.COPIES)), dma((3,)),
            pltpu.VMEM((shards, 16, width), F32),
            pltpu.VMEM((reps, 16, width), F32),
            pltpu.VMEM((shards, 8, width), F32),
            pltpu.VMEM((reps, 8, width), F32),
            dma((shards - 1,)), dma((shards - 1,)), dma((reps - 1,)), dma((reps - 1,)),
            dma((shards - 1,)), dma((shards - 1,)), dma((reps - 1,)), dma((reps - 1,)),
        ],
        compiler_params=pltpu.CompilerParams(
            vmem_limit_bytes=60 * MB, collective_id=4, has_side_effects=True
        ),
        name="back_reduce",
    )(qkv, qkv, qkv, do, o, lse, h1, xp, vecs, wqkv, wqkv, wqkv, g1, slot, early, done, own, plane, gout)


def local(
    reps, shards,
    tokens, masked, cotangent, norm1_gain, norm1_shift, w_qkv, bias_query, bias_value, w_out,
    bias_out, norm2_gain, norm2_shift, w_up, bias_up, w_down, bias_down,
):
    seqs, length, width = tokens.shape
    hidden = w_up.shape[1]
    share = w_qkv.shape[0]
    close = shards == 8 and share % 16 == 0 and share <= LANES and w_down.shape[0] == width
    x = tokens.reshape(seqs * length, width)
    cot = cotangent.reshape(seqs * length, width)
    mask = masked.astype(F32)
    if close:
        pack = jnp.concatenate(
            [
                jnp.pad(
                    jnp.stack(
                        [norm1_gain, norm1_shift, bias_query, bias_value, bias_out, norm2_gain, norm2_shift, bias_down]
                    ),
                    ((0, 0), (0, LANES - share)),
                ),
                jnp.pad(bias_up.reshape(-1, LANES), ((0, 3), (0, 0))),
            ]
        )
        slot, xp, h1, qkv, o, lse, x1, vecs, bup, over, wqkv, wout, wup, wdn = gather_attn(
            reps, shards, x, mask, pack, w_qkv, w_out, w_up, w_down
        )
        small_enough = over[0, 0] < 0.5
    else:
        small_enough = lax.pmax(jnp.sum(masked), ("rep", "fsdp")) <= FEW
        packed = jnp.stack(
            [norm1_gain, norm1_shift, bias_query, bias_value, bias_out, norm2_gain, norm2_shift, bias_down]
        )
        vecs = lax.all_gather(packed, "fsdp", axis=1, tiled=True).astype(F32)
        bup = lax.all_gather(bias_up, "fsdp", axis=0, tiled=True).astype(F32).reshape(1, hidden)
        gather = lambda w: lax.all_gather(w, "fsdp", axis=0, tiled=True)
        wqkv, wout, wup, wdn = gather(w_qkv), gather(w_out), gather(w_up), gather(w_down)
        slot, xp, h1, qkv, o, lse, x1 = attn_forward(x, mask, vecs, wqkv, wout)

    def backward(few):
        def run():
            res, gup, gdn, g1, do, gout, early = feed_forward(
                few, x1, cot, slot, mask, vecs, bup, wup, wdn, wout, o
            )
            if close:
                gtok, gup, gdn, gqkv, gout, early, late = reduce_backward(
                    few, shards, reps, 1,
                    qkv, do, o, lse, h1, xp, vecs, wqkv, g1, slot, early, gout, gup, gdn,
                )
                return res, gtok, gup, gdn, gqkv, gout, early, late
            gtok, gq, gk, gv, late = attn_backward(
                few, qkv, do, o, lse, h1, xp, vecs, wqkv, g1, slot
            )
            return res, gtok, gup, gdn, jnp.concatenate([gout, gq, gk, gv], axis=1), early, late

        return run

    if close:
        res, g1, do, part, early, done, own, plane = ffn_reduce(
            FEW, shards, reps, x1, cot, slot, mask, vecs, bup, wup, wdn, wout, o
        )
        short = (res,) + tuple(
            back_reduce(
                FEW, shards, reps, qkv, do, o, lse, h1, xp, vecs, wqkv, g1, slot, early, done, own, plane, part
            )
        )
    res, gtok, *grads, early, late = lax.cond(
        small_enough, (lambda: short) if close else backward(FEW), backward(length)
    )

    if close:
        gup, gdn, gqkv, gout = grads
    else:
        def scatter(g, dim):
            part = lax.psum_scatter(g, "fsdp", scatter_dimension=dim, tiled=True)
            return lax.psum(part, "rep").astype(F32)

        gup, gdn, gattn = grads
        gup = scatter(gup, 0)
        gdn = scatter(gdn.transpose(0, 2, 1).reshape(hidden, width), 0)
        gattn = scatter(gattn, 0)
        gout, gqkv = gattn[:, :width], gattn[:, width:]
        early = lax.psum(early, ("rep", "fsdp"))
        late = lax.psum(late, ("rep", "fsdp"))
    me = lax.axis_index("fsdp")
    own = bias_up.shape[0]
    gbup = lax.dynamic_slice_in_dim(early[:8].reshape(hidden), me * own, own)
    mine = lax.dynamic_slice_in_dim(jnp.concatenate([late[:4], early[8:12]]), me * share, share, axis=1)
    return (
        res.reshape(seqs, length, width),
        gtok.reshape(seqs, length, width),
        mine[0], mine[1], gqkv, mine[2], mine[3], gout, mine[4], mine[5], mine[6],
        gup, gbup, gdn, mine[7],
    )


def solution(mesh):
    rows3 = P(("rep", "fsdp"), None, None)
    vec = P("fsdp")
    mat = P("fsdp", None)
    in_specs = (
        rows3, P(("rep", "fsdp"), None), rows3,
        vec, vec, mat, vec, vec, mat, vec, vec, vec, mat, vec, mat, vec,
    )
    out_specs = (rows3, rows3, vec, vec, mat, vec, vec, mat, vec, vec, vec, mat, vec, mat, vec)
    body = functools.partial(local, mesh.shape["rep"], mesh.shape["fsdp"])
    return jax.shard_map(body, mesh=mesh, in_specs=in_specs, out_specs=out_specs, check_vma=False)
```

```python
import functools

import jax
import jax.numpy as jnp
from jax import lax
from jax.experimental import pallas as pl
from jax.experimental.pallas import tpu as pltpu
from jax.sharding import PartitionSpec as P

HEADS = 20
HEAD_DIM = 32
GROUP = 4
LANES = 128
SCALE = HEAD_DIM ** (-0.5)
LOG2E = 1.4426950408889634
FEW = 384
F32 = jnp.float32
BF16 = jnp.bfloat16
MB = 1024 * 1024

NN = (((1,), (0,)), ((), ()))
NT = (((1,), (1,)), ((), ()))


def dot(a, b, dims=NN):
    return lax.dot_general(a, b, dims, preferred_element_type=F32)


def norm_stats(x):
    mean = jnp.mean(x, axis=-1, keepdims=True)
    centred = x - mean
    variance = jnp.mean(centred * centred, axis=-1, keepdims=True)
    rstd = lax.rsqrt(variance + 1e-05)
    return centred * rstd, rstd


def norm_back(grad, xhat, rstd, gain):
    dxhat = grad * gain
    first = jnp.mean(dxhat, axis=-1, keepdims=True)
    second = jnp.mean(dxhat * xhat, axis=-1, keepdims=True)
    return rstd * (dxhat - first - xhat * second)


def cdf_parts(u):
    z = jnp.abs(u)
    t = 1.0 / (1.0 + 0.23164189 * z)
    e = jnp.exp2(u * u * (-0.5 * LOG2E))
    poly = t * (
        0.127414796 + t * (-0.142248368 + t * (0.7107068705 + t * (-0.7265760135 + t * 0.5307027145)))
    )
    tail = poly * e
    return jnp.where(u < 0, tail, 1.0 - tail), e


def one_hot_rows(slot, start, size):
    length = slot.shape[1]
    rows = lax.broadcasted_iota(jnp.int32, (size, length), 0).astype(F32) + start
    return jnp.where(rows == slot, 1.0, 0.0)


def unpermute(slot, src_ref, out_ref):
    length = slot.shape[1]
    wide = jnp.transpose(jnp.broadcast_to(slot, (LANES, length)))
    step = 256
    for start in range(0, length, step):
        col = wide[start : start + step, :1]
        cols = lax.broadcasted_iota(jnp.int32, (step, length), 1).astype(F32)
        pick = jnp.where(cols == col, 1.0, 0.0).astype(BF16)
        out_ref[start : start + step, :] = dot(pick, src_ref[...]).astype(BF16)


def slots_of(mask_ref):
    length = mask_ref.shape[1]
    step = 256
    mask8 = jnp.broadcast_to(mask_ref[...], (8, length))
    cum = []
    for start in range(0, length, step):
        up = lax.broadcasted_iota(jnp.int32, (length, step), 0)
        to = lax.broadcasted_iota(jnp.int32, (length, step), 1) + start
        cum.append(dot(mask8.astype(BF16), jnp.where(up <= to, 1.0, 0.0).astype(BF16)))
    cum = jnp.concatenate(cum, axis=1)
    count = jnp.sum(mask8, axis=1, keepdims=True)
    pos = lax.broadcasted_iota(jnp.int32, (8, length), 1).astype(F32)
    return jnp.where(mask8 > 0.5, cum - 1.0, count + pos - cum), count


def permute_rows(tokens_ref, slot, xp_ref):
    step = 256

    def body(i, _):
        rows = pl.ds(pl.multiple_of(i * step, step), step)
        pick = one_hot_rows(slot[:1], (i * step).astype(F32), step).astype(BF16)
        xp_ref[rows, :] = dot(pick, tokens_ref[...]).astype(BF16)
        return 0

    lax.fori_loop(0, tokens_ref.shape[0] // step, body, 0)


def first_norm(xp_ref, vec_ref, h1_ref):
    step = 128
    gain = vec_ref[0:1, :]
    shift = vec_ref[1:2, :]

    def body(i, _):
        rows = pl.ds(pl.multiple_of(i * step, step), step)
        xhat, _ = norm_stats(xp_ref[rows, :].astype(F32))
        h1_ref[rows, :] = (xhat * gain + shift).astype(BF16)
        return 0

    lax.fori_loop(0, xp_ref.shape[0] // step, body, 0)


def project(h1_ref, vec_ref, wqkv_ref, qkv_ref):
    length, width = h1_ref.shape
    step = 256
    bq = vec_ref[2:3, :]
    bv = vec_ref[3:4, :]

    def body(i, _):
        rows = pl.ds(pl.multiple_of(i * step, step), step)
        h1 = h1_ref[rows, :]
        qkv_ref[rows, :width] = (dot(h1, wqkv_ref[:, :width]) + bq).astype(BF16)
        qkv_ref[rows, width : 2 * width] = dot(h1, wqkv_ref[:, width : 2 * width]).astype(BF16)
        qkv_ref[rows, 2 * width :] = (dot(h1, wqkv_ref[:, 2 * width :]) + bv).astype(BF16)
        return 0

    lax.fori_loop(0, length // step, body, 0)


def attend(qkv_ref, o_ref, lse_ref, beside):
    length, width = o_ref.shape
    step = 256
    c = SCALE * LOG2E
    lane = lax.broadcasted_iota(jnp.int32, (step, LANES), 1)

    def body(n, _):
        beside(n)
        t = n // (length // step)
        i = n % (length // step)
        rows = pl.ds(pl.multiple_of(i * step, step), step)
        q = qkv_ref[rows, pl.ds(pl.multiple_of(t * LANES, LANES), LANES)]
        k = qkv_ref[:, pl.ds(pl.multiple_of(width + t * LANES, LANES), LANES)]
        v = qkv_ref[:, pl.ds(pl.multiple_of(2 * width + t * LANES, LANES), LANES)]
        vo = jnp.concatenate([v, jnp.ones_like(v)], axis=1)
        out = jnp.zeros((step, LANES), F32)
        lses = jnp.zeros((step, LANES), F32)
        for h in range(GROUP):
            mine = lane // HEAD_DIM == h
            s = dot(jnp.where(mine, q, jnp.zeros_like(q)), k, NT)
            top = jnp.max(s, axis=-1, keepdims=True)
            p = jnp.exp2((s - top) * c).astype(BF16)
            ov = dot(p, vo)
            total = ov[:, LANES:]
            out = jnp.where(mine, ov[:, :LANES] / total, out)
            lses = jnp.where(lane == h, top * c + jnp.log2(total), lses)
        o_ref[rows, pl.ds(pl.multiple_of(t * LANES, LANES), LANES)] = out.astype(BF16)
        lse_ref[pl.ds(pl.multiple_of(t * 8, 8), 8), rows] = jnp.transpose(lses)[:8, :]
        return 0

    lax.fori_loop(0, (width // LANES) * (length // step), body, 0)


def join(xp_ref, o_ref, wout_ref, vec_ref, x1_ref):
    step = 256
    bout = vec_ref[4:5, :]

    def body(i, _):
        rows = pl.ds(pl.multiple_of(i * step, step), step)
        x1_ref[rows, :] = xp_ref[rows, :].astype(F32) + dot(o_ref[rows, :], wout_ref[...]) + bout
        return 0

    lax.fori_loop(0, xp_ref.shape[0] // step, body, 0)


def attn_kernel(
    tokens_ref, mask_ref, vec_ref, wqkv_ref, wout_ref,
    slot_ref, xp_ref, h1_ref, qkv_ref, o_ref, lse_ref, x1_ref,
):
    slot, _ = slots_of(mask_ref)
    slot_ref[...] = slot
    permute_rows(tokens_ref, slot, xp_ref)
    first_norm(xp_ref, vec_ref, h1_ref)
    project(h1_ref, vec_ref, wqkv_ref, qkv_ref)
    attend(qkv_ref, o_ref, lse_ref, lambda n: None)
    join(xp_ref, o_ref, wout_ref, vec_ref, x1_ref)


class Place:
    def __init__(self):
        self.me = me = lax.axis_index("fsdp")
        core = me % 2
        x = me // 2 % 2
        y = me // 4
        self.sib = me + 1 - 2 * core
        self.xn = me + 2 - 4 * x
        self.yn = me + 4 - 8 * y
        self.dg = me + 6 - 4 * x - 8 * y


def remote(src, dst, send, recv, to):
    return pltpu.make_async_remote_copy(
        src_ref=src, dst_ref=dst, send_sem=send, recv_sem=recv,
        device_id=to, device_id_type=pl.DeviceIdType.MESH,
    )


class Gather:
    def __init__(self, place, own, full, cut, send, recv, local):
        self.place = place
        rows = own.shape[0]
        at = lambda s, lo=0, hi=rows: full.at[pl.ds(pl.multiple_of(s * rows + lo, 16), hi - lo), :]
        me, sib, xn, yn, dg = place.me, place.sib, place.xn, place.yn, place.dg
        moves = [
            (own, at(me), sib), (own, at(me), xn), (own, at(me), yn),
            (at(xn), at(xn), sib), (at(yn), at(yn), sib),
            (at(xn, 0, cut), at(xn, 0, cut), yn), (at(yn, cut), at(yn, cut), xn),
            (at(dg, 0, cut), at(dg, 0, cut), sib), (at(dg, cut), at(dg, cut), sib),
        ]
        self.copies = [
            remote(src, dst, send.at[i], recv.at[i], {"fsdp": to}) for i, (src, dst, to) in enumerate(moves)
        ]
        self.local = pltpu.make_async_copy(own, at(me), local)

    def first(self):
        self.copies[1].start()
        self.copies[2].start()
        self.copies[0].start()
        self.local.start()

    def second(self):
        self.copies[1].wait_recv()
        self.copies[5].start()
        self.copies[3].start()
        self.copies[2].wait_recv()
        self.copies[6].start()
        self.copies[4].start()

    def third(self):
        self.copies[5].wait_recv()
        self.copies[7].start()
        self.copies[6].wait_recv()
        self.copies[8].start()

    def finish(self):
        for i in (0, 3, 4, 7, 8):
            self.copies[i].wait_recv()
        self.local.wait()
        for copy in self.copies:
            copy.wait_send()


def gather_attn_kernel(
    reps,
    tokens_ref, mask_ref, pack_ref, wqkv_in, wout_in, wup_in, wdn_in,
    slot_ref, xp_ref, h1_ref, qkv_ref, o_ref, lse_ref, x1_ref, vec_ref, bup_ref, over_ref,
    wqkv_ref, wout_ref, wup_ref, wdn_ref,
    packs, overs, send, recv, local, psend, precv, rsend, rrecv,
):
    width = tokens_ref.shape[1]
    share = wqkv_in.shape[0]
    place = Place()
    me = place.me
    rep = lax.axis_index("rep")
    shards = packs.shape[0]
    barrier = pltpu.get_barrier_semaphore()
    for d in range(1, shards):
        pl.semaphore_signal(
            barrier, inc=1, device_id={"fsdp": (me + d) % shards}, device_id_type=pl.DeviceIdType.MESH
        )
    for d in range(1, reps):
        pl.semaphore_signal(
            barrier, inc=1, device_id={"rep": (rep + d) % reps}, device_id_type=pl.DeviceIdType.MESH
        )
    slot, count = slots_of(mask_ref)
    slot_ref[...] = slot
    row = lax.broadcasted_iota(jnp.int32, (16, LANES), 0)
    over = jnp.where(count[:1] > FEW, 1.0, 0.0)
    packs[me] = jnp.where(row == 13, over, pack_ref[...].astype(F32)).astype(BF16)
    pl.semaphore_wait(barrier, shards + reps - 2)

    gathers = []
    for n, (own, full, cut) in enumerate(
        ((wqkv_in, wqkv_ref, 48), (wout_in, wout_ref, 32), (wup_in, wup_ref, 48), (wdn_in, wdn_ref, 320))
    ):
        gathers.append(Gather(place, own, full, cut, send.at[n], recv.at[n], local.at[n]))
    qkv, out, up, down = gathers
    vectors = []
    for d in range(1, shards):
        copy = remote(
            packs.at[me], packs.at[me], psend.at[d - 1], precv.at[d - 1], {"fsdp": (me + d) % shards}
        )
        copy.start()
        vectors.append(copy)
    qkv.first()
    permute_rows(tokens_ref, slot, xp_ref)
    for copy in vectors:
        copy.wait_recv()
    all_over = packs[0]
    for s in range(1, shards):
        all_over = jnp.maximum(all_over, packs[s])
    overs[rep] = all_over
    flags = []
    for d in range(1, reps):
        copy = remote(overs.at[rep], overs.at[rep], rsend.at[d - 1], rrecv.at[d - 1], {"rep": (rep + d) % reps})
        copy.start()
        flags.append(copy)
    qkv.second()
    out.first()
    up.first()
    vecs = jnp.zeros((16, width), F32)
    for s in range(shards):
        pack = packs[s]
        lane = lax.broadcasted_iota(jnp.int32, (LANES, width), 0)
        col = lax.broadcasted_iota(jnp.int32, (LANES, width), 1) - s * share
        spot = jnp.where((lane == col) & (lane < share), 1.0, 0.0).astype(BF16)
        vecs = vecs + dot(pack, spot)
        wide = pack.astype(F32)
        for r in range(width // LANES):
            bup_ref[0:1, s * width + r * LANES : s * width + (r + 1) * LANES] = wide[8 + r : 9 + r, :]
    vec_ref[...] = vecs[:8]
    first_norm(xp_ref, vec_ref, h1_ref)
    qkv.third()
    qkv.finish()
    project(h1_ref, vec_ref, wqkv_ref, qkv_ref)

    def beside(n):
        for at, step in (
            (0, out.second), (2, out.third), (4, up.second), (5, down.first), (9, up.third), (14, down.second),
            (18, down.third),
        ):
            pl.when(n == at)(step)

    attend(qkv_ref, o_ref, lse_ref, beside)
    out.finish()
    join(xp_ref, o_ref, wout_ref, vec_ref, x1_ref)
    for copy in flags:
        copy.wait()
    for copy in vectors:
        copy.wait_send()
    worst = overs[0]
    for z in range(1, reps):
        worst = jnp.maximum(worst, overs[z])
    over_ref[...] = worst[13:14, :].astype(F32)
    up.finish()
    down.finish()


def gather_attn(reps, shards, tokens, mask, pack, w_qkv, w_out, w_up, w_down):
    length, width = tokens.shape
    hidden = w_up.shape[1]
    sds = jax.ShapeDtypeStruct
    groups = width // LANES
    vmem = pl.BlockSpec(memory_space=pltpu.VMEM)
    hbm = pl.BlockSpec(memory_space=pl.ANY)
    dma = pltpu.SemaphoreType.DMA
    return pl.pallas_call(
        functools.partial(gather_attn_kernel, reps),
        in_specs=[vmem] * 3 + [hbm] * 4,
        out_specs=[vmem] * 12 + [hbm] * 2,
        out_shape=(
            sds((8, length), F32),
            sds((length, width), BF16),
            sds((length, width), BF16),
            sds((length, 3 * width), BF16),
            sds((length, width), BF16),
            sds((8 * groups, length), F32),
            sds((length, width), F32),
            sds((8, width), F32),
            sds((1, hidden), F32),
            sds((1, LANES), F32),
            sds((width, 3 * width), BF16),
            sds((width, width), BF16),
            sds((width, hidden), BF16),
            sds((hidden, width), BF16),
        ),
        scratch_shapes=[
            pltpu.VMEM((shards, 16, LANES), BF16),
            pltpu.VMEM((reps, 16, LANES), BF16),
            dma((4, 9)), dma((4, 9)), dma((4,)),
            dma((shards - 1,)), dma((shards - 1,)),
            dma((reps - 1,)), dma((reps - 1,)),
        ],
        compiler_params=pltpu.CompilerParams(
            vmem_limit_bytes=56 * MB, collective_id=0, has_side_effects=True
        ),
        name="gather_attn",
    )(tokens, mask, pack, w_qkv, w_out, w_up, w_down)


def attn_forward(tokens, mask, vecs, wqkv, wout):
    length, width = tokens.shape
    sds = jax.ShapeDtypeStruct
    groups = width // LANES
    return pl.pallas_call(
        attn_kernel,
        out_shape=(
            sds((8, length), F32),
            sds((length, width), BF16),
            sds((length, width), BF16),
            sds((length, 3 * width), BF16),
            sds((length, width), BF16),
            sds((8 * groups, length), F32),
            sds((length, width), F32),
        ),
        compiler_params=pltpu.CompilerParams(vmem_limit_bytes=56 * MB),
        name="attn_forward",
    )(tokens, mask, vecs, wqkv, wout)


def ffn_blocks(few, length):
    part = few if few <= 384 else 256
    blocks = [(start, part, True) for start in range(0, few, part)]
    start = few
    while start < length:
        size = min(320, length - start)
        blocks.append((start, size, False))
        start += size
    return blocks


def ffn_start(blocks, x1_ref, cot_ref, slot_ref, mask_ref, vec_ref, acc, h2, h2t, gy, gyt, dh2):
    gain = vec_ref[5:6, :]
    shift = vec_ref[6:7, :]
    bdown = vec_ref[7:8, :]
    for start, size, back in blocks:
        rows = slice(start, start + size)
        x1 = x1_ref[rows, :]
        xhat, _ = norm_stats(x1)
        hidden = (xhat * gain + shift).astype(BF16)
        h2[rows, :] = hidden
        acc[rows, :] = x1 + bdown
        if back:
            h2t[:, rows] = jnp.transpose(hidden)
            pick = one_hot_rows(slot_ref[0:1, :], float(start), size) * mask_ref[...]
            g = dot(pick.astype(BF16), cot_ref[...])
            gy[rows, :] = g.astype(BF16)
            gyt[:, rows] = jnp.transpose(g.astype(BF16))
            dh2[rows, :] = jnp.zeros_like(g)


def ffn_block(block, wup, wdn, bup, acc, h2, h2t, gy, gyt, dh2):
    start, size, back = block
    rows = slice(start, start + size)
    u = dot(h2[rows, :], wup) + bup
    cdf, e = cdf_parts(u)
    a = (u * cdf).astype(BF16)
    acc[rows, :] += dot(a, wdn)
    if not back:
        return None
    da = dot(gy[rows, :], wdn, NT)
    du = ((cdf + u * e * 0.3989422804014327) * da).astype(BF16)
    dh2[rows, :] += dot(du, wup, NT)
    return (
        dot(h2t[:, rows], du),
        dot(gyt[:, rows], a),
        jnp.sum(du.astype(F32), axis=0, keepdims=True),
    )


def ffn_end(blocks, x1_ref, slot_ref, vec_ref, wout_ref, o_ref, acc, gy, dh2, outp, res_ref, g1_ref, do_ref, small_ref):
    gain = vec_ref[5:6, :]
    ggain = gshift = gbdown = gbout = gout = None
    plus = lambda a, b: b if a is None else a + b
    for start, size, back in blocks:
        rows = slice(start, start + size)
        outp[rows, :] = acc[rows, :].astype(BF16)
        if back:
            xhat, rstd = norm_stats(x1_ref[rows, :])
            d = dh2[rows, :]
            g = gy[rows, :].astype(F32)
            g1 = g + norm_back(d, xhat, rstd, gain)
            g1_ref[rows, :] = g1
            g1b = g1.astype(BF16)
            do_ref[rows, :] = dot(g1b, wout_ref[...], NT).astype(BF16)
            gout = plus(gout, dot(jnp.transpose(o_ref[rows, :]), g1b))
            ggain = plus(ggain, jnp.sum(d * xhat, axis=0, keepdims=True))
            gshift = plus(gshift, jnp.sum(d, axis=0, keepdims=True))
            gbdown = plus(gbdown, jnp.sum(g, axis=0, keepdims=True))
            gbout = plus(gbout, jnp.sum(g1b.astype(F32), axis=0, keepdims=True))
    small_ref[8:9, :] = gbout
    small_ref[9:10, :] = ggain
    small_ref[10:11, :] = gshift
    small_ref[11:12, :] = gbdown
    small_ref[12:16, :] = jnp.zeros((4, outp.shape[1]), F32)
    unpermute(slot_ref[0:1, :], outp, res_ref)
    return gout


def ffn_kernel(
    few,
    x1_ref, cot_ref, slot_ref, mask_ref, vec_ref, bup_ref, wup_ref, wdn_ref, wout_ref, o_ref,
    res_ref, gup_ref, gdn_ref, g1_ref, do_ref, gout_ref, small_ref,
    acc, h2, h2t, gy, gyt, dh2, outp,
):
    j = pl.program_id(0)
    length, width = x1_ref.shape
    blocks = ffn_blocks(few, length)

    @pl.when(j == 0)
    def _():
        ffn_start(blocks, x1_ref, cot_ref, slot_ref, mask_ref, vec_ref, acc, h2, h2t, gy, gyt, dh2)

    total = None
    for block in blocks:
        part = ffn_block(block, wup_ref[...], wdn_ref[...], bup_ref[...], acc, h2, h2t, gy, gyt, dh2)
        if part is not None:
            total = part if total is None else [x + y for x, y in zip(total, part)]
    gup, gdn, gbup = total
    gup_ref[...] = gup.astype(BF16)
    for n in range(gdn_ref.shape[0]):
        cols = slice(n * width, (n + 1) * width)
        gdn_ref[n] = gdn[:, cols].astype(BF16)
        small_ref[pl.ds(j * gdn_ref.shape[0] + n, 1), :] = gbup[:, cols]

    @pl.when(j == pl.num_programs(0) - 1)
    def _():
        gout = ffn_end(
            blocks, x1_ref, slot_ref, vec_ref, wout_ref, o_ref, acc, gy, dh2, outp, res_ref, g1_ref, do_ref, small_ref
        )
        gout_ref[...] = gout.astype(BF16)


def feed_forward(few, x1, cot, slot, mask, vecs, bup, wup, wdn, wout, o):
    length, width = x1.shape
    hidden = wup.shape[1]
    fc = 2 * width
    sds = jax.ShapeDtypeStruct
    whole = lambda *shape: pl.BlockSpec(shape, lambda j: (0,) * len(shape))
    return pl.pallas_call(
        functools.partial(ffn_kernel, few),
        grid=(hidden // fc,),
        in_specs=[
            whole(length, width),
            whole(length, width),
            whole(8, length),
            whole(1, length),
            whole(8, width),
            pl.BlockSpec((1, fc), lambda j: (0, j)),
            pl.BlockSpec((width, fc), lambda j: (0, j)),
            pl.BlockSpec((fc, width), lambda j: (j, 0)),
            whole(width, width),
            whole(few, width),
        ],
        out_specs=[
            whole(length, width),
            pl.BlockSpec((width, fc), lambda j: (0, j)),
            pl.BlockSpec((2, width, width), lambda j: (j, 0, 0)),
            whole(few, width),
            whole(few, width),
            whole(width, width),
            whole(16, width),
        ],
        out_shape=(
            sds((length, width), BF16),
            sds((width, hidden), BF16),
            sds((hidden // width, width, width), BF16),
            sds((few, width), F32),
            sds((few, width), BF16),
            sds((width, width), BF16),
            sds((16, width), F32),
        ),
        scratch_shapes=[
            pltpu.VMEM((length, width), F32),
            pltpu.VMEM((length, width), BF16),
            pltpu.VMEM((width, few), BF16),
            pltpu.VMEM((few, width), BF16),
            pltpu.VMEM((width, few), BF16),
            pltpu.VMEM((few, width), F32),
            pltpu.VMEM((length, width), BF16),
        ],
        compiler_params=pltpu.CompilerParams(vmem_limit_bytes=56 * MB),
        name="feed_forward",
    )(x1, cot, slot, mask, vecs, bup, wup, wdn, wout, o)


class Heads:
    step = 256

    def __init__(self, few, q_ref, k_ref, v_ref, do_ref, o_ref, lse_ref, dqt, dkv):
        self.k_ref, self.v_ref, self.lse_ref, self.dqt, self.dkv = k_ref, v_ref, lse_ref, dqt, dkv
        q = q_ref[...]
        do = do_ref[...]
        lane = lax.broadcasted_iota(jnp.int32, (few, LANES), 1)
        head = lax.broadcasted_iota(jnp.int32, (8, LANES), 0)
        lane8 = lax.broadcasted_iota(jnp.int32, (8, LANES), 1)
        pick = jnp.where(lane8 // HEAD_DIM == head, 1.0, 0.0)
        self.delta = lax.dot_general(
            pick, do.astype(F32) * o_ref[...].astype(F32), NT,
            precision=lax.Precision.HIGHEST, preferred_element_type=F32,
        )
        dqt[...] = jnp.zeros_like(dqt)
        zero = jnp.zeros_like(q)
        self.qs = [jnp.where(lane // HEAD_DIM == h, q, zero) for h in range(GROUP)]
        self.dos = [jnp.where(lane // HEAD_DIM == h, do, zero) for h in range(GROUP)]

    def keys(self, i):
        step = self.step
        rows = pl.ds(pl.multiple_of(i * step, step), step)
        k = self.k_ref[rows, :]
        v = self.v_ref[rows, :]
        kt = jnp.transpose(k)
        dk = jnp.zeros((step, LANES), F32)
        dv = jnp.zeros((step, LANES), F32)
        for h in range(GROUP):
            s = dot(k, self.qs[h], NT)
            p = jnp.exp2(s * (SCALE * LOG2E) - self.lse_ref[h : h + 1, :])
            dp = dot(v, self.dos[h], NT)
            ds = (p * (dp - self.delta[h : h + 1, :])).astype(BF16)
            dv = dv + dot(p.astype(BF16), self.dos[h])
            dk = dk + dot(ds, self.qs[h])
            part = slice(h * HEAD_DIM, (h + 1) * HEAD_DIM)
            self.dqt[part, :] += dot(kt[part, :], ds)
        self.dkv[rows, :LANES] = (dk * SCALE).astype(BF16)
        self.dkv[rows, LANES:] = dv.astype(BF16)


def transpose_rows(src_ref, out_ref):
    step = 256
    for start in range(0, src_ref.shape[0], step):
        out_ref[:, start : start + step] = jnp.transpose(src_ref[start : start + step, :])


def group_weights(few, dqt, dkv, h1t, small_ref, cols):
    dq = (jnp.transpose(dqt[...]) * SCALE).astype(BF16)
    gq = dot(h1t[:, :few], dq).astype(BF16)
    gkv = dot(h1t[...], dkv[...]).astype(BF16)
    small_ref[2:3, cols] = jnp.sum(dq.astype(F32), axis=0, keepdims=True)
    small_ref[3:4, cols] = jnp.sum(dkv[:, LANES:].astype(F32), axis=0, keepdims=True)
    return dq, gq, gkv[:, :LANES], gkv[:, LANES:]


def group_inputs(few, dq, dkv, wq_ref, wk_ref, wv_ref, dh1):
    step = 256
    wkv = jnp.concatenate([wk_ref[...], wv_ref[...]], axis=1)
    for start in range(0, dh1.shape[0], step):
        rows = slice(start, start + step)
        dh1[rows, :] += dot(dkv[rows, :], wkv, NT)
    dh1[:few, :] += dot(dq, wq_ref[...], NT)


def back_finish(few, dh1_ref, xp_ref, vec_ref, g1_ref, small_ref, gtp):
    length, width = xp_ref.shape
    gain = vec_ref[0:1, :]
    step = 128
    ggain = gshift = jnp.zeros((1, width), F32)
    for start in range(0, length, step):
        rows = slice(start, start + step)
        xhat, rstd = norm_stats(xp_ref[rows, :].astype(F32))
        d = dh1_ref[rows, :]
        g = norm_back(d, xhat, rstd, gain)
        if start < few:
            g = g + g1_ref[rows, :]
        gtp[rows, :] = g.astype(BF16)
        ggain = ggain + jnp.sum(d * xhat, axis=0, keepdims=True)
        gshift = gshift + jnp.sum(d, axis=0, keepdims=True)
    small_ref[0:1, :] = ggain
    small_ref[1:2, :] = gshift


def back_kernel(
    few,
    q, k, v, do, o, lse, h1, xp, vec, wq, wk, wv, g1, slot,
    gtok, gq_ref, gk_ref, gv_ref, small,
    h1t, dh1, dqt, dkv, gtp,
):
    t = pl.program_id(0)
    cols = pl.ds(pl.multiple_of(t * LANES, LANES), LANES)

    @pl.when(t == 0)
    def _():
        transpose_rows(h1, h1t)
        dh1[...] = jnp.zeros_like(dh1)
        small[...] = jnp.zeros_like(small)

    heads = Heads(few, q, k, v, do, o, lse, dqt, dkv)

    def body(i, _):
        heads.keys(i)
        return 0

    lax.fori_loop(0, h1.shape[0] // heads.step, body, 0)
    dq, gq, gk, gv = group_weights(few, dqt, dkv, h1t, small, cols)
    gq_ref[...] = gq
    gk_ref[...] = gk
    gv_ref[...] = gv
    group_inputs(few, dq, dkv, wq, wk, wv, dh1)

    @pl.when(t == pl.num_programs(0) - 1)
    def _():
        back_finish(few, dh1, xp, vec, g1, small, gtp)
        unpermute(slot[0:1, :], gtp, gtok)


def back_specs(few, length, width):
    groups = width // LANES
    whole = lambda *shape: pl.BlockSpec(shape, lambda t: (0,) * len(shape))
    cols = lambda rows, first: pl.BlockSpec((rows, LANES), lambda t: (0, first + t))
    in_specs = [
        cols(few, 0),
        cols(length, groups),
        cols(length, 2 * groups),
        cols(few, 0),
        cols(few, 0),
        pl.BlockSpec((8, few), lambda t: (t, 0)),
        whole(length, width),
        whole(length, width),
        whole(8, width),
        cols(width, 0),
        cols(width, groups),
        cols(width, 2 * groups),
        whole(few, width),
        whole(8, length),
    ]
    scratch = [
        pltpu.VMEM((width, length), BF16),
        pltpu.VMEM((length, width), F32),
        pltpu.VMEM((LANES, few), F32),
        pltpu.VMEM((length, 2 * LANES), BF16),
        pltpu.VMEM((length, width), BF16),
    ]
    return whole, cols, in_specs, scratch


def attn_backward(few, qkv, do, o, lse, h1, xp, vecs, wqkv, g1, slot):
    length, width = h1.shape
    sds = jax.ShapeDtypeStruct
    whole, cols, in_specs, scratch = back_specs(few, length, width)
    return pl.pallas_call(
        functools.partial(back_kernel, few),
        grid=(width // LANES,),
        in_specs=in_specs,
        out_specs=[whole(length, width), cols(width, 0), cols(width, 0), cols(width, 0), whole(8, width)],
        out_shape=(
            sds((length, width), BF16),
            sds((width, width), BF16),
            sds((width, width), BF16),
            sds((width, width), BF16),
            sds((8, width), F32),
        ),
        scratch_shapes=scratch,
        compiler_params=pltpu.CompilerParams(vmem_limit_bytes=56 * MB),
        name="attn_backward",
    )(qkv, qkv, qkv, do, o, lse, h1, xp, vecs, wqkv, wqkv, wqkv, g1, slot)


class Reduce:
    def __init__(self, place, rep, reps, mine, other, acc, near, side, last, depth, fin, sems):
        send, recv, local = sems
        self.rep, self.reps = rep, reps
        self.acc, self.near, self.side, self.last, self.depth, self.fin = acc, near, side, last, depth, fin
        chip = place.me // 2
        cx, cy, cd = place.xn // 2, place.yn // 2, place.dg // 2
        self.chip, self.cx, self.cy = chip, cx, cy
        fsdp = lambda d: {"fsdp": d}
        low, high = slice(0, 2), slice(2, 4)
        n = iter(range(100))
        def copy(src, dst, to):
            i = next(n)
            return remote(src, dst, send.at[i], recv.at[i], to)
        self.a = [copy(other[q], near.at[:, q], fsdp(place.sib)) for q in range(4)]
        self.own = [pltpu.make_async_copy(mine[q], acc.at[:, q], local.at[q]) for q in range(4)]
        self.b = [
            copy(acc.at[cx, low], side.at[0], fsdp(place.xn)),
            copy(acc.at[cy, high], side.at[2], fsdp(place.yn)),
            copy(acc.at[cd, low], side.at[1], fsdp(place.xn)),
            copy(acc.at[cd, high], side.at[3], fsdp(place.yn)),
        ]
        self.c = [
            copy(acc.at[cy, low], last.at[0], fsdp(place.yn)),
            copy(acc.at[cx, high], last.at[1], fsdp(place.xn)),
        ]
        peers = [(rep + d) % reps for d in range(1, reps)]
        self.d = [copy(acc.at[chip, z], depth.at[i], {"rep": z}) for i, z in enumerate(peers)]
        self.e = [copy(fin.at[rep], fin.at[rep], {"rep": z}) for z in peers]

    COPIES = 16

    def start(self):
        for x in self.a + self.own:
            x.start()

    def near_sum(self):
        for q in range(4):
            self.own[q].wait()
            self.a[q].wait_recv()
            for c in range(4):
                self.acc[c, q] = (self.acc[c, q].astype(F32) + self.near[c, q].astype(F32)).astype(BF16)
        for x in self.b:
            x.start()

    def add(self, c, half, part):
        for q in range(2):
            self.acc[c, half + q] = (self.acc[c, half + q].astype(F32) + part[q].astype(F32)).astype(BF16)

    def side_sum(self):
        for x in self.b:
            x.wait()
        self.add(self.cy, 0, self.side.at[1])
        self.c[0].start()
        self.add(self.cx, 2, self.side.at[3])
        self.c[1].start()
        self.add(self.chip, 0, self.side.at[0])
        self.add(self.chip, 2, self.side.at[2])

    def last_sum(self):
        for x in self.c:
            x.wait()
        self.add(self.chip, 0, self.last.at[0])
        self.add(self.chip, 2, self.last.at[1])
        for x in self.d:
            x.start()

    def depth_sum(self):
        total = self.acc[self.chip, self.rep].astype(F32)
        for i in range(self.reps - 1):
            self.d[i].wait()
            total = total + self.depth[i].astype(F32)
        self.fin[self.rep] = total.astype(BF16)
        for x in self.e:
            x.start()

    def finish(self):
        for x in self.e:
            x.wait()
        for x in self.a:
            x.wait_send()


class Small:
    def __init__(self, me, shards, rep, reps, rows, beside, depth, out, sems):
        psend, precv, rsend, rrecv = sems
        self.me, self.rep, self.rows, self.near, self.depth, self.out = me, rep, rows, beside, depth, out
        self.first = [
            remote(beside.at[me], beside.at[me], psend.at[d - 1], precv.at[d - 1], {"fsdp": (me + d) % shards})
            for d in range(1, shards)
        ]
        self.second = [
            remote(depth.at[rep], depth.at[rep], rsend.at[d - 1], rrecv.at[d - 1], {"rep": (rep + d) % reps})
            for d in range(1, reps)
        ]

    def start(self):
        self.near[self.me] = self.rows[...]
        for x in self.first:
            x.start()

    def middle(self):
        for x in self.first:
            x.wait()
        total = self.near[0]
        for s in range(1, self.near.shape[0]):
            total = total + self.near[s]
        self.depth[self.rep] = total
        for x in self.second:
            x.start()

    def finish(self):
        for x in self.second:
            x.wait()
        total = self.depth[0]
        for z in range(1, self.depth.shape[0]):
            total = total + self.depth[z]
        self.out[...] = total


def reduce_back_kernel(
    few, shards, reps,
    q, k, v, do, o, lse, h1, xp, vec, wq, wk, wv, g1, slot, early_ref, gout_ref, gup_ref, gdn_ref,
    gtok, gup_out, gdn_out, gqkv_out, gout_out, early_out, late_out,
    h1t, dh1, dqt, dkv, gtp, late, gqkv, fin, acc, near, side, last, depth, send, recv, local,
    enear, edepth, lnear, ldepth, es1, er1, es2, er2, ls1, lr1, ls2, lr2,
):
    t = pl.program_id(0)
    cols = pl.ds(pl.multiple_of(t * LANES, LANES), LANES)
    share = h1.shape[1] // shards
    width = h1.shape[1]
    place = Place()
    rep = lax.axis_index("rep")
    core = place.me % 2

    def quarter(n, side):
        u = n // 4
        if u < 2:
            return gup_ref.at[:, side, :, n * width : (n + 1) * width]
        if u < 4:
            return gdn_ref.at[:, side, (n - 8) * share : (n - 7) * share, :]
        return gout_ref.at[:, side] if n == 16 else gqkv.at[n - 17, :, side]

    units = []
    for u in range(5):
        sems = (send.at[u], recv.at[u], local.at[u])
        units.append(
            Reduce(
                place, rep, reps,
                [quarter(4 * u + n, core) for n in range(4)],
                [quarter(4 * u + n, 1 - core) for n in range(4)],
                acc.at[u], near.at[u], side.at[u], last.at[u], depth.at[u], fin.at[u], sems,
            )
        )
    early = Small(place.me, shards, rep, reps, early_ref, enear, edepth, early_out, (es1, er1, es2, er2))
    later = Small(place.me, shards, rep, reps, late, lnear, ldepth, late_out, (ls1, lr1, ls2, lr2))

    @pl.when(t == 0)
    def _():
        barrier = pltpu.get_barrier_semaphore()
        for d in range(1, shards):
            pl.semaphore_signal(
                barrier, inc=1, device_id={"fsdp": (place.me + d) % shards},
                device_id_type=pl.DeviceIdType.MESH,
            )
        for d in range(1, reps):
            pl.semaphore_signal(
                barrier, inc=1, device_id={"rep": (rep + d) % reps}, device_id_type=pl.DeviceIdType.MESH
            )
        pl.semaphore_wait(barrier, shards + reps - 2)
        for u in range(4):
            units[u].start()
        early.start()
        transpose_rows(h1, h1t)
        dh1[...] = jnp.zeros_like(dh1)
        late[...] = jnp.zeros_like(late)

    heads = Heads(few, q, k, v, do, o, lse, dqt, dkv)
    blocks = h1.shape[0] // heads.step

    plan = [
        (1, units[0].near_sum), (2, units[1].near_sum), (3, units[2].near_sum), (4, units[3].near_sum),
        (5, early.middle), (6, units[0].side_sum), (9, units[1].side_sum), (10, units[0].last_sum),
        (11, early.finish), (13, units[2].side_sum), (14, units[1].last_sum), (15, units[0].depth_sum),
        (17, units[3].side_sum), (18, units[2].last_sum), (19, units[1].depth_sum),
    ]

    def body(i, _):
        for at, step in plan:
            pl.when(t * blocks + i == at)(step)
        heads.keys(i)
        return 0

    lax.fori_loop(0, blocks, body, 0)
    dq, gq, gk, gv = group_weights(few, dqt, dkv, h1t, late, cols)
    chips = shards // 2
    for n, g in enumerate((gq, gk, gv)):
        gqkv[n, :, :, :, cols] = g.reshape(chips, 2, share, LANES)
    final = t == pl.num_programs(0) - 1
    pl.when(final)(units[4].start)
    group_inputs(few, dq, dkv, wq, wk, wv, dh1)

    @pl.when(final)
    def _():
        units[4].near_sum()
        units[3].last_sum()
        units[2].depth_sum()
        back_finish(few, dh1, xp, vec, g1, late, gtp)
        later.start()
        units[4].side_sum()
        units[3].depth_sum()
        units[4].last_sum()
        later.middle()
        unpermute(slot[0:1, :], gtp, gtok)
        units[4].depth_sum()
        for n in range(16):
            if n % 4 == 0:
                units[n // 4].finish()
            part = fin[n // 4, n % 4].astype(F32)
            if n < 8:
                gup_out[:, n * width : (n + 1) * width] = part
            else:
                gdn_out[:, (n - 8) * share : (n - 7) * share] = jnp.transpose(part)
        later.finish()
        units[4].finish()
        gout_out[...] = fin[4, 0].astype(F32)
        for n in range(3):
            gqkv_out[:, n * width : (n + 1) * width] = fin[4, 1 + n].astype(F32)


def reduce_backward(few, shards, reps, ident, qkv, do, o, lse, h1, xp, vecs, wqkv, g1, slot, early, gout, gup, gdn):
    length, width = h1.shape
    share = width // shards
    chips = shards // 2
    sds = jax.ShapeDtypeStruct
    whole, cols, in_specs, scratch = back_specs(few, length, width)
    hbm = pl.BlockSpec(memory_space=pl.ANY)
    dma = pltpu.SemaphoreType.DMA
    block = (share, width)
    copies = Reduce.COPIES
    hidden = gup.shape[1]
    return pl.pallas_call(
        functools.partial(reduce_back_kernel, few, shards, reps),
        grid=(width // LANES,),
        in_specs=in_specs + [whole(16, width), hbm, hbm, hbm],
        out_specs=[
            whole(length, width), whole(share, hidden), whole(width, width), whole(share, 3 * width),
            whole(share, width), whole(16, width), whole(8, width),
        ],
        out_shape=(
            sds((length, width), BF16),
            sds((share, hidden), F32),
            sds((width, width), F32),
            sds((share, 3 * width), F32),
            sds((share, width), F32),
            sds((16, width), F32),
            sds((8, width), F32),
        ),
        scratch_shapes=scratch
        + [
            pltpu.VMEM((8, width), F32),
            pltpu.VMEM((3, chips, 2) + block, BF16),
            pltpu.VMEM((5, 4) + block, BF16),
            pltpu.VMEM((5, chips, 4) + block, BF16),
            pltpu.VMEM((5, chips, 4) + block, BF16),
            pltpu.VMEM((5, 4, 2) + block, BF16),
            pltpu.VMEM((5, 2, 2) + block, BF16),
            pltpu.VMEM((5, reps - 1) + block, BF16),
            dma((5, copies)), dma((5, copies)), dma((5, 4)),
            pltpu.VMEM((shards, 16, width), F32),
            pltpu.VMEM((reps, 16, width), F32),
            pltpu.VMEM((shards, 8, width), F32),
            pltpu.VMEM((reps, 8, width), F32),
            dma((shards - 1,)), dma((shards - 1,)), dma((reps - 1,)), dma((reps - 1,)),
            dma((shards - 1,)), dma((shards - 1,)), dma((reps - 1,)), dma((reps - 1,)),
        ],
        compiler_params=pltpu.CompilerParams(
            vmem_limit_bytes=60 * MB, collective_id=ident, has_side_effects=True
        ),
        name="reduce_backward",
    )(
        qkv, qkv, qkv, do, o, lse, h1, xp, vecs, wqkv, wqkv, wqkv, g1, slot, early,
        gout.reshape(chips, 2, share, width),
        gup.reshape(chips, 2, share, hidden),
        gdn.reshape(chips, 2, width, width),
    )


class Unit:
    COPIES = 10

    def __init__(self, place, rep, other, acc, near, side, last, own, depth, fin, send, recv):
        self.acc, self.near, self.side, self.last = acc, near, side, last
        self.own, self.depth, self.fin = own, depth, fin
        chip = place.me // 2
        cx, cy, cd = place.xn // 2, place.yn // 2, place.dg // 2
        self.chip, self.cx, self.cy = chip, cx, cy
        fsdp = lambda d: {"fsdp": d}

        def copy(i, src, dst, to):
            return remote(src, dst, send.at[i], recv.at[i], to)

        if other is not None:
            self.a = copy(0, other, near, fsdp(place.sib))
        if side is not None:
            half = acc.shape[1] // 2
            self.low, self.high = low, high = pl.ds(0, half), pl.ds(half, half)
            self.b = [
                copy(1, acc.at[cd, low], side.at[1], fsdp(place.xn)),
                copy(2, acc.at[cd, high], side.at[3], fsdp(place.yn)),
                copy(3, acc.at[cx, low], side.at[0], fsdp(place.xn)),
                copy(4, acc.at[cy, high], side.at[2], fsdp(place.yn)),
            ]
            self.c = [
                copy(5, acc.at[cy, low], last.at[0], fsdp(place.yn)),
                copy(6, acc.at[cx, high], last.at[1], fsdp(place.xn)),
            ]
        if own is None:
            self.own = own = acc.at[chip]
        if depth is not None:
            inner = (rep == 1) | (rep == 2)
            self.inner, self.outer = inner, jnp.logical_not(inner)
            pair = {"rep": rep + 1 - 2 * (rep % 2)}
            self.d = copy(7, own, depth.at[0], pair)
            self.e = copy(8, own, depth.at[1], {"rep": 3 - rep})
            self.f = copy(9, fin, fin, pair)

    def near_start(self):
        self.a.start()

    def near_add(self):
        self.a.wait_recv()
        for c in range(self.acc.shape[0]):
            self.acc[c] = self.acc[c] + self.near[c]

    def side_start(self):
        for x in self.b:
            x.start()

    def near_sum(self):
        self.near_add()
        self.side_start()

    def add(self, c, half, ref):
        self.acc[c, half, :] = self.acc[c, half, :] + ref[...]

    def side_sum(self):
        self.b[0].wait()
        self.add(self.cy, self.low, self.side.at[1])
        self.c[0].start()
        self.b[1].wait()
        self.add(self.cx, self.high, self.side.at[3])
        self.c[1].start()
        self.b[2].wait()
        self.add(self.chip, self.low, self.side.at[0])
        self.b[3].wait()
        self.add(self.chip, self.high, self.side.at[2])

    def last_add(self):
        for x in self.c:
            x.wait()
        self.add(self.chip, self.low, self.last.at[0])
        self.add(self.chip, self.high, self.last.at[1])

    def z1_start(self):
        pl.when(self.outer)(self.d.start)

    def last_sum(self):
        self.last_add()
        self.z1_start()

    def z1_done(self):
        pl.when(self.outer)(self.d.wait_send)

        @pl.when(self.inner)
        def _():
            self.d.wait_recv()
            self.own[...] = self.own[...] + self.depth[0]

    def z2_start(self):
        pl.when(self.inner)(self.e.start)

    def z1z2(self):
        self.z1_done()
        self.z2_start()

    def z2z3(self):
        @pl.when(self.inner)
        def _():
            self.e.wait()
            self.fin[...] = self.own[...] + self.depth[1]
            self.f.start()

    def z3_done(self):
        pl.when(self.inner)(self.f.wait_send)
        pl.when(self.outer)(self.f.wait_recv)


def per_shard(rows, shards, share):
    out = []
    for n in range(shards):
        at = lax.broadcasted_iota(jnp.int32, (rows.shape[1], LANES), 0) - n * share
        lane = lax.broadcasted_iota(jnp.int32, (rows.shape[1], LANES), 1)
        spot = jnp.where((at == lane) & (lane < share), 1.0, 0.0).astype(BF16)
        out.append(dot(rows, spot).astype(BF16))
    return out


def greet(me, shards, rep, reps):
    barrier = pltpu.get_barrier_semaphore()
    mesh = pl.DeviceIdType.MESH
    for d in range(1, shards):
        pl.semaphore_signal(barrier, inc=1, device_id={"fsdp": (me + d) % shards}, device_id_type=mesh)
    for d in range(1, reps):
        pl.semaphore_signal(barrier, inc=1, device_id={"rep": (rep + d) % reps}, device_id_type=mesh)
    pl.semaphore_wait(barrier, shards + reps - 2)


CHUNKS = 5


def ffn_reduce_kernel(
    few, shards, reps,
    x1_ref, cot_ref, slot_ref, mask_ref, vec_ref, wout_ref, o_ref, *refs,
):
    bups, wups, wdns = refs[:shards], refs[shards : 2 * shards], refs[2 * shards : 3 * shards]
    (
        res_ref, g1_ref, do_ref, gout_ref, state_ref, plane_ref,
        acc, h2, h2t, gy, gyt, dh2, outp, small_ref, g, near, side, last, depth, fin, send, recv,
    ) = refs[3 * shards :]
    j = pl.program_id(0)
    length, width = x1_ref.shape
    share = width // shards
    blocks = ffn_blocks(few, length)
    place = Place()
    rep = lax.axis_index("rep")
    core = place.me % 2
    units = []
    for u in range(CHUNKS):
        xy = u < 4
        z = u < 2
        units.append(
            Unit(
                place, rep, g.at[u, 1 - core], g.at[u, core], near.at[u],
                side.at[u] if xy else None, last.at[u] if xy else None, None,
                depth.at[u] if z else None, fin if z else None, send.at[u], recv.at[u],
            )
        )

    def at(step, *acts):
        @pl.when(j == step)
        def _():
            for act in acts:
                act()

    @pl.when(j == 0)
    def _():
        greet(place.me, shards, rep, reps)
        ffn_start(blocks, x1_ref, cot_ref, slot_ref, mask_ref, vec_ref, acc, h2, h2t, gy, gyt, dh2)

    wup = jnp.concatenate([w[...] for w in wups], axis=1)
    wdn = jnp.concatenate([w[...] for w in wdns], axis=0)
    bup = jnp.concatenate([b[...] for b in bups], axis=1)
    cols = pl.ds(pl.multiple_of(j * LANES, LANES), LANES)
    for n, block in enumerate(blocks):
        part = ffn_block(block, wup, wdn, bup, acc, h2, h2t, gy, gyt, dh2)
        if n == 0:
            gup, gdn, gbup = part
            for s in range(shards):
                mine = slice(s * share, (s + 1) * share)
                lanes = slice(s * LANES, (s + 1) * LANES)
                for b in range(shards):
                    g[j, s % 2, s // 2, b * share : (b + 1) * share, :] = gup[
                        mine, b * LANES : (b + 1) * LANES
                    ].astype(BF16)
                g[j, s % 2, s // 2, width:, :] = gdn[:, lanes].astype(BF16)
                small_ref[s : s + 1, cols] = gbup[:, lanes]
            for u in range(CHUNKS):
                at(u, units[u].near_start)
        if n == 1:
            at(2, units[0].last_sum)
            at(3, units[0].z1z2, units[1].last_sum)
            at(4, units[0].z2z3, units[2].last_add)
        if n == 2:
            for u in range(CHUNKS):
                if u:
                    at(u, units[u - 1].side_sum)
                at(u, units[u].near_sum if u < 4 else units[u].near_add)
            at(4, units[1].z1_done)

    @pl.when(j == CHUNKS - 1)
    def _():
        gout = ffn_end(
            blocks, x1_ref, slot_ref, vec_ref, wout_ref, o_ref, acc, gy, dh2, outp, res_ref, g1_ref, do_ref, small_ref
        )
        for s in range(shards):
            for b in range(CHUNKS):
                gout_ref[s % 2, s // 2, b * share : (b + 1) * share, :] = gout[
                    s * share : (s + 1) * share, b * LANES : (b + 1) * LANES
                ].astype(BF16)
        rows = CHUNKS * share
        vectors = per_shard(small_ref[8:16, :].astype(BF16), shards, share)
        for s in range(shards):
            gout_ref[s % 2, s // 2, rows : rows + 8, :] = vectors[s]
            bias = [small_ref[s : s + 1, b * LANES : (b + 1) * LANES] for b in range(CHUNKS)]
            bias = jnp.concatenate(bias + [jnp.zeros((8 - CHUNKS, LANES), F32)], axis=0)
            gout_ref[s % 2, s // 2, rows + 8 : rows + 16, :] = bias.astype(BF16)
            spare = gout_ref.shape[2] - rows - 16
            gout_ref[s % 2, s // 2, rows + 16 :, :] = jnp.zeros((spare, LANES), BF16)
        plane_ref[...] = g[4, core]
        units[3].last_add()
        for u in range(1, 4):
            state_ref[u] = g[u, core, units[u].chip]
        units[0].z3_done()
        state_ref[0] = fin[...]
        for u in range(CHUNKS):
            units[u].a.wait_send()


def ffn_reduce(few, shards, reps, x1, cot, slot, mask, vecs, bup, wup, wdn, wout, o):
    length, width = x1.shape
    share = width // shards
    chips = shards // 2
    rows = 2 * width
    spare = 448
    sds = jax.ShapeDtypeStruct
    whole = lambda *shape: pl.BlockSpec(shape, lambda j: (0,) * len(shape))
    pick = lambda s, shape, across: pl.BlockSpec(
        shape, lambda j: (0, s * CHUNKS + j) if across else (s * CHUNKS + j, 0)
    )
    dma = pltpu.SemaphoreType.DMA
    return pl.pallas_call(
        functools.partial(ffn_reduce_kernel, few, shards, reps),
        grid=(CHUNKS,),
        in_specs=[
            whole(length, width), whole(length, width), whole(8, length), whole(1, length), whole(8, width),
            whole(width, width), whole(few, width),
        ]
        + [pick(s, (1, LANES), True) for s in range(shards)]
        + [pick(s, (width, LANES), True) for s in range(shards)]
        + [pick(s, (LANES, width), False) for s in range(shards)],
        out_specs=[
            whole(length, width), whole(few, width), whole(few, width), whole(2, chips, spare, LANES),
            whole(4, rows, LANES), whole(chips, rows, LANES),
        ],
        out_shape=(
            sds((length, width), BF16),
            sds((few, width), F32),
            sds((few, width), BF16),
            sds((2, chips, spare, LANES), BF16),
            sds((4, rows, LANES), BF16),
            sds((chips, rows, LANES), BF16),
        ),
        scratch_shapes=[
            pltpu.VMEM((length, width), F32),
            pltpu.VMEM((length, width), BF16),
            pltpu.VMEM((width, few), BF16),
            pltpu.VMEM((few, width), BF16),
            pltpu.VMEM((width, few), BF16),
            pltpu.VMEM((few, width), F32),
            pltpu.VMEM((length, width), BF16),
            pltpu.VMEM((16, width), F32),
            pltpu.VMEM((CHUNKS, 2, chips, rows, LANES), BF16),
            pltpu.VMEM((CHUNKS, chips, rows, LANES), BF16),
            pltpu.VMEM((4, 4, rows // 2, LANES), BF16),
            pltpu.VMEM((4, 2, rows // 2, LANES), BF16),
            pltpu.VMEM((2, 2, rows, LANES), BF16),
            pltpu.VMEM((rows, LANES), BF16),
            dma((CHUNKS, Unit.COPIES)), dma((CHUNKS, Unit.COPIES)),
        ],
        compiler_params=pltpu.CompilerParams(
            vmem_limit_bytes=60 * MB, collective_id=3, has_side_effects=True
        ),
        name="ffn_reduce",
    )(x1, cot, slot, mask, vecs, wout, o, *[bup] * shards, *[wup] * shards, *[wdn] * shards)


GROUP_ROWS = 256


def back_reduce_kernel(
    few, shards, reps,
    q, k, v, do, o, lse, h1, xp, vec, wq, wk, wv, g1, slot, state_in, plane_in, gout_in,
    gtok, gup_out, gdn_out, gqkv_out, gout_out, vec_out,
    h1t, dh1, dqt, dkv, gtp, late,
    own, plane, fside, flast, fdepth, ffin,
    onear, oacc, oside, olast, odepth, ofin,
    gg, gnear, gside, glast, gdepth, gfin,
    sg, snear, sside, slast, sdepth, sfin,
    send, recv, local,
):
    t = pl.program_id(0)
    groups = pl.num_programs(0)
    length, width = h1.shape
    share = width // shards
    cols = pl.ds(pl.multiple_of(t * LANES, LANES), LANES)
    place = Place()
    rep = lax.axis_index("rep")
    core = place.me % 2
    sems = lambda n: (send.at[n], recv.at[n])
    make = functools.partial(Unit, place, rep)
    u1, u2, u3 = [
        make(None, own, None, None, None, own.at[n], fdepth.at[n - 1], ffin.at[n - 1], *sems(n - 1))
        for n in range(1, 4)
    ]
    u4 = make(None, plane, None, fside, flast, None, fdepth.at[3], ffin.at[3], *sems(3))
    uo = make(gout_in.at[1 - core], oacc, onear, oside, olast, None, odepth, ofin, *sems(4))
    us = make(sg.at[1 - core], sg.at[core], snear, sside, slast, None, sdepth, sfin, *sems(5))
    parts = [
        make(
            gg.at[n, 1 - core], gg.at[n, core], gnear.at[n], gside.at[n], glast.at[n], None, gdepth.at[n],
            gfin.at[n], *sems(6 + n)
        )
        for n in range(5)
    ]
    loads = [
        pltpu.make_async_copy(state_in, own, local.at[0]),
        pltpu.make_async_copy(plane_in, plane, local.at[1]),
        pltpu.make_async_copy(gout_in.at[core], oacc, local.at[2]),
    ]

    @pl.when(t == 0)
    def _():
        for x in loads:
            x.start()
        greet(place.me, shards, rep, reps)
        loads[0].wait()
        u1.z2_start()
        u2.z1_start()
        loads[1].wait()
        u4.side_start()
        uo.near_start()
        loads[2].wait()
        transpose_rows(h1, h1t)
        dh1[...] = jnp.zeros_like(dh1)
        late[...] = jnp.zeros_like(late)

    heads = Heads(few, q, k, v, do, o, lse, dqt, dkv)
    blocks = length // heads.step

    plan = [
        (2, uo.near_sum),
        (5, u1.z2z3), (5, u2.z1z2), (5, u3.z1_start), (5, u4.side_sum), (7, uo.side_sum),
        (9, u4.last_add), (10, u1.z3_done), (10, u2.z2z3), (10, u3.z1z2), (10, u4.z1_start),
        (11, uo.last_sum), (13, uo.z1z2), (15, u2.z3_done), (15, u3.z2z3), (15, u4.z1z2), (16, uo.z2z3),
        (18, uo.z3_done), (19, u3.z3_done), (19, u4.z2z3),
    ]
    chain = ("near_sum", "side_sum", "last_sum", "z1z2", "z2z3")
    rest = [[] for _ in range(5)]
    for n in range(5):
        for when, name in zip((2, 5, 7, 9, 11), chain):
            slot_at = 4 * (n + 1) + when
            if slot_at < 20:
                plan.append((slot_at, getattr(parts[n], name)))
            else:
                rest[n].append(getattr(parts[n], name))
    plan.sort(key=lambda entry: entry[0])

    def body(i, _):
        for at, step in plan:
            pl.when(t * blocks + i == at)(step)
        heads.keys(i)
        return 0

    lax.fori_loop(0, blocks, body, 0)
    dq, gq, gk, gv = group_weights(few, dqt, dkv, h1t, late, cols)
    for n, part in enumerate((gq, gk, gv)):
        for s in range(shards):
            gg[t, s % 2, s // 2, n * share : (n + 1) * share, :] = part[s * share : (s + 1) * share, :]
    for s in range(shards):
        gg[t, s % 2, s // 2, 3 * share :, :] = jnp.zeros((GROUP_ROWS - 3 * share, LANES), BF16)
    for n in range(5):
        pl.when(t == n)(parts[n].near_start)
    group_inputs(few, dq, dkv, wq, wk, wv, dh1)

    def step(n):
        if rest[n]:
            rest[n].pop(0)()

    @pl.when(t == groups - 1)
    def _():
        step(4)
        step(3)
        step(2)
        step(1)
        back_finish(few, dh1, xp, vec, g1, late, gtp)
        vectors = per_shard(jnp.concatenate([late[...], jnp.zeros_like(late)], axis=0).astype(BF16), shards, share)
        for s in range(shards):
            sg[s % 2, s // 2, :16, :] = vectors[s]
            sg[s % 2, s // 2, 16:, :] = jnp.zeros((SMALL_ROWS - 16, LANES), BF16)
        us.near_start()
        step(4)
        step(3)
        step(2)
        step(1)
        us.near_sum()
        unpermute(slot[0:1, :], gtp, gtok)
        step(4)
        step(3)
        step(2)
        us.side_sum()
        u4.z3_done()
        for n in range(CHUNKS):
            src = ffin.at[n - 1] if n else own.at[0]
            for b in range(shards):
                gup_out[:, b * width + n * LANES : b * width + (n + 1) * LANES] = src[
                    b * share : (b + 1) * share, :
                ].astype(F32)
            gdn_out[n * LANES : (n + 1) * LANES, :] = jnp.transpose(src[width:, :].astype(F32))
        step(4)
        step(3)
        us.last_sum()
        for b in range(CHUNKS):
            gout_out[:, b * LANES : (b + 1) * LANES] = ofin[b * share : (b + 1) * share, :].astype(F32)
        vec_out[0:16, :] = ofin[CHUNKS * share : CHUNKS * share + 16, :].astype(F32)
        step(3)
        us.z1z2()
        step(4)
        us.z2z3()
        for n in range(5):
            assert not rest[n]
            parts[n].z3_done()
            for m in range(3):
                gqkv_out[:, m * width + n * LANES : m * width + (n + 1) * LANES] = gfin[
                    n, m * share : (m + 1) * share, :
                ].astype(F32)
            parts[n].a.wait_send()
        us.z3_done()
        vec_out[16:32, :] = sfin[0:16, :].astype(F32)
        uo.a.wait_send()
        us.a.wait_send()


SMALL_ROWS = 32


def back_reduce(few, shards, reps, qkv, do, o, lse, h1, xp, vecs, wqkv, g1, slot, state, plane, gout):
    length, width = h1.shape
    share = width // shards
    chips = shards // 2
    rows = 2 * width
    groups = width // LANES
    hidden = shards * width
    sds = jax.ShapeDtypeStruct
    whole, cols, in_specs, scratch = back_specs(few, length, width)
    hbm = pl.BlockSpec(memory_space=pl.ANY)
    dma = pltpu.SemaphoreType.DMA
    vm = lambda *shape: pltpu.VMEM(shape + (LANES,), BF16)
    spare = gout.shape[2]

    def buffers(rows):
        return [vm(4, rows // 2), vm(2, rows // 2), vm(2, rows), vm(rows)]

    many = lambda n, refs: [pltpu.VMEM((n,) + r.shape, BF16) for r in refs]
    fside, flast, fdepth, ffin = buffers(rows)
    return pl.pallas_call(
        functools.partial(back_reduce_kernel, few, shards, reps),
        grid=(groups,),
        in_specs=in_specs + [hbm, hbm, hbm],
        out_specs=[
            whole(length, width), whole(share, hidden), whole(width, width), whole(share, 3 * width),
            whole(share, width), whole(32, LANES),
        ],
        out_shape=(
            sds((length, width), BF16),
            sds((share, hidden), F32),
            sds((width, width), F32),
            sds((share, 3 * width), F32),
            sds((share, width), F32),
            sds((32, LANES), F32),
        ),
        scratch_shapes=scratch
        + [
            pltpu.VMEM((8, width), F32),
            vm(4, rows), vm(chips, rows), fside, flast,
        ]
        + many(4, [fdepth, ffin])
        + [vm(chips, spare), vm(chips, spare)] + buffers(spare)
        + [vm(5, 2, chips, GROUP_ROWS), vm(5, chips, GROUP_ROWS)] + many(5, buffers(GROUP_ROWS))
        + [vm(2, chips, SMALL_ROWS), vm(chips, SMALL_ROWS)] + buffers(SMALL_ROWS)
        + [dma((11, Unit.COPIES)), dma((11, Unit.COPIES)), dma((3,))],
        compiler_params=pltpu.CompilerParams(
            vmem_limit_bytes=60 * MB, collective_id=4, has_side_effects=True
        ),
        name="back_reduce",
    )(qkv, qkv, qkv, do, o, lse, h1, xp, vecs, wqkv, wqkv, wqkv, g1, slot, state, plane, gout)


def local(
    reps, shards,
    tokens, masked, cotangent, norm1_gain, norm1_shift, w_qkv, bias_query, bias_value, w_out,
    bias_out, norm2_gain, norm2_shift, w_up, bias_up, w_down, bias_down,
):
    seqs, length, width = tokens.shape
    hidden = w_up.shape[1]
    share = w_qkv.shape[0]
    close = shards == 8 and reps == 4 and share % 16 == 0 and share <= LANES and w_down.shape[0] == width
    x = tokens.reshape(seqs * length, width)
    cot = cotangent.reshape(seqs * length, width)
    mask = masked.astype(F32)
    if close:
        pack = jnp.concatenate(
            [
                jnp.pad(
                    jnp.stack(
                        [norm1_gain, norm1_shift, bias_query, bias_value, bias_out, norm2_gain, norm2_shift, bias_down]
                    ),
                    ((0, 0), (0, LANES - share)),
                ),
                jnp.pad(bias_up.reshape(-1, LANES), ((0, 3), (0, 0))),
            ]
        )
        slot, xp, h1, qkv, o, lse, x1, vecs, bup, over, wqkv, wout, wup, wdn = gather_attn(
            reps, shards, x, mask, pack, w_qkv, w_out, w_up, w_down
        )
        small_enough = over[0, 0] < 0.5
    else:
        small_enough = lax.pmax(jnp.sum(masked), ("rep", "fsdp")) <= FEW
        packed = jnp.stack(
            [norm1_gain, norm1_shift, bias_query, bias_value, bias_out, norm2_gain, norm2_shift, bias_down]
        )
        vecs = lax.all_gather(packed, "fsdp", axis=1, tiled=True).astype(F32)
        bup = lax.all_gather(bias_up, "fsdp", axis=0, tiled=True).astype(F32).reshape(1, hidden)
        gather = lambda w: lax.all_gather(w, "fsdp", axis=0, tiled=True)
        wqkv, wout, wup, wdn = gather(w_qkv), gather(w_out), gather(w_up), gather(w_down)
        slot, xp, h1, qkv, o, lse, x1 = attn_forward(x, mask, vecs, wqkv, wout)

    def backward(few):
        def run():
            res, gup, gdn, g1, do, gout, early = feed_forward(
                few, x1, cot, slot, mask, vecs, bup, wup, wdn, wout, o
            )
            if close:
                gtok, gup, gdn, gqkv, gout, early, late = reduce_backward(
                    few, shards, reps, 1,
                    qkv, do, o, lse, h1, xp, vecs, wqkv, g1, slot, early, gout, gup, gdn,
                )
                return res, gtok, gup, gdn, gqkv, gout, early, late
            gtok, gq, gk, gv, late = attn_backward(
                few, qkv, do, o, lse, h1, xp, vecs, wqkv, g1, slot
            )
            return res, gtok, gup, gdn, jnp.concatenate([gout, gq, gk, gv], axis=1), early, late

        return run

    me = lax.axis_index("fsdp")
    own = bias_up.shape[0]

    def pick(late, early):
        gbup = lax.dynamic_slice_in_dim(early[:8].reshape(hidden), me * own, own)
        return lax.dynamic_slice_in_dim(jnp.concatenate([late[:4], early[8:12]]), me * share, share, axis=1), gbup

    if close:
        res, g1, do, part, state, plane = ffn_reduce(
            FEW, shards, reps, x1, cot, slot, mask, vecs, bup, wup, wdn, wout, o
        )
        gtok, gup, gdn, gqkv, gout, small = back_reduce(
            FEW, shards, reps, qkv, do, o, lse, h1, xp, vecs, wqkv, g1, slot, state, plane, part
        )

        def redo():
            *outs, early, late = backward(length)()
            mine, gbup = pick(late, early)
            rows = jnp.concatenate([mine[4:], jnp.zeros((4, share), F32)])
            tail = jnp.concatenate([mine[:4], jnp.zeros((12, share), F32)])
            wide = lambda x: jnp.pad(x, ((0, 0), (0, LANES - share)))
            ups = jnp.pad(gbup.reshape(-1, LANES), ((0, 8 - own // LANES), (0, 0)))
            return (*outs, jnp.concatenate([wide(rows), ups, wide(tail)]))

        res, gtok, gup, gdn, gqkv, gout, small = lax.cond(
            small_enough, lambda: (res, gtok, gup, gdn, gqkv, gout, small), redo
        )
        mine = [small[n, :share] for n in (16, 17, 18, 19, 0, 1, 2, 3)]
        gbup = small[8 : 8 + own // LANES].reshape(own)
    else:
        def scatter(g, dim):
            part = lax.psum_scatter(g, "fsdp", scatter_dimension=dim, tiled=True)
            return lax.psum(part, "rep").astype(F32)

        res, gtok, gup, gdn, gattn, early, late = lax.cond(small_enough, backward(FEW), backward(length))
        gup = scatter(gup, 0)
        gdn = scatter(gdn.transpose(0, 2, 1).reshape(hidden, width), 0)
        gattn = scatter(gattn, 0)
        gout, gqkv = gattn[:, :width], gattn[:, width:]
        mine, gbup = pick(lax.psum(late, ("rep", "fsdp")), lax.psum(early, ("rep", "fsdp")))
    return (
        res.reshape(seqs, length, width),
        gtok.reshape(seqs, length, width),
        mine[0], mine[1], gqkv, mine[2], mine[3], gout, mine[4], mine[5], mine[6],
        gup, gbup, gdn, mine[7],
    )


def solution(mesh):
    rows3 = P(("rep", "fsdp"), None, None)
    vec = P("fsdp")
    mat = P("fsdp", None)
    in_specs = (
        rows3, P(("rep", "fsdp"), None), rows3,
        vec, vec, mat, vec, vec, mat, vec, vec, vec, mat, vec, mat, vec,
    )
    out_specs = (rows3, rows3, vec, vec, mat, vec, vec, mat, vec, vec, vec, mat, vec, mat, vec)
    body = functools.partial(local, mesh.shape["rep"], mesh.shape["fsdp"])
    return jax.shard_map(body, mesh=mesh, in_specs=in_specs, out_specs=out_specs, check_vma=False)
```

```python
import functools

import jax
import jax.numpy as jnp
from jax import lax
from jax.experimental import pallas as pl
from jax.experimental.pallas import tpu as pltpu
from jax.sharding import PartitionSpec as P

HEADS = 20
HEAD_DIM = 32
GROUP = 4
LANES = 128
SCALE = HEAD_DIM ** (-0.5)
LOG2E = 1.4426950408889634
FEW = 384
F32 = jnp.float32
BF16 = jnp.bfloat16
MB = 1024 * 1024

NN = (((1,), (0,)), ((), ()))
NT = (((1,), (1,)), ((), ()))


def dot(a, b, dims=NN):
    return lax.dot_general(a, b, dims, preferred_element_type=F32)


def norm_stats(x):
    mean = jnp.mean(x, axis=-1, keepdims=True)
    centred = x - mean
    variance = jnp.mean(centred * centred, axis=-1, keepdims=True)
    rstd = lax.rsqrt(variance + 1e-05)
    return centred * rstd, rstd


def norm_back(grad, xhat, rstd, gain):
    dxhat = grad * gain
    first = jnp.mean(dxhat, axis=-1, keepdims=True)
    second = jnp.mean(dxhat * xhat, axis=-1, keepdims=True)
    return rstd * (dxhat - first - xhat * second)


def cdf_parts(u):
    z = jnp.abs(u)
    t = pl.reciprocal(1.0 + 0.23164189 * z, approx=True)
    e = jnp.exp2(u * u * (-0.5 * LOG2E))
    poly = t * (
        0.127414796 + t * (-0.142248368 + t * (0.7107068705 + t * (-0.7265760135 + t * 0.5307027145)))
    )
    tail = poly * e
    return jnp.where(u < 0, tail, 1.0 - tail), e


def one_hot_rows(slot, start, size):
    length = slot.shape[1]
    rows = lax.broadcasted_iota(jnp.int32, (size, length), 0).astype(F32) + start
    return jnp.where(rows == slot, 1.0, 0.0)


def unpermute(slot, src_ref, out_ref):
    length = slot.shape[1]
    wide = jnp.transpose(jnp.broadcast_to(slot, (LANES, length)))
    step = 256
    for start in range(0, length, step):
        col = wide[start : start + step, :1]
        cols = lax.broadcasted_iota(jnp.int32, (step, length), 1).astype(F32)
        pick = jnp.where(cols == col, 1.0, 0.0).astype(BF16)
        out_ref[start : start + step, :] = dot(pick, src_ref[...]).astype(BF16)


def slots_of(mask_ref):
    length = mask_ref.shape[1]
    step = 256
    mask8 = jnp.broadcast_to(mask_ref[...], (8, length))
    cum = []
    for start in range(0, length, step):
        up = lax.broadcasted_iota(jnp.int32, (length, step), 0)
        to = lax.broadcasted_iota(jnp.int32, (length, step), 1) + start
        cum.append(dot(mask8.astype(BF16), jnp.where(up <= to, 1.0, 0.0).astype(BF16)))
    cum = jnp.concatenate(cum, axis=1)
    count = jnp.sum(mask8, axis=1, keepdims=True)
    pos = lax.broadcasted_iota(jnp.int32, (8, length), 1).astype(F32)
    return jnp.where(mask8 > 0.5, cum - 1.0, count + pos - cum), count


def permute_rows(tokens_ref, slot, xp_ref):
    step = 256

    def body(i, _):
        rows = pl.ds(pl.multiple_of(i * step, step), step)
        pick = one_hot_rows(slot[:1], (i * step).astype(F32), step).astype(BF16)
        xp_ref[rows, :] = dot(pick, tokens_ref[...]).astype(BF16)
        return 0

    lax.fori_loop(0, tokens_ref.shape[0] // step, body, 0)


def first_norm(xp_ref, vec_ref, h1_ref):
    step = 128
    gain = vec_ref[0:1, :]
    shift = vec_ref[1:2, :]

    def body(i, _):
        rows = pl.ds(pl.multiple_of(i * step, step), step)
        xhat, _ = norm_stats(xp_ref[rows, :].astype(F32))
        h1_ref[rows, :] = (xhat * gain + shift).astype(BF16)
        return 0

    lax.fori_loop(0, xp_ref.shape[0] // step, body, 0)


def project(h1_ref, vec_ref, wqkv_ref, qkv_ref):
    length, width = h1_ref.shape
    step = 256
    bq = vec_ref[2:3, :]
    bv = vec_ref[3:4, :]

    def body(i, _):
        rows = pl.ds(pl.multiple_of(i * step, step), step)
        h1 = h1_ref[rows, :]
        qkv_ref[rows, :width] = (dot(h1, wqkv_ref[:, :width]) + bq).astype(BF16)
        qkv_ref[rows, width : 2 * width] = dot(h1, wqkv_ref[:, width : 2 * width]).astype(BF16)
        qkv_ref[rows, 2 * width :] = (dot(h1, wqkv_ref[:, 2 * width :]) + bv).astype(BF16)
        return 0

    lax.fori_loop(0, length // step, body, 0)


def attend(qkv_ref, o_ref, lse_ref, beside, ahead):
    length, width = o_ref.shape
    step = 256
    c = SCALE * LOG2E
    lane = lax.broadcasted_iota(jnp.int32, (step, LANES), 1)

    def body(n, _):
        beside(n)
        t = n // (length // step)
        i = n % (length // step)
        pl.when(i == 0)(lambda: ahead(t))
        rows = pl.ds(pl.multiple_of(i * step, step), step)
        q = qkv_ref[rows, pl.ds(pl.multiple_of(t * LANES, LANES), LANES)]
        k = qkv_ref[:, pl.ds(pl.multiple_of(width + t * LANES, LANES), LANES)]
        v = qkv_ref[:, pl.ds(pl.multiple_of(2 * width + t * LANES, LANES), LANES)]
        vo = jnp.concatenate([v, jnp.ones_like(v)], axis=1)
        out = jnp.zeros((step, LANES), F32)
        lses = jnp.zeros((step, LANES), F32)
        for h in range(GROUP):
            mine = lane // HEAD_DIM == h
            s = dot(jnp.where(mine, q, jnp.zeros_like(q)), k, NT)
            top = jnp.max(s, axis=-1, keepdims=True)
            p = jnp.exp2((s - top) * c).astype(BF16)
            ov = dot(p, vo)
            total = ov[:, LANES:]
            out = jnp.where(mine, ov[:, :LANES] / total, out)
            lses = jnp.where(lane == h, top * c + jnp.log2(total), lses)
        o_ref[rows, pl.ds(pl.multiple_of(t * LANES, LANES), LANES)] = out.astype(BF16)
        lse_ref[pl.ds(pl.multiple_of(t * 8, 8), 8), rows] = jnp.transpose(lses)[:8, :]
        return 0

    lax.fori_loop(0, (width // LANES) * (length // step), body, 0)


def join(xp_ref, o_ref, wout_ref, vec_ref, x1_ref):
    step = 256
    bout = vec_ref[4:5, :]

    def body(i, _):
        rows = pl.ds(pl.multiple_of(i * step, step), step)
        x1_ref[rows, :] = xp_ref[rows, :].astype(F32) + dot(o_ref[rows, :], wout_ref[...]) + bout
        return 0

    lax.fori_loop(0, xp_ref.shape[0] // step, body, 0)


def attn_kernel(
    tokens_ref, mask_ref, vec_ref, wqkv_ref, wout_ref,
    slot_ref, xp_ref, h1_ref, qkv_ref, o_ref, lse_ref, x1_ref,
):
    slot, _ = slots_of(mask_ref)
    slot_ref[...] = slot
    permute_rows(tokens_ref, slot, xp_ref)
    first_norm(xp_ref, vec_ref, h1_ref)
    project(h1_ref, vec_ref, wqkv_ref, qkv_ref)
    attend(qkv_ref, o_ref, lse_ref, lambda n: None, lambda t: None)
    join(xp_ref, o_ref, wout_ref, vec_ref, x1_ref)


class Place:
    def __init__(self):
        self.me = me = lax.axis_index("fsdp")
        core = me % 2
        x = me // 2 % 2
        y = me // 4
        self.sib = me + 1 - 2 * core
        self.xn = me + 2 - 4 * x
        self.yn = me + 4 - 8 * y
        self.dg = me + 6 - 4 * x - 8 * y


def remote(src, dst, send, recv, to):
    return pltpu.make_async_remote_copy(
        src_ref=src, dst_ref=dst, send_sem=send, recv_sem=recv,
        device_id=to, device_id_type=pl.DeviceIdType.MESH,
    )


class Gather:
    def __init__(self, place, own, full, cut, send, recv, local, cols=slice(None)):
        rows = own.shape[0]
        own = own.at[:, cols]
        at = lambda s, lo=0, hi=rows: full.at[pl.ds(pl.multiple_of(s * rows + lo, 16), hi - lo), cols]
        me, sib, xn, yn, dg = place.me, place.sib, place.xn, place.yn, place.dg
        moves = [
            (own, at(me), sib), (own, at(me), xn), (own, at(me), yn),
            (at(xn), at(xn), sib), (at(yn), at(yn), sib),
            (at(xn, 0, cut), at(xn, 0, cut), yn), (at(yn, cut), at(yn, cut), xn),
            (at(dg, 0, cut), at(dg, 0, cut), sib), (at(dg, cut), at(dg, cut), sib),
        ]
        self.copies = [
            remote(src, dst, send.at[i], recv.at[i], {"fsdp": to}) for i, (src, dst, to) in enumerate(moves)
        ]
        self.local = pltpu.make_async_copy(own, at(me), local)

    def first(self):
        self.copies[1].start()
        self.copies[2].start()
        self.copies[0].start()
        self.local.start()

    def second(self):
        self.copies[1].wait_recv()
        self.copies[5].start()
        self.copies[3].start()
        self.copies[2].wait_recv()
        self.copies[6].start()
        self.copies[4].start()

    def third(self):
        self.copies[5].wait_recv()
        self.copies[7].start()
        self.copies[6].wait_recv()
        self.copies[8].start()

    def finish(self):
        for i in (0, 3, 4, 7, 8):
            self.copies[i].wait_recv()
        self.local.wait()
        for copy in self.copies:
            copy.wait_send()


class WideGather:
    COPIES = 14

    def __init__(self, place, rep, own, full, send, recv, local):
        rows, cols = own.shape
        dim, tile = (0, 16) if rows >= cols else (1, 128)
        size = own.shape[dim]
        base = 0
        third = size // tile // 3 * tile
        both = size - 2 * third
        wide = third + both
        even = rep % 2
        mult = lambda n: pl.multiple_of(n, tile)

        def cut(ref, s, lo, n):
            lo = base + lo
            if dim == 0:
                return ref.at[pl.ds(mult(s * rows + lo), n), :]
            return ref.at[pl.ds(pl.multiple_of(s * rows, 16), rows), pl.ds(mult(lo), n)]

        at = functools.partial(cut, full)
        w, mine, others = even * third, even * wide, (1 - even) * wide
        first = max(wide // 2 // tile * tile, third)
        second = wide - first
        assert second >= third
        me, sib, xn, yn, dg = place.me, place.sib, place.xn, place.yn, place.dg
        all_of = lambda s: at(s, 0, size)
        fsdp = lambda d: {"fsdp": d}
        pair = {"rep": rep + 1 - 2 * even}
        piece = cut(own, 0, w, wide)
        whole = cut(own, 0, 0, size)
        moves = [
            (whole, all_of(me), fsdp(sib)),
            (piece, at(me, w, wide), fsdp(xn)),
            (piece, at(me, w, wide), fsdp(yn)),
            (at(xn, w, first),) * 2 + (fsdp(yn),),
            (at(yn, w + first, second),) * 2 + (fsdp(xn),),
            (at(xn, mine, third),) * 2 + (pair,),
            (at(yn, mine, third),) * 2 + (pair,),
            (at(dg, mine, third),) * 2 + (pair,),
            (at(xn, w, wide),) * 2 + (fsdp(sib),),
            (at(yn, w, wide),) * 2 + (fsdp(sib),),
            (at(dg, w, wide),) * 2 + (fsdp(sib),),
            (at(xn, others, third),) * 2 + (fsdp(sib),),
            (at(yn, others, third),) * 2 + (fsdp(sib),),
            (at(dg, others, third),) * 2 + (fsdp(sib),),
        ]
        self.copies = [remote(src, dst, send.at[i], recv.at[i], to) for i, (src, dst, to) in enumerate(moves)]
        self.local = pltpu.make_async_copy(whole, all_of(me), local)

    def start(self, *which):
        for i in which:
            self.copies[i].start()

    def arrived(self, *which):
        for i in which:
            self.copies[i].wait_recv()

    def first(self):
        self.start(1, 2, 0)
        self.local.start()

    def second(self):
        self.arrived(1)
        self.start(3, 5, 8)
        self.arrived(2)
        self.start(4, 6, 9)

    def third(self):
        self.arrived(3, 4)
        self.start(7, 10)

    def fourth(self):
        self.arrived(5, 6)
        self.start(11, 12)

    def fifth(self):
        self.arrived(7)
        self.start(13)

    def finish(self):
        self.arrived(0, 8, 9, 10, 11, 12, 13)
        self.local.wait()
        for copy in self.copies:
            copy.wait_send()


def gather_attn_kernel(
    reps,
    tokens_ref, mask_ref, pack_ref, wqkv_in, wout_in, wup_in, wdn_in,
    slot_ref, xp_ref, h1_ref, qkv_ref, o_ref, lse_ref, x1_ref, vec_ref, bup_ref, over_ref,
    wqkv_ref, wout_ref, wup_ref, wdn_ref,
    packs, overs, wown, send, recv, local, psend, precv, rsend, rrecv,
):
    width = tokens_ref.shape[1]
    share = wqkv_in.shape[0]
    place = Place()
    me = place.me
    rep = lax.axis_index("rep")
    shards = packs.shape[0]
    barrier = pltpu.get_barrier_semaphore()
    for d in range(1, shards):
        pl.semaphore_signal(
            barrier, inc=1, device_id={"fsdp": (me + d) % shards}, device_id_type=pl.DeviceIdType.MESH
        )
    for d in range(1, reps):
        pl.semaphore_signal(
            barrier, inc=1, device_id={"rep": (rep + d) % reps}, device_id_type=pl.DeviceIdType.MESH
        )
    slot, count = slots_of(mask_ref)
    slot_ref[...] = slot
    row = lax.broadcasted_iota(jnp.int32, (16, LANES), 0)
    over = jnp.where(count[:1] > FEW, 1.0, 0.0)
    for n in range(3 * width // LANES):
        t, m = n // 3, n % 3
        wown[:, n * LANES : (n + 1) * LANES] = wqkv_in[:, m * width + t * LANES : m * width + (t + 1) * LANES]
    packs[me] = jnp.where(row == 13, over, pack_ref[...].astype(F32)).astype(BF16)
    pl.semaphore_wait(barrier, shards + reps - 2)

    sems = lambda n: (send.at[n], recv.at[n], local.at[n])
    early = 2 * 3 * LANES
    qkv = Gather(place, wown, wqkv_ref, 48, *sems(0), cols=slice(0, early))
    rest = Gather(place, wown, wqkv_ref, 32, *sems(1), cols=slice(early, 3 * width))
    out = Gather(place, wout_in, wout_ref, 48, *sems(2))
    up = WideGather(place, rep, wup_in, wup_ref, *sems(3))
    down = WideGather(place, rep, wdn_in, wdn_ref, *sems(4))
    qkv.first()
    vectors = []
    for d in range(1, shards):
        copy = remote(
            packs.at[me], packs.at[me], psend.at[d - 1], precv.at[d - 1], {"fsdp": (me + d) % shards}
        )
        copy.start()
        vectors.append(copy)
    permute_rows(tokens_ref, slot, xp_ref)
    qkv.second()
    rest.first()
    up.first()
    for copy in vectors:
        copy.wait_recv()
    all_over = packs[0]
    for s in range(1, shards):
        all_over = jnp.maximum(all_over, packs[s])
    overs[rep] = all_over
    flags = []
    for d in range(1, reps):
        copy = remote(overs.at[rep], overs.at[rep], rsend.at[d - 1], rrecv.at[d - 1], {"rep": (rep + d) % reps})
        copy.start()
        flags.append(copy)
    vecs = jnp.zeros((16, width), F32)
    for s in range(shards):
        pack = packs[s]
        lane = lax.broadcasted_iota(jnp.int32, (LANES, width), 0)
        col = lax.broadcasted_iota(jnp.int32, (LANES, width), 1) - s * share
        spot = jnp.where((lane == col) & (lane < share), 1.0, 0.0).astype(BF16)
        vecs = vecs + dot(pack, spot)
        wide = pack.astype(F32)
        for r in range(width // LANES):
            bup_ref[0:1, s * width + r * LANES : s * width + (r + 1) * LANES] = wide[8 + r : 9 + r, :]
    vec_ref[...] = vecs[:8]
    first_norm(xp_ref, vec_ref, h1_ref)
    qkv.third()
    qkv.finish()

    plan = (
        (3, rest.second), (4, down.first), (5, out.first), (6, up.second), (7, rest.third), (8, rest.finish),
        (9, out.second), (11, up.third), (12, up.fourth), (13, out.third), (13, down.second), (14, up.fifth),
        (18, down.third), (19, down.fourth),
    )

    def beside(n):
        for at, step in plan:
            pl.when(n == at)(step)

    def ahead(t):
        step = 512
        cols = pl.ds(pl.multiple_of(t * 3 * LANES, LANES), 3 * LANES)
        at = [pl.multiple_of(n * width + t * LANES, LANES) for n in range(3)]
        bq = vec_ref[2:3, pl.ds(at[0], LANES)]
        bv = vec_ref[3:4, pl.ds(at[0], LANES)]
        bias = jnp.concatenate([bq, jnp.zeros_like(bq), bv], axis=1)
        for start in range(0, h1_ref.shape[0], step):
            rows = slice(start, start + step)
            part = (dot(h1_ref[rows, :], wqkv_ref[:, cols]) + bias).astype(BF16)
            for n in range(3):
                qkv_ref[rows, pl.ds(at[n], LANES)] = part[:, n * LANES : (n + 1) * LANES]

    attend(qkv_ref, o_ref, lse_ref, beside, ahead)
    out.finish()
    join(xp_ref, o_ref, wout_ref, vec_ref, x1_ref)
    for copy in flags:
        copy.wait()
    for copy in vectors:
        copy.wait_send()
    worst = overs[0]
    for z in range(1, reps):
        worst = jnp.maximum(worst, overs[z])
    over_ref[...] = worst[13:14, :].astype(F32)
    down.fifth()
    up.finish()
    down.finish()


def gather_attn(reps, shards, tokens, mask, pack, w_qkv, w_out, w_up, w_down):
    length, width = tokens.shape
    hidden = w_up.shape[1]
    sds = jax.ShapeDtypeStruct
    groups = width // LANES
    vmem = pl.BlockSpec(memory_space=pltpu.VMEM)
    hbm = pl.BlockSpec(memory_space=pl.ANY)
    dma = pltpu.SemaphoreType.DMA
    return pl.pallas_call(
        functools.partial(gather_attn_kernel, reps),
        in_specs=[vmem] * 7,
        out_specs=[vmem] * 12 + [hbm] * 2,
        out_shape=(
            sds((8, length), F32),
            sds((length, width), BF16),
            sds((length, width), BF16),
            sds((length, 3 * width), BF16),
            sds((length, width), BF16),
            sds((8 * groups, length), F32),
            sds((length, width), F32),
            sds((8, width), F32),
            sds((1, hidden), F32),
            sds((1, LANES), F32),
            sds((width, 3 * width), BF16),
            sds((width, width), BF16),
            sds((width, hidden), BF16),
            sds((hidden, width), BF16),
        ),
        scratch_shapes=[
            pltpu.VMEM((shards, 16, LANES), BF16),
            pltpu.VMEM((reps, 16, LANES), BF16),
            pltpu.VMEM(w_qkv.shape, BF16),
            dma((5, WideGather.COPIES)), dma((5, WideGather.COPIES)), dma((5,)),
            dma((shards - 1,)), dma((shards - 1,)),
            dma((reps - 1,)), dma((reps - 1,)),
        ],
        compiler_params=pltpu.CompilerParams(
            vmem_limit_bytes=56 * MB, collective_id=0, has_side_effects=True
        ),
        name="gather_attn",
    )(tokens, mask, pack, w_qkv, w_out, w_up, w_down)


def attn_forward(tokens, mask, vecs, wqkv, wout):
    length, width = tokens.shape
    sds = jax.ShapeDtypeStruct
    groups = width // LANES
    return pl.pallas_call(
        attn_kernel,
        out_shape=(
            sds((8, length), F32),
            sds((length, width), BF16),
            sds((length, width), BF16),
            sds((length, 3 * width), BF16),
            sds((length, width), BF16),
            sds((8 * groups, length), F32),
            sds((length, width), F32),
        ),
        compiler_params=pltpu.CompilerParams(vmem_limit_bytes=56 * MB),
        name="attn_forward",
    )(tokens, mask, vecs, wqkv, wout)


def ffn_blocks(few, length):
    part = few if few <= 384 else 256
    blocks = [(start, part, True) for start in range(0, few, part)]
    start = few
    while start < length:
        size = min(320, length - start)
        blocks.append((start, size, False))
        start += size
    return blocks


def ffn_start(blocks, x1_ref, cot_ref, slot_ref, mask_ref, vec_ref, acc, h2, h2t, gy, gyt, dh2):
    gain = vec_ref[5:6, :]
    shift = vec_ref[6:7, :]
    bdown = vec_ref[7:8, :]
    for start, size, back in blocks:
        rows = slice(start, start + size)
        x1 = x1_ref[rows, :]
        xhat, _ = norm_stats(x1)
        hidden = (xhat * gain + shift).astype(BF16)
        h2[rows, :] = hidden
        acc[rows, :] = x1 + bdown
        if back:
            h2t[:, rows] = jnp.transpose(hidden)
            pick = one_hot_rows(slot_ref[0:1, :], float(start), size) * mask_ref[...]
            g = dot(pick.astype(BF16), cot_ref[...])
            gy[rows, :] = g.astype(BF16)
            gyt[:, rows] = jnp.transpose(g.astype(BF16))
            dh2[rows, :] = jnp.zeros_like(g)


def ffn_block(block, wup, wdn, bup, acc, h2, h2t, gy, gyt, dh2):
    start, size, back = block
    rows = slice(start, start + size)
    u = dot(h2[rows, :], wup) + bup
    cdf, e = cdf_parts(u)
    a = (u * cdf).astype(BF16)
    acc[rows, :] += dot(a, wdn)
    if not back:
        return None
    da = dot(gy[rows, :], wdn, NT)
    du = ((cdf + u * e * 0.3989422804014327) * da).astype(BF16)
    dh2[rows, :] += dot(du, wup, NT)
    return (
        dot(h2t[:, rows], du),
        dot(gyt[:, rows], a),
        jnp.sum(du.astype(F32), axis=0, keepdims=True),
    )


def ffn_end(blocks, x1_ref, slot_ref, vec_ref, wout_ref, o_ref, acc, gy, dh2, outp, res_ref, g1_ref, do_ref, small_ref):
    gain = vec_ref[5:6, :]
    ggain = gshift = gbdown = gbout = gout = None
    plus = lambda a, b: b if a is None else a + b
    for start, size, back in blocks:
        rows = slice(start, start + size)
        outp[rows, :] = acc[rows, :].astype(BF16)
        if back:
            xhat, rstd = norm_stats(x1_ref[rows, :])
            d = dh2[rows, :]
            g = gy[rows, :].astype(F32)
            g1 = g + norm_back(d, xhat, rstd, gain)
            g1_ref[rows, :] = g1
            g1b = g1.astype(BF16)
            do_ref[rows, :] = dot(g1b, wout_ref[...], NT).astype(BF16)
            gout = plus(gout, dot(jnp.transpose(o_ref[rows, :]), g1b))
            ggain = plus(ggain, jnp.sum(d * xhat, axis=0, keepdims=True))
            gshift = plus(gshift, jnp.sum(d, axis=0, keepdims=True))
            gbdown = plus(gbdown, jnp.sum(g, axis=0, keepdims=True))
            gbout = plus(gbout, jnp.sum(g1b.astype(F32), axis=0, keepdims=True))
    small_ref[8:9, :] = gbout
    small_ref[9:10, :] = ggain
    small_ref[10:11, :] = gshift
    small_ref[11:12, :] = gbdown
    small_ref[12:16, :] = jnp.zeros((4, outp.shape[1]), F32)
    unpermute(slot_ref[0:1, :], outp, res_ref)
    return gout


def ffn_kernel(
    few,
    x1_ref, cot_ref, slot_ref, mask_ref, vec_ref, bup_ref, wup_ref, wdn_ref, wout_ref, o_ref,
    res_ref, gup_ref, gdn_ref, g1_ref, do_ref, gout_ref, small_ref,
    acc, h2, h2t, gy, gyt, dh2, outp,
):
    j = pl.program_id(0)
    length, width = x1_ref.shape
    blocks = ffn_blocks(few, length)

    @pl.when(j == 0)
    def _():
        ffn_start(blocks, x1_ref, cot_ref, slot_ref, mask_ref, vec_ref, acc, h2, h2t, gy, gyt, dh2)

    total = None
    for block in blocks:
        part = ffn_block(block, wup_ref[...], wdn_ref[...], bup_ref[...], acc, h2, h2t, gy, gyt, dh2)
        if part is not None:
            total = part if total is None else [x + y for x, y in zip(total, part)]
    gup, gdn, gbup = total
    gup_ref[...] = gup.astype(BF16)
    for n in range(gdn_ref.shape[0]):
        cols = slice(n * width, (n + 1) * width)
        gdn_ref[n] = gdn[:, cols].astype(BF16)
        small_ref[pl.ds(j * gdn_ref.shape[0] + n, 1), :] = gbup[:, cols]

    @pl.when(j == pl.num_programs(0) - 1)
    def _():
        gout = ffn_end(
            blocks, x1_ref, slot_ref, vec_ref, wout_ref, o_ref, acc, gy, dh2, outp, res_ref, g1_ref, do_ref, small_ref
        )
        gout_ref[...] = gout.astype(BF16)


def feed_forward(few, x1, cot, slot, mask, vecs, bup, wup, wdn, wout, o):
    length, width = x1.shape
    hidden = wup.shape[1]
    fc = 2 * width
    sds = jax.ShapeDtypeStruct
    whole = lambda *shape: pl.BlockSpec(shape, lambda j: (0,) * len(shape))
    return pl.pallas_call(
        functools.partial(ffn_kernel, few),
        grid=(hidden // fc,),
        in_specs=[
            whole(length, width),
            whole(length, width),
            whole(8, length),
            whole(1, length),
            whole(8, width),
            pl.BlockSpec((1, fc), lambda j: (0, j)),
            pl.BlockSpec((width, fc), lambda j: (0, j)),
            pl.BlockSpec((fc, width), lambda j: (j, 0)),
            whole(width, width),
            whole(few, width),
        ],
        out_specs=[
            whole(length, width),
            pl.BlockSpec((width, fc), lambda j: (0, j)),
            pl.BlockSpec((2, width, width), lambda j: (j, 0, 0)),
            whole(few, width),
            whole(few, width),
            whole(width, width),
            whole(16, width),
        ],
        out_shape=(
            sds((length, width), BF16),
            sds((width, hidden), BF16),
            sds((hidden // width, width, width), BF16),
            sds((few, width), F32),
            sds((few, width), BF16),
            sds((width, width), BF16),
            sds((16, width), F32),
        ),
        scratch_shapes=[
            pltpu.VMEM((length, width), F32),
            pltpu.VMEM((length, width), BF16),
            pltpu.VMEM((width, few), BF16),
            pltpu.VMEM((few, width), BF16),
            pltpu.VMEM((width, few), BF16),
            pltpu.VMEM((few, width), F32),
            pltpu.VMEM((length, width), BF16),
        ],
        compiler_params=pltpu.CompilerParams(vmem_limit_bytes=56 * MB),
        name="feed_forward",
    )(x1, cot, slot, mask, vecs, bup, wup, wdn, wout, o)


class Heads:
    step = 256

    def __init__(self, few, q_ref, k_ref, v_ref, do_ref, o_ref, lse_ref, dqt, dkv):
        self.k_ref, self.v_ref, self.lse_ref, self.dqt, self.dkv = k_ref, v_ref, lse_ref, dqt, dkv
        q = q_ref[...]
        do = do_ref[...]
        lane = lax.broadcasted_iota(jnp.int32, (few, LANES), 1)
        head = lax.broadcasted_iota(jnp.int32, (8, LANES), 0)
        lane8 = lax.broadcasted_iota(jnp.int32, (8, LANES), 1)
        pick = jnp.where(lane8 // HEAD_DIM == head, 1.0, 0.0)
        self.delta = lax.dot_general(
            pick, do.astype(F32) * o_ref[...].astype(F32), NT,
            precision=lax.Precision.HIGHEST, preferred_element_type=F32,
        )
        dqt[...] = jnp.zeros_like(dqt)
        zero = jnp.zeros_like(q)
        self.qs = [jnp.where(lane // HEAD_DIM == h, q, zero) for h in range(GROUP)]
        self.dos = [jnp.where(lane // HEAD_DIM == h, do, zero) for h in range(GROUP)]

    def keys(self, i):
        step = self.step
        rows = pl.ds(pl.multiple_of(i * step, step), step)
        k = self.k_ref[rows, :]
        v = self.v_ref[rows, :]
        kt = jnp.transpose(k)
        dk = jnp.zeros((step, LANES), F32)
        dv = jnp.zeros((step, LANES), F32)
        for h in range(GROUP):
            s = dot(k, self.qs[h], NT)
            p = jnp.exp2(s * (SCALE * LOG2E) - self.lse_ref[h : h + 1, :])
            dp = dot(v, self.dos[h], NT)
            ds = (p * (dp - self.delta[h : h + 1, :])).astype(BF16)
            dv = dv + dot(p.astype(BF16), self.dos[h])
            dk = dk + dot(ds, self.qs[h])
            part = slice(h * HEAD_DIM, (h + 1) * HEAD_DIM)
            self.dqt[part, :] += dot(kt[part, :], ds)
        self.dkv[rows, :LANES] = (dk * SCALE).astype(BF16)
        self.dkv[rows, LANES:] = dv.astype(BF16)


def transpose_rows(src_ref, out_ref):
    step = 256
    for start in range(0, src_ref.shape[0], step):
        out_ref[:, start : start + step] = jnp.transpose(src_ref[start : start + step, :])


def group_weights(few, dqt, dkv, h1t, small_ref, cols):
    dq = (jnp.transpose(dqt[...]) * SCALE).astype(BF16)
    gq = dot(h1t[:, :few], dq).astype(BF16)
    gkv = dot(h1t[...], dkv[...]).astype(BF16)
    small_ref[2:3, cols] = jnp.sum(dq.astype(F32), axis=0, keepdims=True)
    small_ref[3:4, cols] = jnp.sum(dkv[:, LANES:].astype(F32), axis=0, keepdims=True)
    return dq, gq, gkv[:, :LANES], gkv[:, LANES:]


def group_inputs(few, dq, dkv, wq_ref, wk_ref, wv_ref, dh1):
    step = 256
    wkv = jnp.concatenate([wk_ref[...], wv_ref[...]], axis=1)
    for start in range(0, dh1.shape[0], step):
        rows = slice(start, start + step)
        dh1[rows, :] += dot(dkv[rows, :], wkv, NT)
    dh1[:few, :] += dot(dq, wq_ref[...], NT)


def back_finish(few, dh1_ref, xp_ref, vec_ref, g1_ref, small_ref, gtp):
    length, width = xp_ref.shape
    gain = vec_ref[0:1, :]
    step = 128
    ggain = gshift = jnp.zeros((1, width), F32)
    for start in range(0, length, step):
        rows = slice(start, start + step)
        xhat, rstd = norm_stats(xp_ref[rows, :].astype(F32))
        d = dh1_ref[rows, :]
        g = norm_back(d, xhat, rstd, gain)
        if start < few:
            g = g + g1_ref[rows, :]
        gtp[rows, :] = g.astype(BF16)
        ggain = ggain + jnp.sum(d * xhat, axis=0, keepdims=True)
        gshift = gshift + jnp.sum(d, axis=0, keepdims=True)
    small_ref[0:1, :] = ggain
    small_ref[1:2, :] = gshift


def back_kernel(
    few,
    q, k, v, do, o, lse, h1, xp, vec, wq, wk, wv, g1, slot,
    gtok, gq_ref, gk_ref, gv_ref, small,
    h1t, dh1, dqt, dkv, gtp,
):
    t = pl.program_id(0)
    cols = pl.ds(pl.multiple_of(t * LANES, LANES), LANES)

    @pl.when(t == 0)
    def _():
        transpose_rows(h1, h1t)
        dh1[...] = jnp.zeros_like(dh1)
        small[...] = jnp.zeros_like(small)

    heads = Heads(few, q, k, v, do, o, lse, dqt, dkv)

    def body(i, _):
        heads.keys(i)
        return 0

    lax.fori_loop(0, h1.shape[0] // heads.step, body, 0)
    dq, gq, gk, gv = group_weights(few, dqt, dkv, h1t, small, cols)
    gq_ref[...] = gq
    gk_ref[...] = gk
    gv_ref[...] = gv
    group_inputs(few, dq, dkv, wq, wk, wv, dh1)

    @pl.when(t == pl.num_programs(0) - 1)
    def _():
        back_finish(few, dh1, xp, vec, g1, small, gtp)
        unpermute(slot[0:1, :], gtp, gtok)


def back_specs(few, length, width, grouped=False):
    groups = width // LANES
    whole = lambda *shape: pl.BlockSpec(shape, lambda t: (0,) * len(shape))
    cols = lambda rows, first: pl.BlockSpec((rows, LANES), lambda t: (0, first + t))
    in_specs = [
        cols(few, 0),
        cols(length, groups),
        cols(length, 2 * groups),
        cols(few, 0),
        cols(few, 0),
        pl.BlockSpec((8, few), lambda t: (t, 0)),
        whole(length, width),
        whole(length, width),
        whole(8, width),
    ]
    if grouped:
        in_specs += [pl.BlockSpec((width, LANES), lambda t, n=n: (0, 3 * t + n)) for n in range(3)]
    else:
        in_specs += [cols(width, n * groups) for n in range(3)]
    in_specs += [
        whole(few, width),
        whole(8, length),
    ]
    scratch = [
        pltpu.VMEM((width, length), BF16),
        pltpu.VMEM((length, width), F32),
        pltpu.VMEM((LANES, few), F32),
        pltpu.VMEM((length, 2 * LANES), BF16),
        pltpu.VMEM((length, width), BF16),
    ]
    return whole, cols, in_specs, scratch


def attn_backward(few, qkv, do, o, lse, h1, xp, vecs, wqkv, g1, slot):
    length, width = h1.shape
    sds = jax.ShapeDtypeStruct
    whole, cols, in_specs, scratch = back_specs(few, length, width)
    return pl.pallas_call(
        functools.partial(back_kernel, few),
        grid=(width // LANES,),
        in_specs=in_specs,
        out_specs=[whole(length, width), cols(width, 0), cols(width, 0), cols(width, 0), whole(8, width)],
        out_shape=(
            sds((length, width), BF16),
            sds((width, width), BF16),
            sds((width, width), BF16),
            sds((width, width), BF16),
            sds((8, width), F32),
        ),
        scratch_shapes=scratch,
        compiler_params=pltpu.CompilerParams(vmem_limit_bytes=56 * MB),
        name="attn_backward",
    )(qkv, qkv, qkv, do, o, lse, h1, xp, vecs, wqkv, wqkv, wqkv, g1, slot)


class Reduce:
    def __init__(self, place, rep, reps, mine, other, acc, near, side, last, depth, fin, sems):
        send, recv, local = sems
        self.rep, self.reps = rep, reps
        self.acc, self.near, self.side, self.last, self.depth, self.fin = acc, near, side, last, depth, fin
        chip = place.me // 2
        cx, cy, cd = place.xn // 2, place.yn // 2, place.dg // 2
        self.chip, self.cx, self.cy = chip, cx, cy
        fsdp = lambda d: {"fsdp": d}
        low, high = slice(0, 2), slice(2, 4)
        n = iter(range(100))
        def copy(src, dst, to):
            i = next(n)
            return remote(src, dst, send.at[i], recv.at[i], to)
        self.a = [copy(other[q], near.at[:, q], fsdp(place.sib)) for q in range(4)]
        self.own = [pltpu.make_async_copy(mine[q], acc.at[:, q], local.at[q]) for q in range(4)]
        self.b = [
            copy(acc.at[cx, low], side.at[0], fsdp(place.xn)),
            copy(acc.at[cy, high], side.at[2], fsdp(place.yn)),
            copy(acc.at[cd, low], side.at[1], fsdp(place.xn)),
            copy(acc.at[cd, high], side.at[3], fsdp(place.yn)),
        ]
        self.c = [
            copy(acc.at[cy, low], last.at[0], fsdp(place.yn)),
            copy(acc.at[cx, high], last.at[1], fsdp(place.xn)),
        ]
        peers = [(rep + d) % reps for d in range(1, reps)]
        self.d = [copy(acc.at[chip, z], depth.at[i], {"rep": z}) for i, z in enumerate(peers)]
        self.e = [copy(fin.at[rep], fin.at[rep], {"rep": z}) for z in peers]

    COPIES = 16

    def start(self):
        for x in self.a + self.own:
            x.start()

    def near_sum(self):
        for q in range(4):
            self.own[q].wait()
            self.a[q].wait_recv()
            for c in range(4):
                self.acc[c, q] = (self.acc[c, q].astype(F32) + self.near[c, q].astype(F32)).astype(BF16)
        for x in self.b:
            x.start()

    def add(self, c, half, part):
        for q in range(2):
            self.acc[c, half + q] = (self.acc[c, half + q].astype(F32) + part[q].astype(F32)).astype(BF16)

    def side_sum(self):
        for x in self.b:
            x.wait()
        self.add(self.cy, 0, self.side.at[1])
        self.c[0].start()
        self.add(self.cx, 2, self.side.at[3])
        self.c[1].start()
        self.add(self.chip, 0, self.side.at[0])
        self.add(self.chip, 2, self.side.at[2])

    def last_sum(self):
        for x in self.c:
            x.wait()
        self.add(self.chip, 0, self.last.at[0])
        self.add(self.chip, 2, self.last.at[1])
        for x in self.d:
            x.start()

    def depth_sum(self):
        total = self.acc[self.chip, self.rep].astype(F32)
        for i in range(self.reps - 1):
            self.d[i].wait()
            total = total + self.depth[i].astype(F32)
        self.fin[self.rep] = total.astype(BF16)
        for x in self.e:
            x.start()

    def finish(self):
        for x in self.e:
            x.wait()
        for x in self.a:
            x.wait_send()


class Small:
    def __init__(self, me, shards, rep, reps, rows, beside, depth, out, sems):
        psend, precv, rsend, rrecv = sems
        self.me, self.rep, self.rows, self.near, self.depth, self.out = me, rep, rows, beside, depth, out
        self.first = [
            remote(beside.at[me], beside.at[me], psend.at[d - 1], precv.at[d - 1], {"fsdp": (me + d) % shards})
            for d in range(1, shards)
        ]
        self.second = [
            remote(depth.at[rep], depth.at[rep], rsend.at[d - 1], rrecv.at[d - 1], {"rep": (rep + d) % reps})
            for d in range(1, reps)
        ]

    def start(self):
        self.near[self.me] = self.rows[...]
        for x in self.first:
            x.start()

    def middle(self):
        for x in self.first:
            x.wait()
        total = self.near[0]
        for s in range(1, self.near.shape[0]):
            total = total + self.near[s]
        self.depth[self.rep] = total
        for x in self.second:
            x.start()

    def finish(self):
        for x in self.second:
            x.wait()
        total = self.depth[0]
        for z in range(1, self.depth.shape[0]):
            total = total + self.depth[z]
        self.out[...] = total


def reduce_back_kernel(
    few, shards, reps,
    q, k, v, do, o, lse, h1, xp, vec, wq, wk, wv, g1, slot, early_ref, gout_ref, gup_ref, gdn_ref,
    gtok, gup_out, gdn_out, gqkv_out, gout_out, early_out, late_out,
    h1t, dh1, dqt, dkv, gtp, late, gqkv, fin, acc, near, side, last, depth, send, recv, local,
    enear, edepth, lnear, ldepth, es1, er1, es2, er2, ls1, lr1, ls2, lr2,
):
    t = pl.program_id(0)
    cols = pl.ds(pl.multiple_of(t * LANES, LANES), LANES)
    share = h1.shape[1] // shards
    width = h1.shape[1]
    place = Place()
    rep = lax.axis_index("rep")
    core = place.me % 2

    def quarter(n, side):
        u = n // 4
        if u < 2:
            return gup_ref.at[:, side, :, n * width : (n + 1) * width]
        if u < 4:
            return gdn_ref.at[:, side, (n - 8) * share : (n - 7) * share, :]
        return gout_ref.at[:, side] if n == 16 else gqkv.at[n - 17, :, side]

    units = []
    for u in range(5):
        sems = (send.at[u], recv.at[u], local.at[u])
        units.append(
            Reduce(
                place, rep, reps,
                [quarter(4 * u + n, core) for n in range(4)],
                [quarter(4 * u + n, 1 - core) for n in range(4)],
                acc.at[u], near.at[u], side.at[u], last.at[u], depth.at[u], fin.at[u], sems,
            )
        )
    early = Small(place.me, shards, rep, reps, early_ref, enear, edepth, early_out, (es1, er1, es2, er2))
    later = Small(place.me, shards, rep, reps, late, lnear, ldepth, late_out, (ls1, lr1, ls2, lr2))

    @pl.when(t == 0)
    def _():
        barrier = pltpu.get_barrier_semaphore()
        for d in range(1, shards):
            pl.semaphore_signal(
                barrier, inc=1, device_id={"fsdp": (place.me + d) % shards},
                device_id_type=pl.DeviceIdType.MESH,
            )
        for d in range(1, reps):
            pl.semaphore_signal(
                barrier, inc=1, device_id={"rep": (rep + d) % reps}, device_id_type=pl.DeviceIdType.MESH
            )
        pl.semaphore_wait(barrier, shards + reps - 2)
        for u in range(4):
            units[u].start()
        early.start()
        transpose_rows(h1, h1t)
        dh1[...] = jnp.zeros_like(dh1)
        late[...] = jnp.zeros_like(late)

    heads = Heads(few, q, k, v, do, o, lse, dqt, dkv)
    blocks = h1.shape[0] // heads.step

    plan = [
        (1, units[0].near_sum), (2, units[1].near_sum), (3, units[2].near_sum), (4, units[3].near_sum),
        (5, early.middle), (6, units[0].side_sum), (9, units[1].side_sum), (10, units[0].last_sum),
        (11, early.finish), (13, units[2].side_sum), (14, units[1].last_sum), (15, units[0].depth_sum),
        (17, units[3].side_sum), (18, units[2].last_sum), (19, units[1].depth_sum),
    ]

    def body(i, _):
        for at, step in plan:
            pl.when(t * blocks + i == at)(step)
        heads.keys(i)
        return 0

    lax.fori_loop(0, blocks, body, 0)
    dq, gq, gk, gv = group_weights(few, dqt, dkv, h1t, late, cols)
    chips = shards // 2
    for n, g in enumerate((gq, gk, gv)):
        gqkv[n, :, :, :, cols] = g.reshape(chips, 2, share, LANES)
    final = t == pl.num_programs(0) - 1
    pl.when(final)(units[4].start)
    group_inputs(few, dq, dkv, wq, wk, wv, dh1)

    @pl.when(final)
    def _():
        units[4].near_sum()
        units[3].last_sum()
        units[2].depth_sum()
        back_finish(few, dh1, xp, vec, g1, late, gtp)
        later.start()
        units[4].side_sum()
        units[3].depth_sum()
        units[4].last_sum()
        later.middle()
        unpermute(slot[0:1, :], gtp, gtok)
        units[4].depth_sum()
        for n in range(16):
            if n % 4 == 0:
                units[n // 4].finish()
            part = fin[n // 4, n % 4].astype(F32)
            if n < 8:
                gup_out[:, n * width : (n + 1) * width] = part
            else:
                gdn_out[:, (n - 8) * share : (n - 7) * share] = jnp.transpose(part)
        later.finish()
        units[4].finish()
        gout_out[...] = fin[4, 0].astype(F32)
        for n in range(3):
            gqkv_out[:, n * width : (n + 1) * width] = fin[4, 1 + n].astype(F32)


def reduce_backward(few, shards, reps, ident, qkv, do, o, lse, h1, xp, vecs, wqkv, g1, slot, early, gout, gup, gdn):
    length, width = h1.shape
    share = width // shards
    chips = shards // 2
    sds = jax.ShapeDtypeStruct
    whole, cols, in_specs, scratch = back_specs(few, length, width, True)
    hbm = pl.BlockSpec(memory_space=pl.ANY)
    dma = pltpu.SemaphoreType.DMA
    block = (share, width)
    copies = Reduce.COPIES
    hidden = gup.shape[1]
    return pl.pallas_call(
        functools.partial(reduce_back_kernel, few, shards, reps),
        grid=(width // LANES,),
        in_specs=in_specs + [whole(16, width), hbm, hbm, hbm],
        out_specs=[
            whole(length, width), whole(share, hidden), whole(width, width), whole(share, 3 * width),
            whole(share, width), whole(16, width), whole(8, width),
        ],
        out_shape=(
            sds((length, width), BF16),
            sds((share, hidden), F32),
            sds((width, width), F32),
            sds((share, 3 * width), F32),
            sds((share, width), F32),
            sds((16, width), F32),
            sds((8, width), F32),
        ),
        scratch_shapes=scratch
        + [
            pltpu.VMEM((8, width), F32),
            pltpu.VMEM((3, chips, 2) + block, BF16),
            pltpu.VMEM((5, 4) + block, BF16),
            pltpu.VMEM((5, chips, 4) + block, BF16),
            pltpu.VMEM((5, chips, 4) + block, BF16),
            pltpu.VMEM((5, 4, 2) + block, BF16),
            pltpu.VMEM((5, 2, 2) + block, BF16),
            pltpu.VMEM((5, reps - 1) + block, BF16),
            dma((5, copies)), dma((5, copies)), dma((5, 4)),
            pltpu.VMEM((shards, 16, width), F32),
            pltpu.VMEM((reps, 16, width), F32),
            pltpu.VMEM((shards, 8, width), F32),
            pltpu.VMEM((reps, 8, width), F32),
            dma((shards - 1,)), dma((shards - 1,)), dma((reps - 1,)), dma((reps - 1,)),
            dma((shards - 1,)), dma((shards - 1,)), dma((reps - 1,)), dma((reps - 1,)),
        ],
        compiler_params=pltpu.CompilerParams(
            vmem_limit_bytes=60 * MB, collective_id=ident, has_side_effects=True
        ),
        name="reduce_backward",
    )(
        qkv, qkv, qkv, do, o, lse, h1, xp, vecs, wqkv, wqkv, wqkv, g1, slot, early,
        gout.reshape(chips, 2, share, width),
        gup.reshape(chips, 2, share, hidden),
        gdn.reshape(chips, 2, width, width),
    )


class Unit:
    COPIES = 10

    def __init__(self, place, rep, other, acc, near, side, last, own, depth, fin, send, recv):
        self.acc, self.near, self.side, self.last = acc, near, side, last
        self.own, self.depth, self.fin = own, depth, fin
        chip = place.me // 2
        cx, cy, cd = place.xn // 2, place.yn // 2, place.dg // 2
        self.chip, self.cx, self.cy = chip, cx, cy
        fsdp = lambda d: {"fsdp": d}

        def copy(i, src, dst, to):
            return remote(src, dst, send.at[i], recv.at[i], to)

        if other is not None:
            self.a = copy(0, other, near, fsdp(place.sib))
        if side is not None:
            half = acc.shape[1] // 2
            self.low, self.high = low, high = pl.ds(0, half), pl.ds(half, half)
            self.b = [
                copy(1, acc.at[cd, low], side.at[1], fsdp(place.xn)),
                copy(2, acc.at[cd, high], side.at[3], fsdp(place.yn)),
                copy(3, acc.at[cx, low], side.at[0], fsdp(place.xn)),
                copy(4, acc.at[cy, high], side.at[2], fsdp(place.yn)),
            ]
            self.c = [
                copy(5, acc.at[cy, low], last.at[0], fsdp(place.yn)),
                copy(6, acc.at[cx, high], last.at[1], fsdp(place.xn)),
            ]
        if own is None:
            self.own = own = acc.at[chip]
        if depth is not None:
            inner = (rep == 1) | (rep == 2)
            self.inner, self.outer = inner, jnp.logical_not(inner)
            pair = {"rep": rep + 1 - 2 * (rep % 2)}
            self.d = copy(7, own, depth.at[0], pair)
            self.e = copy(8, own, depth.at[1], {"rep": 3 - rep})
            self.f = copy(9, fin, fin, pair)

    def near_start(self):
        self.a.start()

    def near_add(self):
        self.a.wait_recv()
        for c in range(self.acc.shape[0]):
            self.acc[c] = self.acc[c] + self.near[c]

    def side_start(self):
        for x in self.b:
            x.start()

    def near_sum(self):
        self.near_add()
        self.side_start()

    def add(self, c, half, ref):
        self.acc[c, half, :] = self.acc[c, half, :] + ref[...]

    def side_sum(self):
        self.b[0].wait()
        self.add(self.cy, self.low, self.side.at[1])
        self.c[0].start()
        self.b[1].wait()
        self.add(self.cx, self.high, self.side.at[3])
        self.c[1].start()
        self.b[2].wait()
        self.add(self.chip, self.low, self.side.at[0])
        self.b[3].wait()
        self.add(self.chip, self.high, self.side.at[2])

    def last_add(self):
        for x in self.c:
            x.wait()
        self.add(self.chip, self.low, self.last.at[0])
        self.add(self.chip, self.high, self.last.at[1])

    def z1_start(self):
        pl.when(self.outer)(self.d.start)

    def last_sum(self):
        self.last_add()
        self.z1_start()

    def z1_done(self):
        pl.when(self.outer)(self.d.wait_send)

        @pl.when(self.inner)
        def _():
            self.d.wait_recv()
            self.own[...] = self.own[...] + self.depth[0]

    def z2_start(self):
        pl.when(self.inner)(self.e.start)

    def z1z2(self):
        self.z1_done()
        self.z2_start()

    def z2z3(self):
        @pl.when(self.inner)
        def _():
            self.e.wait()
            self.fin[...] = self.own[...] + self.depth[1]
            self.f.start()

    def z3_done(self):
        pl.when(self.inner)(self.f.wait_send)
        pl.when(self.outer)(self.f.wait_recv)


class Direct:
    def __init__(self, me, shards, rep, reps, src, near, depth, send, recv):
        self.me, self.shards, self.rep, self.reps = me, shards, rep, reps
        self.src, self.near, self.depth = src, near, depth
        self.first = []
        for d in range(1, shards):
            to = (me + d) % shards
            self.first.append(
                remote(src.at[to % 2, to // 2], near.at[me], send.at[d - 1], recv.at[d - 1], {"fsdp": to})
            )
        self.second = []
        for d in range(1, reps):
            n = shards - 2 + d
            self.second.append(remote(depth.at[rep], depth.at[rep], send.at[n], recv.at[n], {"rep": (rep + d) % reps}))

    def start(self):
        for x in self.first:
            x.start()

    def middle(self):
        total = self.src[self.me % 2, self.me // 2].astype(F32)
        for d in range(1, self.shards):
            self.first[d - 1].wait()
            total = total + self.near[(self.me + self.shards - d) % self.shards].astype(F32)
        self.depth[self.rep] = total.astype(BF16)
        for x in self.second:
            x.start()

    def finish(self):
        for x in self.second:
            x.wait()
        total = self.depth[0].astype(F32)
        for z in range(1, self.reps):
            total = total + self.depth[z].astype(F32)
        return total


def per_shard(rows, shards, share):
    out = []
    for n in range(shards):
        at = lax.broadcasted_iota(jnp.int32, (rows.shape[1], LANES), 0) - n * share
        lane = lax.broadcasted_iota(jnp.int32, (rows.shape[1], LANES), 1)
        spot = jnp.where((at == lane) & (lane < share), 1.0, 0.0).astype(BF16)
        out.append(dot(rows, spot).astype(BF16))
    return out


def greet(me, shards, rep, reps):
    barrier = pltpu.get_barrier_semaphore()
    mesh = pl.DeviceIdType.MESH
    for d in range(1, shards):
        pl.semaphore_signal(barrier, inc=1, device_id={"fsdp": (me + d) % shards}, device_id_type=mesh)
    for d in range(1, reps):
        pl.semaphore_signal(barrier, inc=1, device_id={"rep": (rep + d) % reps}, device_id_type=mesh)
    pl.semaphore_wait(barrier, shards + reps - 2)


CHUNKS = 5


def ffn_reduce_kernel(
    few, shards, reps,
    x1_ref, cot_ref, slot_ref, mask_ref, vec_ref, wout_ref, o_ref, *refs,
):
    bups, wups, wdns = refs[:shards], refs[shards : 2 * shards], refs[2 * shards : 3 * shards]
    (
        res_ref, g1_ref, do_ref, gout_ref, state_ref, plane_ref,
        acc, h2, h2t, gy, gyt, dh2, outp, small_ref, g, near, side, last, depth, fin, send, recv,
    ) = refs[3 * shards :]
    j = pl.program_id(0)
    length, width = x1_ref.shape
    share = width // shards
    blocks = ffn_blocks(few, length)
    place = Place()
    rep = lax.axis_index("rep")
    core = place.me % 2
    units = []
    for u in range(CHUNKS):
        xy = u < 4
        z = u < 2
        units.append(
            Unit(
                place, rep, g.at[u, 1 - core], g.at[u, core], near.at[u],
                side.at[u] if xy else None, last.at[u] if xy else None, None,
                depth.at[u] if z else None, fin if z else None, send.at[u], recv.at[u],
            )
        )

    def at(step, *acts):
        @pl.when(j == step)
        def _():
            for act in acts:
                act()

    @pl.when(j == 0)
    def _():
        greet(place.me, shards, rep, reps)
        ffn_start(blocks, x1_ref, cot_ref, slot_ref, mask_ref, vec_ref, acc, h2, h2t, gy, gyt, dh2)

    wup = jnp.concatenate([w[...] for w in wups], axis=1)
    wdn = jnp.concatenate([w[...] for w in wdns], axis=0)
    bup = jnp.concatenate([b[...] for b in bups], axis=1)
    cols = pl.ds(pl.multiple_of(j * LANES, LANES), LANES)
    for n, block in enumerate(blocks):
        part = ffn_block(block, wup, wdn, bup, acc, h2, h2t, gy, gyt, dh2)
        if n == 0:
            gup, gdn, gbup = part
            for s in range(shards):
                mine = slice(s * share, (s + 1) * share)
                lanes = slice(s * LANES, (s + 1) * LANES)
                for b in range(shards):
                    g[j, s % 2, s // 2, b * share : (b + 1) * share, :] = gup[
                        mine, b * LANES : (b + 1) * LANES
                    ].astype(BF16)
                g[j, s % 2, s // 2, width:, :] = gdn[:, lanes].astype(BF16)
                small_ref[s : s + 1, cols] = gbup[:, lanes]
            for u in range(CHUNKS):
                at(u, units[u].near_start)
        if n == 1:
            at(2, units[0].last_sum)
            at(3, units[0].z1z2, units[1].last_sum)
            at(4, units[0].z2z3, units[2].last_add)
        if n == 2:
            for u in range(CHUNKS):
                if u:
                    at(u, units[u - 1].side_sum)
                at(u, units[u].near_sum if u < 4 else units[u].near_add)
            at(4, units[1].z1_done)

    @pl.when(j == CHUNKS - 1)
    def _():
        gout = ffn_end(
            blocks, x1_ref, slot_ref, vec_ref, wout_ref, o_ref, acc, gy, dh2, outp, res_ref, g1_ref, do_ref, small_ref
        )
        for s in range(shards):
            for b in range(CHUNKS):
                gout_ref[s % 2, s // 2, b * share : (b + 1) * share, :] = gout[
                    s * share : (s + 1) * share, b * LANES : (b + 1) * LANES
                ].astype(BF16)
        rows = CHUNKS * share
        vectors = per_shard(small_ref[8:16, :].astype(BF16), shards, share)
        for s in range(shards):
            gout_ref[s % 2, s // 2, rows : rows + 8, :] = vectors[s]
            bias = [small_ref[s : s + 1, b * LANES : (b + 1) * LANES] for b in range(CHUNKS)]
            bias = jnp.concatenate(bias + [jnp.zeros((8 - CHUNKS, LANES), F32)], axis=0)
            gout_ref[s % 2, s // 2, rows + 8 : rows + 16, :] = bias.astype(BF16)
            spare = gout_ref.shape[2] - rows - 16
            gout_ref[s % 2, s // 2, rows + 16 :, :] = jnp.zeros((spare, LANES), BF16)
        plane_ref[...] = g[4, core]
        units[3].last_add()
        for u in range(1, 4):
            state_ref[u] = g[u, core, units[u].chip]
        units[0].z3_done()
        state_ref[0] = fin[...]
        for u in range(CHUNKS):
            units[u].a.wait_send()


def ffn_reduce(few, shards, reps, x1, cot, slot, mask, vecs, bup, wup, wdn, wout, o):
    length, width = x1.shape
    share = width // shards
    chips = shards // 2
    rows = 2 * width
    spare = 448
    sds = jax.ShapeDtypeStruct
    whole = lambda *shape: pl.BlockSpec(shape, lambda j: (0,) * len(shape))
    pick = lambda s, shape, across: pl.BlockSpec(
        shape, lambda j: (0, s * CHUNKS + j) if across else (s * CHUNKS + j, 0)
    )
    dma = pltpu.SemaphoreType.DMA
    return pl.pallas_call(
        functools.partial(ffn_reduce_kernel, few, shards, reps),
        grid=(CHUNKS,),
        in_specs=[
            whole(length, width), whole(length, width), whole(8, length), whole(1, length), whole(8, width),
            whole(width, width), whole(few, width),
        ]
        + [pick(s, (1, LANES), True) for s in range(shards)]
        + [pick(s, (width, LANES), True) for s in range(shards)]
        + [pick(s, (LANES, width), False) for s in range(shards)],
        out_specs=[
            whole(length, width), whole(few, width), whole(few, width), whole(2, chips, spare, LANES),
            whole(4, rows, LANES), whole(chips, rows, LANES),
        ],
        out_shape=(
            sds((length, width), BF16),
            sds((few, width), F32),
            sds((few, width), BF16),
            sds((2, chips, spare, LANES), BF16),
            sds((4, rows, LANES), BF16),
            sds((chips, rows, LANES), BF16),
        ),
        scratch_shapes=[
            pltpu.VMEM((length, width), F32),
            pltpu.VMEM((length, width), BF16),
            pltpu.VMEM((width, few), BF16),
            pltpu.VMEM((few, width), BF16),
            pltpu.VMEM((width, few), BF16),
            pltpu.VMEM((few, width), F32),
            pltpu.VMEM((length, width), BF16),
            pltpu.VMEM((16, width), F32),
            pltpu.VMEM((CHUNKS, 2, chips, rows, LANES), BF16),
            pltpu.VMEM((CHUNKS, chips, rows, LANES), BF16),
            pltpu.VMEM((4, 4, rows // 2, LANES), BF16),
            pltpu.VMEM((4, 2, rows // 2, LANES), BF16),
            pltpu.VMEM((2, 2, rows, LANES), BF16),
            pltpu.VMEM((rows, LANES), BF16),
            dma((CHUNKS, Unit.COPIES)), dma((CHUNKS, Unit.COPIES)),
        ],
        compiler_params=pltpu.CompilerParams(
            vmem_limit_bytes=60 * MB, collective_id=3, has_side_effects=True
        ),
        name="ffn_reduce",
    )(x1, cot, slot, mask, vecs, wout, o, *[bup] * shards, *[wup] * shards, *[wdn] * shards)


GROUP_ROWS = 256


def back_reduce_kernel(
    few, shards, reps,
    q, k, v, do, o, lse, h1, xp, vec, wq, wk, wv, g1, slot, state_in, plane_in, gout_in,
    gtok, gup_out, gdn_out, gqkv_out, gout_out, vec_out,
    h1t, dh1, dqt, dkv, gtp, late,
    own, plane, fside, flast, fdepth, ffin,
    onear, oacc, oside, olast, odepth, ofin,
    gg, gnear, gside, glast, gdepth, gfin,
    dnear, ddepth, sg, snear, sdepth,
    send, recv, local, dsend, drecv,
):
    t = pl.program_id(0)
    groups = pl.num_programs(0)
    length, width = h1.shape
    share = width // shards
    cols = pl.ds(pl.multiple_of(t * LANES, LANES), LANES)
    place = Place()
    rep = lax.axis_index("rep")
    core = place.me % 2
    sems = lambda n: (send.at[n], recv.at[n])
    make = functools.partial(Unit, place, rep)
    u1, u2, u3 = [
        make(None, own, None, None, None, own.at[n], fdepth.at[n - 1], ffin.at[n - 1], *sems(n - 1))
        for n in range(1, 4)
    ]
    u4 = make(None, plane, None, fside, flast, None, fdepth.at[3], ffin.at[3], *sems(3))
    uo = make(gout_in.at[1 - core], oacc, onear, oside, olast, None, odepth, ofin, *sems(4))
    parts = [
        make(
            gg.at[n, 1 - core], gg.at[n, core], gnear.at[n], gside.at[n], glast.at[n], None, gdepth.at[n],
            gfin.at[n], *sems(5 + n)
        )
        for n in range(3)
    ]
    direct = functools.partial(Direct, place.me, shards, rep, reps)
    parts += [
        direct(gg.at[3 + n], dnear.at[n], ddepth.at[n], dsend.at[n], drecv.at[n]) for n in range(2)
    ]
    us = direct(sg, snear, sdepth, dsend.at[2], drecv.at[2])
    loads = [
        pltpu.make_async_copy(state_in, own, local.at[0]),
        pltpu.make_async_copy(plane_in, plane, local.at[1]),
        pltpu.make_async_copy(gout_in.at[core], oacc, local.at[2]),
    ]

    @pl.when(t == 0)
    def _():
        for x in loads:
            x.start()
        greet(place.me, shards, rep, reps)
        loads[0].wait()
        u1.z2_start()
        u2.z1_start()
        loads[1].wait()
        u4.side_start()
        uo.near_start()
        loads[2].wait()
        transpose_rows(h1, h1t)
        dh1[...] = jnp.zeros_like(dh1)
        late[...] = jnp.zeros_like(late)

    heads = Heads(few, q, k, v, do, o, lse, dqt, dkv)
    blocks = length // heads.step

    plan = [
        (2, uo.near_sum),
        (5, u1.z2z3), (5, u2.z1z2), (5, u3.z1_start), (5, u4.side_sum), (7, uo.side_sum),
        (9, u4.last_add), (10, u1.z3_done), (10, u2.z2z3), (10, u3.z1z2), (10, u4.z1_start),
        (11, uo.last_sum), (13, uo.z1z2), (15, u2.z3_done), (15, u3.z2z3), (15, u4.z1z2), (16, uo.z2z3),
        (18, uo.z3_done), (19, u3.z3_done), (19, u4.z2z3),
    ]
    chain = ("near_sum", "side_sum", "last_sum", "z1z2", "z2z3")
    rest = []
    for n in range(3):
        for when, name in zip((2, 5, 7, 9, 11), chain):
            slot_at = 4 * (n + 1) + when
            if slot_at < 20:
                plan.append((slot_at, getattr(parts[n], name)))
            else:
                rest.append(getattr(parts[n], name))
    plan.append((19, parts[3].middle))
    plan.sort(key=lambda entry: entry[0])

    def body(i, _):
        for at, step in plan:
            pl.when(t * blocks + i == at)(step)
        heads.keys(i)
        return 0

    lax.fori_loop(0, blocks, body, 0)
    dq, gq, gk, gv = group_weights(few, dqt, dkv, h1t, late, cols)
    for n, part in enumerate((gq, gk, gv)):
        for s in range(shards):
            gg[t, s % 2, s // 2, n * share : (n + 1) * share, :] = part[s * share : (s + 1) * share, :]
    for s in range(shards):
        gg[t, s % 2, s // 2, 3 * share :, :] = jnp.zeros((GROUP_ROWS - 3 * share, LANES), BF16)
    for n in range(5):
        pl.when(t == n)(parts[n].near_start if n < 3 else parts[n].start)
    group_inputs(few, dq, dkv, wq, wk, wv, dh1)

    @pl.when(t == groups - 1)
    def _():
        z1z2, z2z3 = rest
        z1z2()
        back_finish(few, dh1, xp, vec, g1, late, gtp)
        vectors = per_shard(jnp.concatenate([late[...], jnp.zeros_like(late)], axis=0).astype(BF16), shards, share)
        for s in range(shards):
            sg[s % 2, s // 2] = vectors[s]
        us.start()
        z2z3()
        parts[4].middle()
        unpermute(slot[0:1, :], gtp, gtok)
        us.middle()
        u4.z3_done()
        for n in range(CHUNKS):
            src = ffin.at[n - 1] if n else own.at[0]
            for b in range(shards):
                gup_out[:, b * width + n * LANES : b * width + (n + 1) * LANES] = src[
                    b * share : (b + 1) * share, :
                ].astype(F32)
            gdn_out[n * LANES : (n + 1) * LANES, :] = jnp.transpose(src[width:, :].astype(F32))
        for b in range(CHUNKS):
            gout_out[:, b * LANES : (b + 1) * LANES] = ofin[b * share : (b + 1) * share, :].astype(F32)
        vec_out[0:16, :] = ofin[CHUNKS * share : CHUNKS * share + 16, :].astype(F32)
        for n in range(5):
            if n < 3:
                parts[n].z3_done()
                parts[n].a.wait_send()
                done = gfin[n].astype(F32)
            else:
                done = parts[n].finish()
            for m in range(3):
                gqkv_out[:, m * width + n * LANES : m * width + (n + 1) * LANES] = done[m * share : (m + 1) * share, :]
        vec_out[16:32, :] = us.finish()
        uo.a.wait_send()


SMALL_ROWS = 16


def back_reduce(few, shards, reps, qkv, do, o, lse, h1, xp, vecs, wqkv, g1, slot, state, plane, gout):
    length, width = h1.shape
    share = width // shards
    chips = shards // 2
    rows = 2 * width
    groups = width // LANES
    hidden = shards * width
    sds = jax.ShapeDtypeStruct
    whole, cols, in_specs, scratch = back_specs(few, length, width, True)
    hbm = pl.BlockSpec(memory_space=pl.ANY)
    dma = pltpu.SemaphoreType.DMA
    vm = lambda *shape: pltpu.VMEM(shape + (LANES,), BF16)
    spare = gout.shape[2]

    def buffers(rows):
        return [vm(4, rows // 2), vm(2, rows // 2), vm(2, rows), vm(rows)]

    many = lambda n, refs: [pltpu.VMEM((n,) + r.shape, BF16) for r in refs]
    fside, flast, fdepth, ffin = buffers(rows)
    return pl.pallas_call(
        functools.partial(back_reduce_kernel, few, shards, reps),
        grid=(groups,),
        in_specs=in_specs + [hbm, hbm, hbm],
        out_specs=[
            whole(length, width), whole(share, hidden), whole(width, width), whole(share, 3 * width),
            whole(share, width), whole(32, LANES),
        ],
        out_shape=(
            sds((length, width), BF16),
            sds((share, hidden), F32),
            sds((width, width), F32),
            sds((share, 3 * width), F32),
            sds((share, width), F32),
            sds((32, LANES), F32),
        ),
        scratch_shapes=scratch
        + [
            pltpu.VMEM((8, width), F32),
            vm(4, rows), vm(chips, rows), fside, flast,
        ]
        + many(4, [fdepth, ffin])
        + [vm(chips, spare), vm(chips, spare)] + buffers(spare)
        + [vm(5, 2, chips, GROUP_ROWS), vm(3, chips, GROUP_ROWS)] + many(3, buffers(GROUP_ROWS))
        + [vm(2, shards, GROUP_ROWS), vm(2, reps, GROUP_ROWS)]
        + [vm(2, chips, SMALL_ROWS), vm(shards, SMALL_ROWS), vm(reps, SMALL_ROWS)]
        + [dma((8, Unit.COPIES)), dma((8, Unit.COPIES)), dma((3,))]
        + [dma((3, shards + reps - 2)), dma((3, shards + reps - 2))],
        compiler_params=pltpu.CompilerParams(
            vmem_limit_bytes=60 * MB, collective_id=4, has_side_effects=True
        ),
        name="back_reduce",
    )(qkv, qkv, qkv, do, o, lse, h1, xp, vecs, wqkv, wqkv, wqkv, g1, slot, state, plane, gout)


def local(
    reps, shards,
    tokens, masked, cotangent, norm1_gain, norm1_shift, w_qkv, bias_query, bias_value, w_out,
    bias_out, norm2_gain, norm2_shift, w_up, bias_up, w_down, bias_down,
):
    seqs, length, width = tokens.shape
    hidden = w_up.shape[1]
    share = w_qkv.shape[0]
    close = shards == 8 and reps == 4 and share % 16 == 0 and share <= LANES and w_down.shape[0] == width
    x = tokens.reshape(seqs * length, width)
    cot = cotangent.reshape(seqs * length, width)
    mask = masked.astype(F32)
    if close:
        pack = jnp.concatenate(
            [
                jnp.pad(
                    jnp.stack(
                        [norm1_gain, norm1_shift, bias_query, bias_value, bias_out, norm2_gain, norm2_shift, bias_down]
                    ),
                    ((0, 0), (0, LANES - share)),
                ),
                jnp.pad(bias_up.reshape(-1, LANES), ((0, 3), (0, 0))),
            ]
        )
        slot, xp, h1, qkv, o, lse, x1, vecs, bup, over, wqkv, wout, wup, wdn = gather_attn(
            reps, shards, x, mask, pack, w_qkv, w_out, w_up, w_down
        )
        small_enough = over[0, 0] < 0.5
    else:
        small_enough = lax.pmax(jnp.sum(masked), ("rep", "fsdp")) <= FEW
        packed = jnp.stack(
            [norm1_gain, norm1_shift, bias_query, bias_value, bias_out, norm2_gain, norm2_shift, bias_down]
        )
        vecs = lax.all_gather(packed, "fsdp", axis=1, tiled=True).astype(F32)
        bup = lax.all_gather(bias_up, "fsdp", axis=0, tiled=True).astype(F32).reshape(1, hidden)
        gather = lambda w: lax.all_gather(w, "fsdp", axis=0, tiled=True)
        wqkv, wout, wup, wdn = gather(w_qkv), gather(w_out), gather(w_up), gather(w_down)
        slot, xp, h1, qkv, o, lse, x1 = attn_forward(x, mask, vecs, wqkv, wout)

    def backward(few):
        def run():
            res, gup, gdn, g1, do, gout, early = feed_forward(
                few, x1, cot, slot, mask, vecs, bup, wup, wdn, wout, o
            )
            if close:
                gtok, gup, gdn, gqkv, gout, early, late = reduce_backward(
                    few, shards, reps, 1,
                    qkv, do, o, lse, h1, xp, vecs, wqkv, g1, slot, early, gout, gup, gdn,
                )
                return res, gtok, gup, gdn, gqkv, gout, early, late
            gtok, gq, gk, gv, late = attn_backward(
                few, qkv, do, o, lse, h1, xp, vecs, wqkv, g1, slot
            )
            return res, gtok, gup, gdn, jnp.concatenate([gout, gq, gk, gv], axis=1), early, late

        return run

    me = lax.axis_index("fsdp")
    own = bias_up.shape[0]

    def pick(late, early):
        gbup = lax.dynamic_slice_in_dim(early[:8].reshape(hidden), me * own, own)
        return lax.dynamic_slice_in_dim(jnp.concatenate([late[:4], early[8:12]]), me * share, share, axis=1), gbup

    if close:
        res, g1, do, part, state, plane = ffn_reduce(
            FEW, shards, reps, x1, cot, slot, mask, vecs, bup, wup, wdn, wout, o
        )
        gtok, gup, gdn, gqkv, gout, small = back_reduce(
            FEW, shards, reps, qkv, do, o, lse, h1, xp, vecs, wqkv, g1, slot, state, plane, part
        )

        def redo():
            *outs, early, late = backward(length)()
            mine, gbup = pick(late, early)
            rows = jnp.concatenate([mine[4:], jnp.zeros((4, share), F32)])
            tail = jnp.concatenate([mine[:4], jnp.zeros((12, share), F32)])
            wide = lambda x: jnp.pad(x, ((0, 0), (0, LANES - share)))
            ups = jnp.pad(gbup.reshape(-1, LANES), ((0, 8 - own // LANES), (0, 0)))
            return (*outs, jnp.concatenate([wide(rows), ups, wide(tail)]))

        res, gtok, gup, gdn, gqkv, gout, small = lax.cond(
            small_enough, lambda: (res, gtok, gup, gdn, gqkv, gout, small), redo
        )
        mine = [small[n, :share] for n in (16, 17, 18, 19, 0, 1, 2, 3)]
        gbup = small[8 : 8 + own // LANES].reshape(own)
    else:
        def scatter(g, dim):
            part = lax.psum_scatter(g, "fsdp", scatter_dimension=dim, tiled=True)
            return lax.psum(part, "rep").astype(F32)

        res, gtok, gup, gdn, gattn, early, late = lax.cond(small_enough, backward(FEW), backward(length))
        gup = scatter(gup, 0)
        gdn = scatter(gdn.transpose(0, 2, 1).reshape(hidden, width), 0)
        gattn = scatter(gattn, 0)
        gout, gqkv = gattn[:, :width], gattn[:, width:]
        mine, gbup = pick(lax.psum(late, ("rep", "fsdp")), lax.psum(early, ("rep", "fsdp")))
    return (
        res.reshape(seqs, length, width),
        gtok.reshape(seqs, length, width),
        mine[0], mine[1], gqkv, mine[2], mine[3], gout, mine[4], mine[5], mine[6],
        gup, gbup, gdn, mine[7],
    )


def solution(mesh):
    rows3 = P(("rep", "fsdp"), None, None)
    vec = P("fsdp")
    mat = P("fsdp", None)
    in_specs = (
        rows3, P(("rep", "fsdp"), None), rows3,
        vec, vec, mat, vec, vec, mat, vec, vec, vec, mat, vec, mat, vec,
    )
    out_specs = (rows3, rows3, vec, vec, mat, vec, vec, mat, vec, vec, vec, mat, vec, mat, vec)
    body = functools.partial(local, mesh.shape["rep"], mesh.shape["fsdp"])
    return jax.shard_map(body, mesh=mesh, in_specs=in_specs, out_specs=out_specs, check_vma=False)
```

```python
import functools

import jax
import jax.numpy as jnp
from jax import lax
from jax.experimental import pallas as pl
from jax.experimental.pallas import tpu as pltpu
from jax.sharding import PartitionSpec as P

HEADS = 20
HEAD_DIM = 32
GROUP = 4
LANES = 128
SCALE = HEAD_DIM ** (-0.5)
LOG2E = 1.4426950408889634
FEW = 384
F32 = jnp.float32
BF16 = jnp.bfloat16
MB = 1024 * 1024

NN = (((1,), (0,)), ((), ()))
NT = (((1,), (1,)), ((), ()))


def dot(a, b, dims=NN):
    return lax.dot_general(a, b, dims, preferred_element_type=F32)


def norm_stats(x):
    mean = jnp.mean(x, axis=-1, keepdims=True)
    centred = x - mean
    variance = jnp.mean(centred * centred, axis=-1, keepdims=True)
    rstd = lax.rsqrt(variance + 1e-05)
    return centred * rstd, rstd


def norm_back(grad, xhat, rstd, gain):
    dxhat = grad * gain
    first = jnp.mean(dxhat, axis=-1, keepdims=True)
    second = jnp.mean(dxhat * xhat, axis=-1, keepdims=True)
    return rstd * (dxhat - first - xhat * second)


def cdf_parts(u):
    z = jnp.abs(u)
    t = pl.reciprocal(1.0 + 0.23164189 * z, approx=True)
    e = jnp.exp2(u * u * (-0.5 * LOG2E))
    poly = t * (
        0.127414796 + t * (-0.142248368 + t * (0.7107068705 + t * (-0.7265760135 + t * 0.5307027145)))
    )
    tail = poly * e
    return jnp.where(u < 0, tail, 1.0 - tail), e


def one_hot_rows(slot, start, size):
    length = slot.shape[1]
    rows = lax.broadcasted_iota(jnp.int32, (size, length), 0).astype(F32) + start
    return jnp.where(rows == slot, 1.0, 0.0)


def unpermute(slot, src_ref, out_ref):
    length = slot.shape[1]
    wide = jnp.transpose(jnp.broadcast_to(slot, (LANES, length)))
    step = 256
    for start in range(0, length, step):
        col = wide[start : start + step, :1]
        cols = lax.broadcasted_iota(jnp.int32, (step, length), 1).astype(F32)
        pick = jnp.where(cols == col, 1.0, 0.0).astype(BF16)
        out_ref[start : start + step, :] = dot(pick, src_ref[...]).astype(BF16)


def slots_of(mask_ref):
    length = mask_ref.shape[1]
    step = 256
    mask8 = jnp.broadcast_to(mask_ref[...], (8, length))
    cum = []
    for start in range(0, length, step):
        up = lax.broadcasted_iota(jnp.int32, (length, step), 0)
        to = lax.broadcasted_iota(jnp.int32, (length, step), 1) + start
        cum.append(dot(mask8.astype(BF16), jnp.where(up <= to, 1.0, 0.0).astype(BF16)))
    cum = jnp.concatenate(cum, axis=1)
    count = jnp.sum(mask8, axis=1, keepdims=True)
    pos = lax.broadcasted_iota(jnp.int32, (8, length), 1).astype(F32)
    return jnp.where(mask8 > 0.5, cum - 1.0, count + pos - cum), count


def permute_rows(tokens_ref, slot, xp_ref):
    step = 256

    def body(i, _):
        rows = pl.ds(pl.multiple_of(i * step, step), step)
        pick = one_hot_rows(slot[:1], (i * step).astype(F32), step).astype(BF16)
        xp_ref[rows, :] = dot(pick, tokens_ref[...]).astype(BF16)
        return 0

    lax.fori_loop(0, tokens_ref.shape[0] // step, body, 0)


def first_norm(xp_ref, vec_ref, h1_ref):
    step = 128
    gain = vec_ref[0:1, :]
    shift = vec_ref[1:2, :]

    def body(i, _):
        rows = pl.ds(pl.multiple_of(i * step, step), step)
        xhat, _ = norm_stats(xp_ref[rows, :].astype(F32))
        h1_ref[rows, :] = (xhat * gain + shift).astype(BF16)
        return 0

    lax.fori_loop(0, xp_ref.shape[0] // step, body, 0)


def project(h1_ref, vec_ref, wqkv_ref, qkv_ref):
    length, width = h1_ref.shape
    step = 256
    bq = vec_ref[2:3, :]
    bv = vec_ref[3:4, :]

    def body(i, _):
        rows = pl.ds(pl.multiple_of(i * step, step), step)
        h1 = h1_ref[rows, :]
        qkv_ref[rows, :width] = (dot(h1, wqkv_ref[:, :width]) + bq).astype(BF16)
        qkv_ref[rows, width : 2 * width] = dot(h1, wqkv_ref[:, width : 2 * width]).astype(BF16)
        qkv_ref[rows, 2 * width :] = (dot(h1, wqkv_ref[:, 2 * width :]) + bv).astype(BF16)
        return 0

    lax.fori_loop(0, length // step, body, 0)


def attend(qkv_ref, o_ref, lse_ref, beside, ahead):
    length, width = o_ref.shape
    step = 256
    c = SCALE * LOG2E
    lane = lax.broadcasted_iota(jnp.int32, (step, LANES), 1)

    def body(n, _):
        beside(n)
        t = n // (length // step)
        i = n % (length // step)
        pl.when(i == 0)(lambda: ahead(t))
        rows = pl.ds(pl.multiple_of(i * step, step), step)
        q = qkv_ref[rows, pl.ds(pl.multiple_of(t * LANES, LANES), LANES)]
        k = qkv_ref[:, pl.ds(pl.multiple_of(width + t * LANES, LANES), LANES)]
        v = qkv_ref[:, pl.ds(pl.multiple_of(2 * width + t * LANES, LANES), LANES)]
        vo = jnp.concatenate([v, jnp.ones_like(v)], axis=1)
        out = jnp.zeros((step, LANES), F32)
        lses = jnp.zeros((step, LANES), F32)
        for h in range(GROUP):
            mine = lane // HEAD_DIM == h
            s = dot(jnp.where(mine, q, jnp.zeros_like(q)), k, NT)
            top = jnp.max(s, axis=-1, keepdims=True)
            p = jnp.exp2((s - top) * c).astype(BF16)
            ov = dot(p, vo)
            total = ov[:, LANES:]
            out = jnp.where(mine, ov[:, :LANES] / total, out)
            lses = jnp.where(lane == h, top * c + jnp.log2(total), lses)
        o_ref[rows, pl.ds(pl.multiple_of(t * LANES, LANES), LANES)] = out.astype(BF16)
        lse_ref[pl.ds(pl.multiple_of(t * 8, 8), 8), rows] = jnp.transpose(lses)[:8, :]
        return 0

    lax.fori_loop(0, (width // LANES) * (length // step), body, 0)


def join(xp_ref, o_ref, wout_ref, vec_ref, x1_ref):
    step = 256
    bout = vec_ref[4:5, :]

    def body(i, _):
        rows = pl.ds(pl.multiple_of(i * step, step), step)
        x1_ref[rows, :] = xp_ref[rows, :].astype(F32) + dot(o_ref[rows, :], wout_ref[...]) + bout
        return 0

    lax.fori_loop(0, xp_ref.shape[0] // step, body, 0)


def attn_kernel(
    tokens_ref, mask_ref, vec_ref, wqkv_ref, wout_ref,
    slot_ref, xp_ref, h1_ref, qkv_ref, o_ref, lse_ref, x1_ref,
):
    slot, _ = slots_of(mask_ref)
    slot_ref[...] = slot
    permute_rows(tokens_ref, slot, xp_ref)
    first_norm(xp_ref, vec_ref, h1_ref)
    project(h1_ref, vec_ref, wqkv_ref, qkv_ref)
    attend(qkv_ref, o_ref, lse_ref, lambda n: None, lambda t: None)
    join(xp_ref, o_ref, wout_ref, vec_ref, x1_ref)


class Place:
    def __init__(self):
        self.me = me = lax.axis_index("fsdp")
        core = me % 2
        x = me // 2 % 2
        y = me // 4
        self.sib = me + 1 - 2 * core
        self.xn = me + 2 - 4 * x
        self.yn = me + 4 - 8 * y
        self.dg = me + 6 - 4 * x - 8 * y


def remote(src, dst, send, recv, to):
    return pltpu.make_async_remote_copy(
        src_ref=src, dst_ref=dst, send_sem=send, recv_sem=recv,
        device_id=to, device_id_type=pl.DeviceIdType.MESH,
    )


class Gather:
    def __init__(self, place, own, full, cut, send, recv, local, cols=slice(None)):
        rows = own.shape[0]
        own = own.at[:, cols]
        at = lambda s, lo=0, hi=rows: full.at[pl.ds(pl.multiple_of(s * rows + lo, 16), hi - lo), cols]
        me, sib, xn, yn, dg = place.me, place.sib, place.xn, place.yn, place.dg
        moves = [
            (own, at(me), sib), (own, at(me), xn), (own, at(me), yn),
            (at(xn), at(xn), sib), (at(yn), at(yn), sib),
            (at(xn, 0, cut), at(xn, 0, cut), yn), (at(yn, cut), at(yn, cut), xn),
            (at(dg, 0, cut), at(dg, 0, cut), sib), (at(dg, cut), at(dg, cut), sib),
        ]
        self.copies = [
            remote(src, dst, send.at[i], recv.at[i], {"fsdp": to}) for i, (src, dst, to) in enumerate(moves)
        ]
        self.local = pltpu.make_async_copy(own, at(me), local)

    def first(self):
        self.copies[1].start()
        self.copies[2].start()
        self.copies[0].start()
        self.local.start()

    def second(self):
        self.copies[1].wait_recv()
        self.copies[5].start()
        self.copies[3].start()
        self.copies[2].wait_recv()
        self.copies[6].start()
        self.copies[4].start()

    def third(self):
        self.copies[5].wait_recv()
        self.copies[7].start()
        self.copies[6].wait_recv()
        self.copies[8].start()

    def finish(self):
        for i in (0, 3, 4, 7, 8):
            self.copies[i].wait_recv()
        self.local.wait()
        for copy in self.copies:
            copy.wait_send()


class WideGather:
    COPIES = 14

    def __init__(self, place, rep, own, full, send, recv, local):
        rows, cols = own.shape
        dim, tile = (0, 16) if rows >= cols else (1, 128)
        size = own.shape[dim]
        base = 0
        third = size // tile // 3 * tile
        both = size - 2 * third
        wide = third + both
        even = rep % 2
        mult = lambda n: pl.multiple_of(n, tile)

        def cut(ref, s, lo, n):
            lo = base + lo
            if dim == 0:
                return ref.at[pl.ds(mult(s * rows + lo), n), :]
            return ref.at[pl.ds(pl.multiple_of(s * rows, 16), rows), pl.ds(mult(lo), n)]

        at = functools.partial(cut, full)
        w, mine, others = even * third, even * wide, (1 - even) * wide
        first = max(wide // 2 // tile * tile, third)
        second = wide - first
        assert second >= third
        me, sib, xn, yn, dg = place.me, place.sib, place.xn, place.yn, place.dg
        all_of = lambda s: at(s, 0, size)
        fsdp = lambda d: {"fsdp": d}
        pair = {"rep": rep + 1 - 2 * even}
        piece = cut(own, 0, w, wide)
        whole = cut(own, 0, 0, size)
        moves = [
            (whole, all_of(me), fsdp(sib)),
            (piece, at(me, w, wide), fsdp(xn)),
            (piece, at(me, w, wide), fsdp(yn)),
            (at(xn, w, first),) * 2 + (fsdp(yn),),
            (at(yn, w + first, second),) * 2 + (fsdp(xn),),
            (at(xn, mine, third),) * 2 + (pair,),
            (at(yn, mine, third),) * 2 + (pair,),
            (at(dg, mine, third),) * 2 + (pair,),
            (at(xn, w, wide),) * 2 + (fsdp(sib),),
            (at(yn, w, wide),) * 2 + (fsdp(sib),),
            (at(dg, w, wide),) * 2 + (fsdp(sib),),
            (at(xn, others, third),) * 2 + (fsdp(sib),),
            (at(yn, others, third),) * 2 + (fsdp(sib),),
            (at(dg, others, third),) * 2 + (fsdp(sib),),
        ]
        self.copies = [remote(src, dst, send.at[i], recv.at[i], to) for i, (src, dst, to) in enumerate(moves)]
        self.local = pltpu.make_async_copy(whole, all_of(me), local)

    def start(self, *which):
        for i in which:
            self.copies[i].start()

    def arrived(self, *which):
        for i in which:
            self.copies[i].wait_recv()

    def first(self):
        self.start(1, 2, 0)
        self.local.start()

    def second(self):
        self.arrived(1)
        self.start(3, 5, 8)
        self.arrived(2)
        self.start(4, 6, 9)

    def third(self):
        self.arrived(3, 4)
        self.start(7, 10)

    def fourth(self):
        self.arrived(5, 6)
        self.start(11, 12)

    def fifth(self):
        self.arrived(7)
        self.start(13)

    def finish(self):
        self.arrived(0, 8, 9, 10, 11, 12, 13)
        self.local.wait()
        for copy in self.copies:
            copy.wait_send()


def gather_attn_kernel(
    reps,
    tokens_ref, mask_ref, pack_ref, wqkv_in, wout_in, wup_in, wdn_in,
    slot_ref, xp_ref, h1_ref, qkv_ref, o_ref, lse_ref, x1_ref, vec_ref, bup_ref, over_ref,
    wqkv_ref, wout_ref, wup_ref, wdn_ref,
    packs, overs, wown, send, recv, local, psend, precv, rsend, rrecv,
):
    width = tokens_ref.shape[1]
    share = wqkv_in.shape[0]
    place = Place()
    me = place.me
    rep = lax.axis_index("rep")
    shards = packs.shape[0]
    barrier = pltpu.get_barrier_semaphore()
    for d in range(1, shards):
        pl.semaphore_signal(
            barrier, inc=1, device_id={"fsdp": (me + d) % shards}, device_id_type=pl.DeviceIdType.MESH
        )
    for d in range(1, reps):
        pl.semaphore_signal(
            barrier, inc=1, device_id={"rep": (rep + d) % reps}, device_id_type=pl.DeviceIdType.MESH
        )
    slot, count = slots_of(mask_ref)
    slot_ref[...] = slot
    row = lax.broadcasted_iota(jnp.int32, (16, LANES), 0)
    over = jnp.where(count[:1] > FEW, 1.0, 0.0)
    for n in range(3 * width // LANES):
        t, m = n // 3, n % 3
        wown[:, n * LANES : (n + 1) * LANES] = wqkv_in[:, m * width + t * LANES : m * width + (t + 1) * LANES]
    packs[me] = jnp.where(row == 13, over, pack_ref[...].astype(F32)).astype(BF16)
    pl.semaphore_wait(barrier, shards + reps - 2)

    sems = lambda n: (send.at[n], recv.at[n], local.at[n])
    early = 2 * 3 * LANES
    qkv = Gather(place, wown, wqkv_ref, 48, *sems(0), cols=slice(0, early))
    rest = Gather(place, wown, wqkv_ref, 32, *sems(1), cols=slice(early, 3 * width))
    out = Gather(place, wout_in, wout_ref, 48, *sems(2))
    up = WideGather(place, rep, wup_in, wup_ref, *sems(3))
    down = WideGather(place, rep, wdn_in, wdn_ref, *sems(4))
    qkv.first()
    vectors = []
    for d in range(1, shards):
        copy = remote(
            packs.at[me], packs.at[me], psend.at[d - 1], precv.at[d - 1], {"fsdp": (me + d) % shards}
        )
        copy.start()
        vectors.append(copy)
    permute_rows(tokens_ref, slot, xp_ref)
    qkv.second()
    rest.first()
    up.first()
    for copy in vectors:
        copy.wait_recv()
    all_over = packs[0]
    for s in range(1, shards):
        all_over = jnp.maximum(all_over, packs[s])
    overs[rep] = all_over
    flags = []
    for d in range(1, reps):
        copy = remote(overs.at[rep], overs.at[rep], rsend.at[d - 1], rrecv.at[d - 1], {"rep": (rep + d) % reps})
        copy.start()
        flags.append(copy)
    vecs = jnp.zeros((16, width), F32)
    for s in range(shards):
        pack = packs[s]
        lane = lax.broadcasted_iota(jnp.int32, (LANES, width), 0)
        col = lax.broadcasted_iota(jnp.int32, (LANES, width), 1) - s * share
        spot = jnp.where((lane == col) & (lane < share), 1.0, 0.0).astype(BF16)
        vecs = vecs + dot(pack, spot)
        wide = pack.astype(F32)
        for r in range(width // LANES):
            bup_ref[0:1, s * width + r * LANES : s * width + (r + 1) * LANES] = wide[8 + r : 9 + r, :]
    vec_ref[...] = vecs[:8]
    first_norm(xp_ref, vec_ref, h1_ref)
    qkv.third()
    qkv.finish()

    plan = (
        (3, rest.second), (4, down.first), (5, out.first), (6, up.second), (7, rest.third), (8, rest.finish),
        (9, out.second), (11, up.third), (12, up.fourth), (13, out.third), (13, down.second), (14, up.fifth),
        (18, down.third), (19, down.fourth),
    )

    def beside(n):
        for at, step in plan:
            pl.when(n == at)(step)

    def ahead(t):
        step = 512
        cols = pl.ds(pl.multiple_of(t * 3 * LANES, LANES), 3 * LANES)
        at = [pl.multiple_of(n * width + t * LANES, LANES) for n in range(3)]
        bq = vec_ref[2:3, pl.ds(at[0], LANES)]
        bv = vec_ref[3:4, pl.ds(at[0], LANES)]
        bias = jnp.concatenate([bq, jnp.zeros_like(bq), bv], axis=1)
        for start in range(0, h1_ref.shape[0], step):
            rows = slice(start, start + step)
            part = (dot(h1_ref[rows, :], wqkv_ref[:, cols]) + bias).astype(BF16)
            for n in range(3):
                qkv_ref[rows, pl.ds(at[n], LANES)] = part[:, n * LANES : (n + 1) * LANES]

    attend(qkv_ref, o_ref, lse_ref, beside, ahead)
    out.finish()
    join(xp_ref, o_ref, wout_ref, vec_ref, x1_ref)
    for copy in flags:
        copy.wait()
    for copy in vectors:
        copy.wait_send()
    worst = overs[0]
    for z in range(1, reps):
        worst = jnp.maximum(worst, overs[z])
    over_ref[...] = worst[13:14, :].astype(F32)
    down.fifth()
    up.finish()
    down.finish()


def gather_attn(reps, shards, tokens, mask, pack, w_qkv, w_out, w_up, w_down):
    length, width = tokens.shape
    hidden = w_up.shape[1]
    sds = jax.ShapeDtypeStruct
    groups = width // LANES
    vmem = pl.BlockSpec(memory_space=pltpu.VMEM)
    hbm = pl.BlockSpec(memory_space=pl.ANY)
    dma = pltpu.SemaphoreType.DMA
    return pl.pallas_call(
        functools.partial(gather_attn_kernel, reps),
        in_specs=[vmem] * 7,
        out_specs=[vmem] * 12 + [hbm] * 2,
        out_shape=(
            sds((8, length), F32),
            sds((length, width), BF16),
            sds((length, width), BF16),
            sds((length, 3 * width), BF16),
            sds((length, width), BF16),
            sds((8 * groups, length), F32),
            sds((length, width), F32),
            sds((8, width), F32),
            sds((1, hidden), F32),
            sds((1, LANES), F32),
            sds((width, 3 * width), BF16),
            sds((width, width), BF16),
            sds((width, hidden), BF16),
            sds((hidden, width), BF16),
        ),
        scratch_shapes=[
            pltpu.VMEM((shards, 16, LANES), BF16),
            pltpu.VMEM((reps, 16, LANES), BF16),
            pltpu.VMEM(w_qkv.shape, BF16),
            dma((5, WideGather.COPIES)), dma((5, WideGather.COPIES)), dma((5,)),
            dma((shards - 1,)), dma((shards - 1,)),
            dma((reps - 1,)), dma((reps - 1,)),
        ],
        compiler_params=pltpu.CompilerParams(
            vmem_limit_bytes=56 * MB, collective_id=0, has_side_effects=True
        ),
        name="gather_attn",
    )(tokens, mask, pack, w_qkv, w_out, w_up, w_down)


def attn_forward(tokens, mask, vecs, wqkv, wout):
    length, width = tokens.shape
    sds = jax.ShapeDtypeStruct
    groups = width // LANES
    return pl.pallas_call(
        attn_kernel,
        out_shape=(
            sds((8, length), F32),
            sds((length, width), BF16),
            sds((length, width), BF16),
            sds((length, 3 * width), BF16),
            sds((length, width), BF16),
            sds((8 * groups, length), F32),
            sds((length, width), F32),
        ),
        compiler_params=pltpu.CompilerParams(vmem_limit_bytes=56 * MB),
        name="attn_forward",
    )(tokens, mask, vecs, wqkv, wout)


def ffn_blocks(few, length):
    part = few if few <= 384 else 256
    blocks = [(start, part, True) for start in range(0, few, part)]
    start = few
    while start < length:
        size = min(320, length - start)
        blocks.append((start, size, False))
        start += size
    return blocks


def ffn_start(blocks, x1_ref, cot_ref, slot_ref, mask_ref, vec_ref, acc, h2, h2t, gy, gyt, dh2):
    gain = vec_ref[5:6, :]
    shift = vec_ref[6:7, :]
    bdown = vec_ref[7:8, :]
    for start, size, back in blocks:
        rows = slice(start, start + size)
        x1 = x1_ref[rows, :]
        xhat, _ = norm_stats(x1)
        hidden = (xhat * gain + shift).astype(BF16)
        h2[rows, :] = hidden
        acc[rows, :] = x1 + bdown
        if back:
            h2t[:, rows] = jnp.transpose(hidden)
            pick = one_hot_rows(slot_ref[0:1, :], float(start), size) * mask_ref[...]
            g = dot(pick.astype(BF16), cot_ref[...])
            gy[rows, :] = g.astype(BF16)
            gyt[:, rows] = jnp.transpose(g.astype(BF16))
            dh2[rows, :] = jnp.zeros_like(g)


def ffn_block(block, wup, wdn, bup, acc, h2, h2t, gy, gyt, dh2):
    start, size, back = block
    rows = slice(start, start + size)
    u = dot(h2[rows, :], wup) + bup
    cdf, e = cdf_parts(u)
    a = (u * cdf).astype(BF16)
    acc[rows, :] += dot(a, wdn)
    if not back:
        return None
    da = dot(gy[rows, :], wdn, NT)
    du = ((cdf + u * e * 0.3989422804014327) * da).astype(BF16)
    dh2[rows, :] += dot(du, wup, NT)
    return (
        dot(h2t[:, rows], du),
        dot(gyt[:, rows], a),
        jnp.sum(du.astype(F32), axis=0, keepdims=True),
    )


def ffn_end(blocks, x1_ref, slot_ref, vec_ref, wout_ref, o_ref, acc, gy, dh2, outp, res_ref, g1_ref, do_ref, small_ref):
    gain = vec_ref[5:6, :]
    ggain = gshift = gbdown = gbout = gout = None
    plus = lambda a, b: b if a is None else a + b
    for start, size, back in blocks:
        rows = slice(start, start + size)
        outp[rows, :] = acc[rows, :].astype(BF16)
        if back:
            xhat, rstd = norm_stats(x1_ref[rows, :])
            d = dh2[rows, :]
            g = gy[rows, :].astype(F32)
            g1 = g + norm_back(d, xhat, rstd, gain)
            g1_ref[rows, :] = g1
            g1b = g1.astype(BF16)
            do_ref[rows, :] = dot(g1b, wout_ref[...], NT).astype(BF16)
            gout = plus(gout, dot(jnp.transpose(o_ref[rows, :]), g1b))
            ggain = plus(ggain, jnp.sum(d * xhat, axis=0, keepdims=True))
            gshift = plus(gshift, jnp.sum(d, axis=0, keepdims=True))
            gbdown = plus(gbdown, jnp.sum(g, axis=0, keepdims=True))
            gbout = plus(gbout, jnp.sum(g1b.astype(F32), axis=0, keepdims=True))
    small_ref[8:9, :] = gbout
    small_ref[9:10, :] = ggain
    small_ref[10:11, :] = gshift
    small_ref[11:12, :] = gbdown
    small_ref[12:16, :] = jnp.zeros((4, outp.shape[1]), F32)
    unpermute(slot_ref[0:1, :], outp, res_ref)
    return gout


def ffn_kernel(
    few,
    x1_ref, cot_ref, slot_ref, mask_ref, vec_ref, bup_ref, wup_ref, wdn_ref, wout_ref, o_ref,
    res_ref, gup_ref, gdn_ref, g1_ref, do_ref, gout_ref, small_ref,
    acc, h2, h2t, gy, gyt, dh2, outp,
):
    j = pl.program_id(0)
    length, width = x1_ref.shape
    blocks = ffn_blocks(few, length)

    @pl.when(j == 0)
    def _():
        ffn_start(blocks, x1_ref, cot_ref, slot_ref, mask_ref, vec_ref, acc, h2, h2t, gy, gyt, dh2)

    total = None
    for block in blocks:
        part = ffn_block(block, wup_ref[...], wdn_ref[...], bup_ref[...], acc, h2, h2t, gy, gyt, dh2)
        if part is not None:
            total = part if total is None else [x + y for x, y in zip(total, part)]
    gup, gdn, gbup = total
    gup_ref[...] = gup.astype(BF16)
    for n in range(gdn_ref.shape[0]):
        cols = slice(n * width, (n + 1) * width)
        gdn_ref[n] = gdn[:, cols].astype(BF16)
        small_ref[pl.ds(j * gdn_ref.shape[0] + n, 1), :] = gbup[:, cols]

    @pl.when(j == pl.num_programs(0) - 1)
    def _():
        gout = ffn_end(
            blocks, x1_ref, slot_ref, vec_ref, wout_ref, o_ref, acc, gy, dh2, outp, res_ref, g1_ref, do_ref, small_ref
        )
        gout_ref[...] = gout.astype(BF16)


def feed_forward(few, x1, cot, slot, mask, vecs, bup, wup, wdn, wout, o):
    length, width = x1.shape
    hidden = wup.shape[1]
    fc = 2 * width
    sds = jax.ShapeDtypeStruct
    whole = lambda *shape: pl.BlockSpec(shape, lambda j: (0,) * len(shape))
    return pl.pallas_call(
        functools.partial(ffn_kernel, few),
        grid=(hidden // fc,),
        in_specs=[
            whole(length, width),
            whole(length, width),
            whole(8, length),
            whole(1, length),
            whole(8, width),
            pl.BlockSpec((1, fc), lambda j: (0, j)),
            pl.BlockSpec((width, fc), lambda j: (0, j)),
            pl.BlockSpec((fc, width), lambda j: (j, 0)),
            whole(width, width),
            whole(few, width),
        ],
        out_specs=[
            whole(length, width),
            pl.BlockSpec((width, fc), lambda j: (0, j)),
            pl.BlockSpec((2, width, width), lambda j: (j, 0, 0)),
            whole(few, width),
            whole(few, width),
            whole(width, width),
            whole(16, width),
        ],
        out_shape=(
            sds((length, width), BF16),
            sds((width, hidden), BF16),
            sds((hidden // width, width, width), BF16),
            sds((few, width), F32),
            sds((few, width), BF16),
            sds((width, width), BF16),
            sds((16, width), F32),
        ),
        scratch_shapes=[
            pltpu.VMEM((length, width), F32),
            pltpu.VMEM((length, width), BF16),
            pltpu.VMEM((width, few), BF16),
            pltpu.VMEM((few, width), BF16),
            pltpu.VMEM((width, few), BF16),
            pltpu.VMEM((few, width), F32),
            pltpu.VMEM((length, width), BF16),
        ],
        compiler_params=pltpu.CompilerParams(vmem_limit_bytes=56 * MB),
        name="feed_forward",
    )(x1, cot, slot, mask, vecs, bup, wup, wdn, wout, o)


class Heads:
    step = 256

    def __init__(self, few, q_ref, k_ref, v_ref, do_ref, o_ref, lse_ref, dqt, dkv):
        self.k_ref, self.v_ref, self.lse_ref, self.dqt, self.dkv = k_ref, v_ref, lse_ref, dqt, dkv
        q = q_ref[...]
        do = do_ref[...]
        lane = lax.broadcasted_iota(jnp.int32, (few, LANES), 1)
        head = lax.broadcasted_iota(jnp.int32, (8, LANES), 0)
        lane8 = lax.broadcasted_iota(jnp.int32, (8, LANES), 1)
        pick = jnp.where(lane8 // HEAD_DIM == head, 1.0, 0.0)
        self.delta = lax.dot_general(
            pick, do.astype(F32) * o_ref[...].astype(F32), NT,
            precision=lax.Precision.HIGHEST, preferred_element_type=F32,
        )
        dqt[...] = jnp.zeros_like(dqt)
        zero = jnp.zeros_like(q)
        self.qs = [jnp.where(lane // HEAD_DIM == h, q, zero) for h in range(GROUP)]
        self.dos = [jnp.where(lane // HEAD_DIM == h, do, zero) for h in range(GROUP)]

    def keys(self, i):
        step = self.step
        rows = pl.ds(pl.multiple_of(i * step, step), step)
        k = self.k_ref[rows, :]
        v = self.v_ref[rows, :]
        kt = jnp.transpose(k)
        dk = jnp.zeros((step, LANES), F32)
        dv = jnp.zeros((step, LANES), F32)
        for h in range(GROUP):
            s = dot(k, self.qs[h], NT)
            p = jnp.exp2(s * (SCALE * LOG2E) - self.lse_ref[h : h + 1, :])
            dp = dot(v, self.dos[h], NT)
            ds = (p * (dp - self.delta[h : h + 1, :])).astype(BF16)
            dv = dv + dot(p.astype(BF16), self.dos[h])
            dk = dk + dot(ds, self.qs[h])
            part = slice(h * HEAD_DIM, (h + 1) * HEAD_DIM)
            self.dqt[part, :] += dot(kt[part, :], ds)
        self.dkv[rows, :LANES] = (dk * SCALE).astype(BF16)
        self.dkv[rows, LANES:] = dv.astype(BF16)


def transpose_rows(src_ref, out_ref):
    step = 256
    for start in range(0, src_ref.shape[0], step):
        out_ref[:, start : start + step] = jnp.transpose(src_ref[start : start + step, :])


def group_weights(few, dqt, dkv, h1t, small_ref, cols):
    dq = (jnp.transpose(dqt[...]) * SCALE).astype(BF16)
    gq = dot(h1t[:, :few], dq).astype(BF16)
    gkv = dot(h1t[...], dkv[...]).astype(BF16)
    small_ref[2:3, cols] = jnp.sum(dq.astype(F32), axis=0, keepdims=True)
    small_ref[3:4, cols] = jnp.sum(dkv[:, LANES:].astype(F32), axis=0, keepdims=True)
    return dq, gq, gkv[:, :LANES], gkv[:, LANES:]


def group_inputs(few, dq, dkv, wq_ref, wk_ref, wv_ref, dh1):
    step = 256
    wkv = jnp.concatenate([wk_ref[...], wv_ref[...]], axis=1)
    for start in range(0, dh1.shape[0], step):
        rows = slice(start, start + step)
        dh1[rows, :] += dot(dkv[rows, :], wkv, NT)
    dh1[:few, :] += dot(dq, wq_ref[...], NT)


def back_finish(few, dh1_ref, xp_ref, vec_ref, g1_ref, small_ref, gtp):
    length, width = xp_ref.shape
    gain = vec_ref[0:1, :]
    step = 128
    ggain = gshift = jnp.zeros((1, width), F32)
    for start in range(0, length, step):
        rows = slice(start, start + step)
        xhat, rstd = norm_stats(xp_ref[rows, :].astype(F32))
        d = dh1_ref[rows, :]
        g = norm_back(d, xhat, rstd, gain)
        if start < few:
            g = g + g1_ref[rows, :]
        gtp[rows, :] = g.astype(BF16)
        ggain = ggain + jnp.sum(d * xhat, axis=0, keepdims=True)
        gshift = gshift + jnp.sum(d, axis=0, keepdims=True)
    small_ref[0:1, :] = ggain
    small_ref[1:2, :] = gshift


def back_kernel(
    few,
    q, k, v, do, o, lse, h1, xp, vec, wq, wk, wv, g1, slot,
    gtok, gq_ref, gk_ref, gv_ref, small,
    h1t, dh1, dqt, dkv, gtp,
):
    t = pl.program_id(0)
    cols = pl.ds(pl.multiple_of(t * LANES, LANES), LANES)

    @pl.when(t == 0)
    def _():
        transpose_rows(h1, h1t)
        dh1[...] = jnp.zeros_like(dh1)
        small[...] = jnp.zeros_like(small)

    heads = Heads(few, q, k, v, do, o, lse, dqt, dkv)

    def body(i, _):
        heads.keys(i)
        return 0

    lax.fori_loop(0, h1.shape[0] // heads.step, body, 0)
    dq, gq, gk, gv = group_weights(few, dqt, dkv, h1t, small, cols)
    gq_ref[...] = gq
    gk_ref[...] = gk
    gv_ref[...] = gv
    group_inputs(few, dq, dkv, wq, wk, wv, dh1)

    @pl.when(t == pl.num_programs(0) - 1)
    def _():
        back_finish(few, dh1, xp, vec, g1, small, gtp)
        unpermute(slot[0:1, :], gtp, gtok)


def back_specs(few, length, width, grouped=False):
    groups = width // LANES
    whole = lambda *shape: pl.BlockSpec(shape, lambda t: (0,) * len(shape))
    cols = lambda rows, first: pl.BlockSpec((rows, LANES), lambda t: (0, first + t))
    in_specs = [
        cols(few, 0),
        cols(length, groups),
        cols(length, 2 * groups),
        cols(few, 0),
        cols(few, 0),
        pl.BlockSpec((8, few), lambda t: (t, 0)),
        whole(length, width),
        whole(length, width),
        whole(8, width),
    ]
    if grouped:
        in_specs += [pl.BlockSpec((width, LANES), lambda t, n=n: (0, 3 * t + n)) for n in range(3)]
    else:
        in_specs += [cols(width, n * groups) for n in range(3)]
    in_specs += [
        whole(few, width),
        whole(8, length),
    ]
    scratch = [
        pltpu.VMEM((width, length), BF16),
        pltpu.VMEM((length, width), F32),
        pltpu.VMEM((LANES, few), F32),
        pltpu.VMEM((length, 2 * LANES), BF16),
        pltpu.VMEM((length, width), BF16),
    ]
    return whole, cols, in_specs, scratch


def attn_backward(few, qkv, do, o, lse, h1, xp, vecs, wqkv, g1, slot):
    length, width = h1.shape
    sds = jax.ShapeDtypeStruct
    whole, cols, in_specs, scratch = back_specs(few, length, width)
    return pl.pallas_call(
        functools.partial(back_kernel, few),
        grid=(width // LANES,),
        in_specs=in_specs,
        out_specs=[whole(length, width), cols(width, 0), cols(width, 0), cols(width, 0), whole(8, width)],
        out_shape=(
            sds((length, width), BF16),
            sds((width, width), BF16),
            sds((width, width), BF16),
            sds((width, width), BF16),
            sds((8, width), F32),
        ),
        scratch_shapes=scratch,
        compiler_params=pltpu.CompilerParams(vmem_limit_bytes=56 * MB),
        name="attn_backward",
    )(qkv, qkv, qkv, do, o, lse, h1, xp, vecs, wqkv, wqkv, wqkv, g1, slot)


class Reduce:
    def __init__(self, place, rep, reps, mine, other, acc, near, side, last, depth, fin, sems):
        send, recv, local = sems
        self.rep, self.reps = rep, reps
        self.acc, self.near, self.side, self.last, self.depth, self.fin = acc, near, side, last, depth, fin
        chip = place.me // 2
        cx, cy, cd = place.xn // 2, place.yn // 2, place.dg // 2
        self.chip, self.cx, self.cy = chip, cx, cy
        fsdp = lambda d: {"fsdp": d}
        low, high = slice(0, 2), slice(2, 4)
        n = iter(range(100))
        def copy(src, dst, to):
            i = next(n)
            return remote(src, dst, send.at[i], recv.at[i], to)
        self.a = [copy(other[q], near.at[:, q], fsdp(place.sib)) for q in range(4)]
        self.own = [pltpu.make_async_copy(mine[q], acc.at[:, q], local.at[q]) for q in range(4)]
        self.b = [
            copy(acc.at[cx, low], side.at[0], fsdp(place.xn)),
            copy(acc.at[cy, high], side.at[2], fsdp(place.yn)),
            copy(acc.at[cd, low], side.at[1], fsdp(place.xn)),
            copy(acc.at[cd, high], side.at[3], fsdp(place.yn)),
        ]
        self.c = [
            copy(acc.at[cy, low], last.at[0], fsdp(place.yn)),
            copy(acc.at[cx, high], last.at[1], fsdp(place.xn)),
        ]
        peers = [(rep + d) % reps for d in range(1, reps)]
        self.d = [copy(acc.at[chip, z], depth.at[i], {"rep": z}) for i, z in enumerate(peers)]
        self.e = [copy(fin.at[rep], fin.at[rep], {"rep": z}) for z in peers]

    COPIES = 16

    def start(self):
        for x in self.a + self.own:
            x.start()

    def near_sum(self):
        for q in range(4):
            self.own[q].wait()
            self.a[q].wait_recv()
            for c in range(4):
                self.acc[c, q] = (self.acc[c, q].astype(F32) + self.near[c, q].astype(F32)).astype(BF16)
        for x in self.b:
            x.start()

    def add(self, c, half, part):
        for q in range(2):
            self.acc[c, half + q] = (self.acc[c, half + q].astype(F32) + part[q].astype(F32)).astype(BF16)

    def side_sum(self):
        for x in self.b:
            x.wait()
        self.add(self.cy, 0, self.side.at[1])
        self.c[0].start()
        self.add(self.cx, 2, self.side.at[3])
        self.c[1].start()
        self.add(self.chip, 0, self.side.at[0])
        self.add(self.chip, 2, self.side.at[2])

    def last_sum(self):
        for x in self.c:
            x.wait()
        self.add(self.chip, 0, self.last.at[0])
        self.add(self.chip, 2, self.last.at[1])
        for x in self.d:
            x.start()

    def depth_sum(self):
        total = self.acc[self.chip, self.rep].astype(F32)
        for i in range(self.reps - 1):
            self.d[i].wait()
            total = total + self.depth[i].astype(F32)
        self.fin[self.rep] = total.astype(BF16)
        for x in self.e:
            x.start()

    def finish(self):
        for x in self.e:
            x.wait()
        for x in self.a:
            x.wait_send()


class Small:
    def __init__(self, me, shards, rep, reps, rows, beside, depth, out, sems):
        psend, precv, rsend, rrecv = sems
        self.me, self.rep, self.rows, self.near, self.depth, self.out = me, rep, rows, beside, depth, out
        self.first = [
            remote(beside.at[me], beside.at[me], psend.at[d - 1], precv.at[d - 1], {"fsdp": (me + d) % shards})
            for d in range(1, shards)
        ]
        self.second = [
            remote(depth.at[rep], depth.at[rep], rsend.at[d - 1], rrecv.at[d - 1], {"rep": (rep + d) % reps})
            for d in range(1, reps)
        ]

    def start(self):
        self.near[self.me] = self.rows[...]
        for x in self.first:
            x.start()

    def middle(self):
        for x in self.first:
            x.wait()
        total = self.near[0]
        for s in range(1, self.near.shape[0]):
            total = total + self.near[s]
        self.depth[self.rep] = total
        for x in self.second:
            x.start()

    def finish(self):
        for x in self.second:
            x.wait()
        total = self.depth[0]
        for z in range(1, self.depth.shape[0]):
            total = total + self.depth[z]
        self.out[...] = total


def reduce_back_kernel(
    few, shards, reps,
    q, k, v, do, o, lse, h1, xp, vec, wq, wk, wv, g1, slot, early_ref, gout_ref, gup_ref, gdn_ref,
    gtok, gup_out, gdn_out, gqkv_out, gout_out, early_out, late_out,
    h1t, dh1, dqt, dkv, gtp, late, gqkv, fin, acc, near, side, last, depth, send, recv, local,
    enear, edepth, lnear, ldepth, es1, er1, es2, er2, ls1, lr1, ls2, lr2,
):
    t = pl.program_id(0)
    cols = pl.ds(pl.multiple_of(t * LANES, LANES), LANES)
    share = h1.shape[1] // shards
    width = h1.shape[1]
    place = Place()
    rep = lax.axis_index("rep")
    core = place.me % 2

    def quarter(n, side):
        u = n // 4
        if u < 2:
            return gup_ref.at[:, side, :, n * width : (n + 1) * width]
        if u < 4:
            return gdn_ref.at[:, side, (n - 8) * share : (n - 7) * share, :]
        return gout_ref.at[:, side] if n == 16 else gqkv.at[n - 17, :, side]

    units = []
    for u in range(5):
        sems = (send.at[u], recv.at[u], local.at[u])
        units.append(
            Reduce(
                place, rep, reps,
                [quarter(4 * u + n, core) for n in range(4)],
                [quarter(4 * u + n, 1 - core) for n in range(4)],
                acc.at[u], near.at[u], side.at[u], last.at[u], depth.at[u], fin.at[u], sems,
            )
        )
    early = Small(place.me, shards, rep, reps, early_ref, enear, edepth, early_out, (es1, er1, es2, er2))
    later = Small(place.me, shards, rep, reps, late, lnear, ldepth, late_out, (ls1, lr1, ls2, lr2))

    @pl.when(t == 0)
    def _():
        barrier = pltpu.get_barrier_semaphore()
        for d in range(1, shards):
            pl.semaphore_signal(
                barrier, inc=1, device_id={"fsdp": (place.me + d) % shards},
                device_id_type=pl.DeviceIdType.MESH,
            )
        for d in range(1, reps):
            pl.semaphore_signal(
                barrier, inc=1, device_id={"rep": (rep + d) % reps}, device_id_type=pl.DeviceIdType.MESH
            )
        pl.semaphore_wait(barrier, shards + reps - 2)
        for u in range(4):
            units[u].start()
        early.start()
        transpose_rows(h1, h1t)
        dh1[...] = jnp.zeros_like(dh1)
        late[...] = jnp.zeros_like(late)

    heads = Heads(few, q, k, v, do, o, lse, dqt, dkv)
    blocks = h1.shape[0] // heads.step

    plan = [
        (1, units[0].near_sum), (2, units[1].near_sum), (3, units[2].near_sum), (4, units[3].near_sum),
        (5, early.middle), (6, units[0].side_sum), (9, units[1].side_sum), (10, units[0].last_sum),
        (11, early.finish), (13, units[2].side_sum), (14, units[1].last_sum), (15, units[0].depth_sum),
        (17, units[3].side_sum), (18, units[2].last_sum), (19, units[1].depth_sum),
    ]

    def body(i, _):
        for at, step in plan:
            pl.when(t * blocks + i == at)(step)
        heads.keys(i)
        return 0

    lax.fori_loop(0, blocks, body, 0)
    dq, gq, gk, gv = group_weights(few, dqt, dkv, h1t, late, cols)
    chips = shards // 2
    for n, g in enumerate((gq, gk, gv)):
        gqkv[n, :, :, :, cols] = g.reshape(chips, 2, share, LANES)
    final = t == pl.num_programs(0) - 1
    pl.when(final)(units[4].start)
    group_inputs(few, dq, dkv, wq, wk, wv, dh1)

    @pl.when(final)
    def _():
        units[4].near_sum()
        units[3].last_sum()
        units[2].depth_sum()
        back_finish(few, dh1, xp, vec, g1, late, gtp)
        later.start()
        units[4].side_sum()
        units[3].depth_sum()
        units[4].last_sum()
        later.middle()
        unpermute(slot[0:1, :], gtp, gtok)
        units[4].depth_sum()
        for n in range(16):
            if n % 4 == 0:
                units[n // 4].finish()
            part = fin[n // 4, n % 4].astype(F32)
            if n < 8:
                gup_out[:, n * width : (n + 1) * width] = part
            else:
                gdn_out[:, (n - 8) * share : (n - 7) * share] = jnp.transpose(part)
        later.finish()
        units[4].finish()
        gout_out[...] = fin[4, 0].astype(F32)
        for n in range(3):
            gqkv_out[:, n * width : (n + 1) * width] = fin[4, 1 + n].astype(F32)


def reduce_backward(few, shards, reps, ident, qkv, do, o, lse, h1, xp, vecs, wqkv, g1, slot, early, gout, gup, gdn):
    length, width = h1.shape
    share = width // shards
    chips = shards // 2
    sds = jax.ShapeDtypeStruct
    whole, cols, in_specs, scratch = back_specs(few, length, width, True)
    hbm = pl.BlockSpec(memory_space=pl.ANY)
    dma = pltpu.SemaphoreType.DMA
    block = (share, width)
    copies = Reduce.COPIES
    hidden = gup.shape[1]
    return pl.pallas_call(
        functools.partial(reduce_back_kernel, few, shards, reps),
        grid=(width // LANES,),
        in_specs=in_specs + [whole(16, width), hbm, hbm, hbm],
        out_specs=[
            whole(length, width), whole(share, hidden), whole(width, width), whole(share, 3 * width),
            whole(share, width), whole(16, width), whole(8, width),
        ],
        out_shape=(
            sds((length, width), BF16),
            sds((share, hidden), F32),
            sds((width, width), F32),
            sds((share, 3 * width), F32),
            sds((share, width), F32),
            sds((16, width), F32),
            sds((8, width), F32),
        ),
        scratch_shapes=scratch
        + [
            pltpu.VMEM((8, width), F32),
            pltpu.VMEM((3, chips, 2) + block, BF16),
            pltpu.VMEM((5, 4) + block, BF16),
            pltpu.VMEM((5, chips, 4) + block, BF16),
            pltpu.VMEM((5, chips, 4) + block, BF16),
            pltpu.VMEM((5, 4, 2) + block, BF16),
            pltpu.VMEM((5, 2, 2) + block, BF16),
            pltpu.VMEM((5, reps - 1) + block, BF16),
            dma((5, copies)), dma((5, copies)), dma((5, 4)),
            pltpu.VMEM((shards, 16, width), F32),
            pltpu.VMEM((reps, 16, width), F32),
            pltpu.VMEM((shards, 8, width), F32),
            pltpu.VMEM((reps, 8, width), F32),
            dma((shards - 1,)), dma((shards - 1,)), dma((reps - 1,)), dma((reps - 1,)),
            dma((shards - 1,)), dma((shards - 1,)), dma((reps - 1,)), dma((reps - 1,)),
        ],
        compiler_params=pltpu.CompilerParams(
            vmem_limit_bytes=60 * MB, collective_id=ident, has_side_effects=True
        ),
        name="reduce_backward",
    )(
        qkv, qkv, qkv, do, o, lse, h1, xp, vecs, wqkv, wqkv, wqkv, g1, slot, early,
        gout.reshape(chips, 2, share, width),
        gup.reshape(chips, 2, share, hidden),
        gdn.reshape(chips, 2, width, width),
    )


class Unit:
    COPIES = 10

    def __init__(self, place, rep, other, acc, near, side, last, own, depth, fin, send, recv):
        self.acc, self.near, self.side, self.last = acc, near, side, last
        self.own, self.depth, self.fin = own, depth, fin
        chip = place.me // 2
        cx, cy, cd = place.xn // 2, place.yn // 2, place.dg // 2
        self.chip, self.cx, self.cy = chip, cx, cy
        fsdp = lambda d: {"fsdp": d}

        def copy(i, src, dst, to):
            return remote(src, dst, send.at[i], recv.at[i], to)

        if other is not None:
            self.a = copy(0, other, near, fsdp(place.sib))
        if side is not None:
            half = acc.shape[1] // 2
            self.low, self.high = low, high = pl.ds(0, half), pl.ds(half, half)
            self.b = [
                copy(1, acc.at[cd, low], side.at[1], fsdp(place.xn)),
                copy(2, acc.at[cd, high], side.at[3], fsdp(place.yn)),
                copy(3, acc.at[cx, low], side.at[0], fsdp(place.xn)),
                copy(4, acc.at[cy, high], side.at[2], fsdp(place.yn)),
            ]
            self.c = [
                copy(5, acc.at[cy, low], last.at[0], fsdp(place.yn)),
                copy(6, acc.at[cx, high], last.at[1], fsdp(place.xn)),
            ]
        if own is None:
            self.own = own = acc.at[chip]
        if depth is not None:
            inner = (rep == 1) | (rep == 2)
            self.inner, self.outer = inner, jnp.logical_not(inner)
            pair = {"rep": rep + 1 - 2 * (rep % 2)}
            self.d = copy(7, own, depth.at[0], pair)
            self.e = copy(8, own, depth.at[1], {"rep": 3 - rep})
            self.f = copy(9, fin, fin, pair)

    def near_start(self):
        self.a.start()

    def near_add(self):
        self.a.wait_recv()
        for c in range(self.acc.shape[0]):
            self.acc[c] = self.acc[c] + self.near[c]

    def side_start(self):
        for x in self.b:
            x.start()

    def near_sum(self):
        self.near_add()
        self.side_start()

    def add(self, c, half, ref):
        self.acc[c, half, :] = self.acc[c, half, :] + ref[...]

    def side_sum(self):
        self.b[0].wait()
        self.add(self.cy, self.low, self.side.at[1])
        self.c[0].start()
        self.b[1].wait()
        self.add(self.cx, self.high, self.side.at[3])
        self.c[1].start()
        self.b[2].wait()
        self.add(self.chip, self.low, self.side.at[0])
        self.b[3].wait()
        self.add(self.chip, self.high, self.side.at[2])

    def last_add(self):
        for x in self.c:
            x.wait()
        self.add(self.chip, self.low, self.last.at[0])
        self.add(self.chip, self.high, self.last.at[1])

    def z1_start(self):
        pl.when(self.outer)(self.d.start)

    def last_sum(self):
        self.last_add()
        self.z1_start()

    def z1_done(self):
        pl.when(self.outer)(self.d.wait_send)

        @pl.when(self.inner)
        def _():
            self.d.wait_recv()
            self.own[...] = self.own[...] + self.depth[0]

    def z2_start(self):
        pl.when(self.inner)(self.e.start)

    def z1z2(self):
        self.z1_done()
        self.z2_start()

    def z2z3(self):
        @pl.when(self.inner)
        def _():
            self.e.wait()
            self.fin[...] = self.own[...] + self.depth[1]
            self.f.start()

    def z3_done(self):
        pl.when(self.inner)(self.f.wait_send)
        pl.when(self.outer)(self.f.wait_recv)


class Direct:
    def __init__(self, me, shards, rep, reps, src, near, depth, send, recv):
        self.me, self.shards, self.rep, self.reps = me, shards, rep, reps
        self.src, self.near, self.depth = src, near, depth
        self.first = []
        for d in range(1, shards):
            to = (me + d) % shards
            self.first.append(
                remote(src.at[to % 2, to // 2], near.at[me], send.at[d - 1], recv.at[d - 1], {"fsdp": to})
            )
        self.second = []
        for d in range(1, reps):
            n = shards - 2 + d
            self.second.append(remote(depth.at[rep], depth.at[rep], send.at[n], recv.at[n], {"rep": (rep + d) % reps}))

    def start(self):
        for x in self.first:
            x.start()

    def middle(self):
        total = self.src[self.me % 2, self.me // 2].astype(F32)
        for d in range(1, self.shards):
            self.first[d - 1].wait()
            total = total + self.near[(self.me + self.shards - d) % self.shards].astype(F32)
        self.depth[self.rep] = total.astype(BF16)
        for x in self.second:
            x.start()

    def finish(self):
        for x in self.second:
            x.wait()
        total = self.depth[0].astype(F32)
        for z in range(1, self.reps):
            total = total + self.depth[z].astype(F32)
        return total


def per_shard(rows, shards, share):
    out = []
    for n in range(shards):
        at = lax.broadcasted_iota(jnp.int32, (rows.shape[1], LANES), 0) - n * share
        lane = lax.broadcasted_iota(jnp.int32, (rows.shape[1], LANES), 1)
        spot = jnp.where((at == lane) & (lane < share), 1.0, 0.0).astype(BF16)
        out.append(dot(rows, spot).astype(BF16))
    return out


def greet(me, shards, rep, reps):
    barrier = pltpu.get_barrier_semaphore()
    mesh = pl.DeviceIdType.MESH
    for d in range(1, shards):
        pl.semaphore_signal(barrier, inc=1, device_id={"fsdp": (me + d) % shards}, device_id_type=mesh)
    for d in range(1, reps):
        pl.semaphore_signal(barrier, inc=1, device_id={"rep": (rep + d) % reps}, device_id_type=mesh)
    pl.semaphore_wait(barrier, shards + reps - 2)


CHUNKS = 5


def ffn_reduce_kernel(
    few, shards, reps,
    x1_ref, cot_ref, slot_ref, mask_ref, vec_ref, wout_ref, o_ref, *refs,
):
    bups, wups, wdns = refs[:shards], refs[shards : 2 * shards], refs[2 * shards : 3 * shards]
    (
        res_ref, g1_ref, do_ref, gout_ref, state_ref, plane_ref,
        acc, h2, h2t, gy, gyt, dh2, outp, small_ref, g, near, side, last, depth, fin, send, recv,
    ) = refs[3 * shards :]
    j = pl.program_id(0)
    length, width = x1_ref.shape
    share = width // shards
    blocks = ffn_blocks(few, length)
    place = Place()
    rep = lax.axis_index("rep")
    core = place.me % 2
    units = []
    for u in range(CHUNKS):
        xy = u < 4
        z = u < 2
        units.append(
            Unit(
                place, rep, g.at[u, 1 - core], g.at[u, core], near.at[u],
                side.at[u] if xy else None, last.at[u] if xy else None, None,
                depth.at[u] if z else None, fin if z else None, send.at[u], recv.at[u],
            )
        )

    def at(step, *acts):
        @pl.when(j == step)
        def _():
            for act in acts:
                act()

    @pl.when(j == 0)
    def _():
        greet(place.me, shards, rep, reps)
        ffn_start(blocks, x1_ref, cot_ref, slot_ref, mask_ref, vec_ref, acc, h2, h2t, gy, gyt, dh2)

    wup = jnp.concatenate([w[...] for w in wups], axis=1)
    wdn = jnp.concatenate([w[...] for w in wdns], axis=0)
    bup = jnp.concatenate([b[...] for b in bups], axis=1)
    cols = pl.ds(pl.multiple_of(j * LANES, LANES), LANES)
    for n, block in enumerate(blocks):
        part = ffn_block(block, wup, wdn, bup, acc, h2, h2t, gy, gyt, dh2)
        if n == 0:
            gup, gdn, gbup = part
            for s in range(shards):
                mine = slice(s * share, (s + 1) * share)
                lanes = slice(s * LANES, (s + 1) * LANES)
                for b in range(shards):
                    g[j, s % 2, s // 2, b * share : (b + 1) * share, :] = gup[
                        mine, b * LANES : (b + 1) * LANES
                    ].astype(BF16)
                g[j, s % 2, s // 2, width:, :] = gdn[:, lanes].astype(BF16)
                small_ref[s : s + 1, cols] = gbup[:, lanes]
            for u in range(CHUNKS):
                at(u, units[u].near_start)
        if n == 1:
            at(2, units[0].last_sum)
            at(3, units[0].z1z2, units[1].last_sum)
            at(4, units[0].z2z3, units[2].last_add)
        if n == 2:
            for u in range(CHUNKS):
                if u:
                    at(u, units[u - 1].side_sum)
                at(u, units[u].near_sum if u < 4 else units[u].near_add)
            at(4, units[1].z1_done)

    @pl.when(j == CHUNKS - 1)
    def _():
        gout = ffn_end(
            blocks, x1_ref, slot_ref, vec_ref, wout_ref, o_ref, acc, gy, dh2, outp, res_ref, g1_ref, do_ref, small_ref
        )
        for s in range(shards):
            for b in range(CHUNKS):
                gout_ref[s % 2, s // 2, b * share : (b + 1) * share, :] = gout[
                    s * share : (s + 1) * share, b * LANES : (b + 1) * LANES
                ].astype(BF16)
        rows = CHUNKS * share
        vectors = per_shard(small_ref[8:16, :].astype(BF16), shards, share)
        for s in range(shards):
            gout_ref[s % 2, s // 2, rows : rows + 8, :] = vectors[s]
            bias = [small_ref[s : s + 1, b * LANES : (b + 1) * LANES] for b in range(CHUNKS)]
            bias = jnp.concatenate(bias + [jnp.zeros((8 - CHUNKS, LANES), F32)], axis=0)
            gout_ref[s % 2, s // 2, rows + 8 : rows + 16, :] = bias.astype(BF16)
            spare = gout_ref.shape[2] - rows - 16
            gout_ref[s % 2, s // 2, rows + 16 :, :] = jnp.zeros((spare, LANES), BF16)
        plane_ref[...] = g[4, core]
        units[3].last_add()
        for u in range(1, 4):
            state_ref[u] = g[u, core, units[u].chip]
        units[0].z3_done()
        state_ref[0] = fin[...]
        for u in range(CHUNKS):
            units[u].a.wait_send()


def ffn_reduce(few, shards, reps, x1, cot, slot, mask, vecs, bup, wup, wdn, wout, o):
    length, width = x1.shape
    share = width // shards
    chips = shards // 2
    rows = 2 * width
    spare = 448
    sds = jax.ShapeDtypeStruct
    whole = lambda *shape: pl.BlockSpec(shape, lambda j: (0,) * len(shape))
    pick = lambda s, shape, across: pl.BlockSpec(
        shape, lambda j: (0, s * CHUNKS + j) if across else (s * CHUNKS + j, 0)
    )
    dma = pltpu.SemaphoreType.DMA
    return pl.pallas_call(
        functools.partial(ffn_reduce_kernel, few, shards, reps),
        grid=(CHUNKS,),
        in_specs=[
            whole(length, width), whole(length, width), whole(8, length), whole(1, length), whole(8, width),
            whole(width, width), whole(few, width),
        ]
        + [pick(s, (1, LANES), True) for s in range(shards)]
        + [pick(s, (width, LANES), True) for s in range(shards)]
        + [pick(s, (LANES, width), False) for s in range(shards)],
        out_specs=[
            whole(length, width), whole(few, width), whole(few, width), whole(2, chips, spare, LANES),
            whole(4, rows, LANES), whole(chips, rows, LANES),
        ],
        out_shape=(
            sds((length, width), BF16),
            sds((few, width), F32),
            sds((few, width), BF16),
            sds((2, chips, spare, LANES), BF16),
            sds((4, rows, LANES), BF16),
            sds((chips, rows, LANES), BF16),
        ),
        scratch_shapes=[
            pltpu.VMEM((length, width), F32),
            pltpu.VMEM((length, width), BF16),
            pltpu.VMEM((width, few), BF16),
            pltpu.VMEM((few, width), BF16),
            pltpu.VMEM((width, few), BF16),
            pltpu.VMEM((few, width), F32),
            pltpu.VMEM((length, width), BF16),
            pltpu.VMEM((16, width), F32),
            pltpu.VMEM((CHUNKS, 2, chips, rows, LANES), BF16),
            pltpu.VMEM((CHUNKS, chips, rows, LANES), BF16),
            pltpu.VMEM((4, 4, rows // 2, LANES), BF16),
            pltpu.VMEM((4, 2, rows // 2, LANES), BF16),
            pltpu.VMEM((2, 2, rows, LANES), BF16),
            pltpu.VMEM((rows, LANES), BF16),
            dma((CHUNKS, Unit.COPIES)), dma((CHUNKS, Unit.COPIES)),
        ],
        compiler_params=pltpu.CompilerParams(
            vmem_limit_bytes=60 * MB, collective_id=3, has_side_effects=True
        ),
        name="ffn_reduce",
    )(x1, cot, slot, mask, vecs, wout, o, *[bup] * shards, *[wup] * shards, *[wdn] * shards)


GROUP_ROWS = 256


def back_reduce_kernel(
    few, shards, reps,
    q, k, v, do, o, lse, h1, xp, vec, wq, wk, wv, g1, slot, state_in, plane_in, gout_in,
    gtok, gup_out, gdn_out, gqkv_out, gout_out, vec_out,
    h1t, dh1, dqt, dkv, gtp, late,
    own, plane, fside, flast, fdepth, ffin,
    onear, oacc, oside, olast, odepth, ofin,
    gg, gnear, gside, glast, gdepth, gfin,
    dnear, ddepth, sg, snear, sdepth,
    send, recv, local, dsend, drecv,
):
    t = pl.program_id(0)
    groups = pl.num_programs(0)
    length, width = h1.shape
    share = width // shards
    cols = pl.ds(pl.multiple_of(t * LANES, LANES), LANES)
    place = Place()
    rep = lax.axis_index("rep")
    core = place.me % 2
    sems = lambda n: (send.at[n], recv.at[n])
    make = functools.partial(Unit, place, rep)
    u1, u2, u3 = [
        make(None, own, None, None, None, own.at[n], fdepth.at[n - 1], ffin.at[n - 1], *sems(n - 1))
        for n in range(1, 4)
    ]
    u4 = make(None, plane, None, fside, flast, None, fdepth.at[3], ffin.at[3], *sems(3))
    uo = make(gout_in.at[1 - core], oacc, onear, oside, olast, None, odepth, ofin, *sems(4))
    parts = [
        make(
            gg.at[n, 1 - core], gg.at[n, core], gnear.at[n], gside.at[n], glast.at[n], None, gdepth.at[n],
            gfin.at[n], *sems(5 + n)
        )
        for n in range(3)
    ]
    direct = functools.partial(Direct, place.me, shards, rep, reps)
    parts += [
        direct(gg.at[3 + n], dnear.at[n], ddepth.at[n], dsend.at[n], drecv.at[n]) for n in range(2)
    ]
    us = direct(sg, snear, sdepth, dsend.at[2], drecv.at[2])
    loads = [
        pltpu.make_async_copy(state_in, own, local.at[0]),
        pltpu.make_async_copy(plane_in, plane, local.at[1]),
        pltpu.make_async_copy(gout_in.at[core], oacc, local.at[2]),
    ]

    @pl.when(t == 0)
    def _():
        for x in loads:
            x.start()
        greet(place.me, shards, rep, reps)
        loads[0].wait()
        u1.z2_start()
        u2.z1_start()
        loads[1].wait()
        u4.side_start()
        uo.near_start()
        loads[2].wait()
        transpose_rows(h1, h1t)
        dh1[...] = jnp.zeros_like(dh1)
        late[...] = jnp.zeros_like(late)

    heads = Heads(few, q, k, v, do, o, lse, dqt, dkv)
    blocks = length // heads.step

    plan = [
        (2, uo.near_sum),
        (5, u1.z2z3), (5, u2.z1z2), (5, u3.z1_start), (5, u4.side_sum), (7, uo.side_sum),
        (9, u4.last_add), (10, u1.z3_done), (10, u2.z2z3), (10, u3.z1z2), (10, u4.z1_start),
        (11, uo.last_sum), (13, uo.z1z2), (15, u2.z3_done), (15, u3.z2z3), (15, u4.z1z2), (16, uo.z2z3),
        (18, uo.z3_done), (19, u3.z3_done), (19, u4.z2z3),
    ]
    chain = ("near_sum", "side_sum", "last_sum", "z1z2", "z2z3")
    rest = []
    for n in range(3):
        for when, name in zip((2, 5, 7, 9, 11), chain):
            slot_at = 4 * (n + 1) + when
            if slot_at < 20:
                plan.append((slot_at, getattr(parts[n], name)))
            else:
                rest.append(getattr(parts[n], name))
    plan.append((19, parts[3].middle))
    plan.sort(key=lambda entry: entry[0])

    def body(i, _):
        for at, step in plan:
            pl.when(t * blocks + i == at)(step)
        heads.keys(i)
        return 0

    lax.fori_loop(0, blocks, body, 0)
    dq, gq, gk, gv = group_weights(few, dqt, dkv, h1t, late, cols)
    for n, part in enumerate((gq, gk, gv)):
        for s in range(shards):
            gg[t, s % 2, s // 2, n * share : (n + 1) * share, :] = part[s * share : (s + 1) * share, :]
    for s in range(shards):
        gg[t, s % 2, s // 2, 3 * share :, :] = jnp.zeros((GROUP_ROWS - 3 * share, LANES), BF16)
    for n in range(5):
        pl.when(t == n)(parts[n].near_start if n < 3 else parts[n].start)
    group_inputs(few, dq, dkv, wq, wk, wv, dh1)

    @pl.when(t == groups - 1)
    def _():
        z1z2, z2z3 = rest
        z1z2()
        back_finish(few, dh1, xp, vec, g1, late, gtp)
        vectors = per_shard(jnp.concatenate([late[...], jnp.zeros_like(late)], axis=0).astype(BF16), shards, share)
        for s in range(shards):
            sg[s % 2, s // 2] = vectors[s]
        us.start()
        z2z3()
        parts[4].middle()
        unpermute(slot[0:1, :], gtp, gtok)
        us.middle()
        u4.z3_done()
        for n in range(CHUNKS):
            src = ffin.at[n - 1] if n else own.at[0]
            for b in range(shards):
                gup_out[:, b * width + n * LANES : b * width + (n + 1) * LANES] = src[b * share : (b + 1) * share, :]
            gdn_out[n * LANES : (n + 1) * LANES, :] = jnp.transpose(src[width:, :])
        for b in range(CHUNKS):
            gout_out[:, b * LANES : (b + 1) * LANES] = ofin[b * share : (b + 1) * share, :]
        vec_out[0:16, :] = ofin[CHUNKS * share : CHUNKS * share + 16, :].astype(F32)
        for n in range(5):
            if n < 3:
                parts[n].z3_done()
                parts[n].a.wait_send()
                done = gfin[n]
            else:
                done = parts[n].finish().astype(BF16)
            for m in range(3):
                gqkv_out[:, m * width + n * LANES : m * width + (n + 1) * LANES] = done[m * share : (m + 1) * share, :]
        vec_out[16:32, :] = us.finish()
        uo.a.wait_send()


SMALL_ROWS = 16


def back_reduce(few, shards, reps, qkv, do, o, lse, h1, xp, vecs, wqkv, g1, slot, state, plane, gout):
    length, width = h1.shape
    share = width // shards
    chips = shards // 2
    rows = 2 * width
    groups = width // LANES
    hidden = shards * width
    sds = jax.ShapeDtypeStruct
    whole, cols, in_specs, scratch = back_specs(few, length, width, True)
    hbm = pl.BlockSpec(memory_space=pl.ANY)
    dma = pltpu.SemaphoreType.DMA
    vm = lambda *shape: pltpu.VMEM(shape + (LANES,), BF16)
    spare = gout.shape[2]

    def buffers(rows):
        return [vm(4, rows // 2), vm(2, rows // 2), vm(2, rows), vm(rows)]

    many = lambda n, refs: [pltpu.VMEM((n,) + r.shape, BF16) for r in refs]
    fside, flast, fdepth, ffin = buffers(rows)
    return pl.pallas_call(
        functools.partial(back_reduce_kernel, few, shards, reps),
        grid=(groups,),
        in_specs=in_specs + [hbm, hbm, hbm],
        out_specs=[
            whole(length, width), whole(share, hidden), whole(width, width), whole(share, 3 * width),
            whole(share, width), whole(32, LANES),
        ],
        out_shape=(
            sds((length, width), BF16),
            sds((share, hidden), BF16),
            sds((width, width), BF16),
            sds((share, 3 * width), BF16),
            sds((share, width), BF16),
            sds((32, LANES), F32),
        ),
        scratch_shapes=scratch
        + [
            pltpu.VMEM((8, width), F32),
            vm(4, rows), vm(chips, rows), fside, flast,
        ]
        + many(4, [fdepth, ffin])
        + [vm(chips, spare), vm(chips, spare)] + buffers(spare)
        + [vm(5, 2, chips, GROUP_ROWS), vm(3, chips, GROUP_ROWS)] + many(3, buffers(GROUP_ROWS))
        + [vm(2, shards, GROUP_ROWS), vm(2, reps, GROUP_ROWS)]
        + [vm(2, chips, SMALL_ROWS), vm(shards, SMALL_ROWS), vm(reps, SMALL_ROWS)]
        + [dma((8, Unit.COPIES)), dma((8, Unit.COPIES)), dma((3,))]
        + [dma((3, shards + reps - 2)), dma((3, shards + reps - 2))],
        compiler_params=pltpu.CompilerParams(
            vmem_limit_bytes=60 * MB, collective_id=4, has_side_effects=True
        ),
        name="back_reduce",
    )(qkv, qkv, qkv, do, o, lse, h1, xp, vecs, wqkv, wqkv, wqkv, g1, slot, state, plane, gout)


def local(
    reps, shards,
    tokens, masked, cotangent, norm1_gain, norm1_shift, w_qkv, bias_query, bias_value, w_out,
    bias_out, norm2_gain, norm2_shift, w_up, bias_up, w_down, bias_down,
):
    seqs, length, width = tokens.shape
    hidden = w_up.shape[1]
    share = w_qkv.shape[0]
    close = shards == 8 and reps == 4 and share % 16 == 0 and share <= LANES and w_down.shape[0] == width
    x = tokens.reshape(seqs * length, width)
    cot = cotangent.reshape(seqs * length, width)
    mask = masked.astype(F32)
    if close:
        pack = jnp.concatenate(
            [
                jnp.pad(
                    jnp.stack(
                        [norm1_gain, norm1_shift, bias_query, bias_value, bias_out, norm2_gain, norm2_shift, bias_down]
                    ),
                    ((0, 0), (0, LANES - share)),
                ),
                jnp.pad(bias_up.reshape(-1, LANES), ((0, 3), (0, 0))),
            ]
        )
        slot, xp, h1, qkv, o, lse, x1, vecs, bup, over, wqkv, wout, wup, wdn = gather_attn(
            reps, shards, x, mask, pack, w_qkv, w_out, w_up, w_down
        )
        small_enough = over[0, 0] < 0.5
    else:
        small_enough = lax.pmax(jnp.sum(masked), ("rep", "fsdp")) <= FEW
        packed = jnp.stack(
            [norm1_gain, norm1_shift, bias_query, bias_value, bias_out, norm2_gain, norm2_shift, bias_down]
        )
        vecs = lax.all_gather(packed, "fsdp", axis=1, tiled=True).astype(F32)
        bup = lax.all_gather(bias_up, "fsdp", axis=0, tiled=True).astype(F32).reshape(1, hidden)
        gather = lambda w: lax.all_gather(w, "fsdp", axis=0, tiled=True)
        wqkv, wout, wup, wdn = gather(w_qkv), gather(w_out), gather(w_up), gather(w_down)
        slot, xp, h1, qkv, o, lse, x1 = attn_forward(x, mask, vecs, wqkv, wout)

    def backward(few):
        def run():
            res, gup, gdn, g1, do, gout, early = feed_forward(
                few, x1, cot, slot, mask, vecs, bup, wup, wdn, wout, o
            )
            if close:
                gtok, gup, gdn, gqkv, gout, early, late = reduce_backward(
                    few, shards, reps, 1,
                    qkv, do, o, lse, h1, xp, vecs, wqkv, g1, slot, early, gout, gup, gdn,
                )
                return res, gtok, gup, gdn, gqkv, gout, early, late
            gtok, gq, gk, gv, late = attn_backward(
                few, qkv, do, o, lse, h1, xp, vecs, wqkv, g1, slot
            )
            return res, gtok, gup, gdn, jnp.concatenate([gout, gq, gk, gv], axis=1), early, late

        return run

    me = lax.axis_index("fsdp")
    own = bias_up.shape[0]

    def pick(late, early):
        gbup = lax.dynamic_slice_in_dim(early[:8].reshape(hidden), me * own, own)
        return lax.dynamic_slice_in_dim(jnp.concatenate([late[:4], early[8:12]]), me * share, share, axis=1), gbup

    if close:
        res, g1, do, part, state, plane = ffn_reduce(
            FEW, shards, reps, x1, cot, slot, mask, vecs, bup, wup, wdn, wout, o
        )
        gtok, gup, gdn, gqkv, gout, small = back_reduce(
            FEW, shards, reps, qkv, do, o, lse, h1, xp, vecs, wqkv, g1, slot, state, plane, part
        )

        def redo():
            res, gtok, *outs, early, late = backward(length)()
            outs = [x.astype(BF16) for x in outs]
            mine, gbup = pick(late, early)
            rows = jnp.concatenate([mine[4:], jnp.zeros((4, share), F32)])
            tail = jnp.concatenate([mine[:4], jnp.zeros((12, share), F32)])
            wide = lambda x: jnp.pad(x, ((0, 0), (0, LANES - share)))
            ups = jnp.pad(gbup.reshape(-1, LANES), ((0, 8 - own // LANES), (0, 0)))
            return (res, gtok, *outs, jnp.concatenate([wide(rows), ups, wide(tail)]))

        res, gtok, gup, gdn, gqkv, gout, small = lax.cond(
            small_enough, lambda: (res, gtok, gup, gdn, gqkv, gout, small), redo
        )
        gup, gdn, gqkv, gout = [x.astype(F32) for x in (gup, gdn, gqkv, gout)]
        mine = [small[n, :share] for n in (16, 17, 18, 19, 0, 1, 2, 3)]
        gbup = small[8 : 8 + own // LANES].reshape(own)
    else:
        def scatter(g, dim):
            part = lax.psum_scatter(g, "fsdp", scatter_dimension=dim, tiled=True)
            return lax.psum(part, "rep").astype(F32)

        res, gtok, gup, gdn, gattn, early, late = lax.cond(small_enough, backward(FEW), backward(length))
        gup = scatter(gup, 0)
        gdn = scatter(gdn.transpose(0, 2, 1).reshape(hidden, width), 0)
        gattn = scatter(gattn, 0)
        gout, gqkv = gattn[:, :width], gattn[:, width:]
        mine, gbup = pick(lax.psum(late, ("rep", "fsdp")), lax.psum(early, ("rep", "fsdp")))
    return (
        res.reshape(seqs, length, width),
        gtok.reshape(seqs, length, width),
        mine[0], mine[1], gqkv, mine[2], mine[3], gout, mine[4], mine[5], mine[6],
        gup, gbup, gdn, mine[7],
    )


def solution(mesh):
    rows3 = P(("rep", "fsdp"), None, None)
    vec = P("fsdp")
    mat = P("fsdp", None)
    in_specs = (
        rows3, P(("rep", "fsdp"), None), rows3,
        vec, vec, mat, vec, vec, mat, vec, vec, vec, mat, vec, mat, vec,
    )
    out_specs = (rows3, rows3, vec, vec, mat, vec, vec, mat, vec, vec, vec, mat, vec, mat, vec)
    body = functools.partial(local, mesh.shape["rep"], mesh.shape["fsdp"])
    return jax.shard_map(body, mesh=mesh, in_specs=in_specs, out_specs=out_specs, check_vma=False)
```
